32 devices in a mesh: dp: 8 (over z, x), mp: 4 (over y, core).
Axes of the slice: x: 2, y: 2, z: 4, core: 2. Of those that a mesh axis runs over, the one named last changes fastest.
Arguments:
- latents: float32 [16, 64, 1536], P('dp', 'mp'), may hold values from -6 to 6
- media: bfloat16 [16, 2048, 1536], P('dp', 'mp'), may hold values from -6 to 6
- frames: int32 [16], P('dp'), may hold values from 1 to 8, as said below
- cotangent: float32 [16, 64, 1536], P('dp', 'mp'), may hold values from -16 to 16
- qkv_master: float32 [3, 1536, 1536], P(None, 'dp', 'mp'), may hold values from -0.15625 to 0.15625
- qkv_momentum: float32 [3, 1536, 1536], P(None, 'dp', 'mp'), may hold values from -0.001953125 to 0.001953125
- qkv_average: float32 [3, 1536, 1536], P(None, 'dp', 'mp'), may hold values from -0.15625 to 0.15625
- out_master: float32 [1536, 1536], P('mp', 'dp'), may hold values from -8 to 8
- out_momentum: float32 [1536, 1536], P('mp', 'dp'), may hold values from -0.00024414062 to 0.00024414062
- out_average: float32 [1536, 1536], P('mp', 'dp'), may hold values from -0.75 to 0.75
- up_master: float32 [1536, 6144], P('dp', 'mp'), may hold values from -2 to 2
- up_momentum: float32 [1536, 6144], P('dp', 'mp'), may hold values from -0.00048828125 to 0.00048828125
- up_average: float32 [1536, 6144], P('dp', 'mp'), may hold values from -0.15625 to 0.15625
- down_master: float32 [6144, 1536], P('mp', 'dp'), may hold values from -2 to 2
- down_momentum: float32 [6144, 1536], P('mp', 'dp'), may hold values from -0.0008544922 to 0.0008544922
- down_average: float32 [6144, 1536], P('mp', 'dp'), may hold values from -0.078125 to 0.078125
- norm_params: float32 [6, 1536], replicated, may hold values from -2 to 4
- norm_momentum: float32 [6, 1536], replicated, may hold values from -0.0017089844 to 0.0017089844
- norm_average: float32 [6, 1536], replicated, may hold values from 0.5 to 1.5
- time_table: float32 [8, 1536], replicated, may hold values from -3 to 3
- time_momentum: float32 [8, 1536], replicated, may hold values from -0.0007324219 to 0.0007324219
- time_average: float32 [8, 1536], replicated, may hold values from -3 to 3
Outputs:
- latents_out: float32 [16, 64, 1536], P('dp', 'mp')
- latents_grad: float32 [16, 64, 1536], P('dp', 'mp')
- media_grad: float32 [16, 2048, 1536], P('dp', 'mp')
- grad_norm: float32 [], replicated
- qkv_grad: float32 [3, 1536, 1536], P(None, 'dp', 'mp')
- qkv_new: float32 [3, 1536, 1536], P(None, 'dp', 'mp')
- qkv_momentum_new: float32 [3, 1536, 1536], P(None, 'dp', 'mp')
- qkv_average_new: float32 [3, 1536, 1536], P(None, 'dp', 'mp')
- out_grad: float32 [1536, 1536], P('mp', 'dp')
- out_new: float32 [1536, 1536], P('mp', 'dp')
- out_momentum_new: float32 [1536, 1536], P('mp', 'dp')
- out_average_new: float32 [1536, 1536], P('mp', 'dp')
- up_grad: float32 [1536, 6144], P('dp', 'mp')
- up_new: float32 [1536, 6144], P('dp', 'mp')
- up_momentum_new: float32 [1536, 6144], P('dp', 'mp')
- up_average_new: float32 [1536, 6144], P('dp', 'mp')
- down_grad: float32 [6144, 1536], P('mp', 'dp')
- down_new: float32 [6144, 1536], P('mp', 'dp')
- down_momentum_new: float32 [6144, 1536], P('mp', 'dp')
- down_average_new: float32 [6144, 1536], P('mp', 'dp')
- norm_grad: float32 [6, 1536], replicated
- norm_new: float32 [6, 1536], replicated
- norm_momentum_new: float32 [6, 1536], replicated
- norm_average_new: float32 [6, 1536], replicated
- time_grad: float32 [8, 1536], replicated
- time_new: float32 [8, 1536], replicated
- time_momentum_new: float32 [8, 1536], replicated
- time_average_new: float32 [8, 1536], replicated
- qkv_copy: bfloat16 [3, 1536, 1536], P(None, 'dp', 'mp')
- out_copy: bfloat16 [1536, 1536], P('mp', 'dp')
- up_copy: bfloat16 [1536, 6144], P('dp', 'mp')
- down_copy: bfloat16 [6144, 1536], P('mp', 'dp')
The draws below stay inside these ranges and needn't reach their ends.
Inputs may be any that keep to these rules, and one draw needn't show every extreme that they name: Every item has 1 or 8 frames, and among the 2 items of each index of dp at least one has 8.
All inputs are finite; a program needn't handle non-finite values.
Results may differ from the reference program's by a relative error of at most 0.018.
The reference program's roundings to bfloat16 on the way count: a program that leaves them out, or rounds other values in their place, can miss the bound.
Values may be sent and summed in bfloat16 or wider, within the bound.
A program may use at most 192 MiB of HBM per device.

```python
import jax
import jax.numpy as jnp
from jax import lax

D = 1536
HEADS = 16
HEAD_DIM = 96
FF = 6144
LAT = 64
FRAMES = 8
PATCHES = 256
ITEMS_DEV = 2
CAP = 2048
ITEMS = 16


def ramp(count, start_value, end_value):
    return jnp.linspace(start_value, end_value, count, dtype=jnp.float32)


def bounded(key, shape):
    return jnp.clip(jax.random.normal(key, shape, jnp.float32), -6.0, 6.0)


def draw_frames(key, part):
    key = jax.random.fold_in(key, 5)
    keys = jax.random.split(key, 4)
    blocks = ITEMS // ITEMS_DEV
    clips = jax.random.randint(keys[0], (blocks, ITEMS_DEV), 0, 2)
    counts = jnp.where(clips == 1, FRAMES, 1)
    places = jnp.arange(ITEMS_DEV)[None, :]
    chosen = jax.random.randint(keys[1], (blocks, 1), 0, ITEMS_DEV)
    counts = jnp.where(places == chosen, FRAMES, counts)
    block_pick = jax.random.randint(keys[2], (), 0, blocks)
    other_place = (chosen[block_pick, 0] + jax.random.randint(keys[3], (), 1, ITEMS_DEV)) % ITEMS_DEV
    image_spot = (jnp.arange(blocks)[:, None] == block_pick) & (places == other_place)
    counts = jnp.where(image_spot, 1, counts)
    return counts.reshape(ITEMS).astype(jnp.int32)


def draw_cotangent(key, part):
    key = jax.random.fold_in(key, 7)
    row_scale = ramp(D, 0.6, 1.8)
    return bounded(key, (ITEMS, LAT, D)) * row_scale[None, None, :]


def draw_out_master(key, part):
    key = jax.random.fold_in(key, 21)
    row_scale = ramp(D, 0.6, 1.8)
    fan_width = max(2.0, D * D / (16.0 * (LAT + FRAMES * PATCHES)))
    return bounded(key, (D, D)) * fan_width ** (-0.5) * row_scale[:, None]


def draw_up_master(key, part):
    key = jax.random.fold_in(key, 33)
    row_scale = ramp(FF, 0.6, 1.8)
    return bounded(key, (D, FF)) * D ** (-0.5) * row_scale[None, :]


def draw_down_master(key, part):
    key = jax.random.fold_in(key, 45)
    row_scale = ramp(FF, 0.6, 1.8)
    return bounded(key, (FF, D)) * FF ** (-0.5) * row_scale[:, None]


def draw_norm_params(key, part):
    key = jax.random.fold_in(key, 57)
    keys = jax.random.split(key, 2)
    row_scale = ramp(D, 0.6, 1.8)
    jitter = jax.random.uniform(keys[0], (3, D), jnp.float32, 0.8, 1.25)
    gains_part = row_scale[None, :] * jitter
    biases_part = 0.3 * bounded(keys[1], (3, D))
    return jnp.stack([gains_part[0], biases_part[0], gains_part[1], biases_part[1], gains_part[2], biases_part[2]])


def block_levels(rng, dims, pieces, smallest, largest):
    level = 1.0
    for position, blocks in pieces:
        heights = jax.random.uniform(jax.random.fold_in(jax.random.fold_in(rng, 6), position), (blocks,), jnp.float32, smallest / len(pieces), largest / len(pieces))
        level = level * jnp.repeat(jnp.exp(heights), dims[position] // blocks).reshape((-1,) + (1,) * (len(dims) - 1 - position))
    return level


def bell_draw(stream_key, shape, scale, limit, shards=(), held_as=jnp.bfloat16):
    gain = block_levels(stream_key, shape, shards, -0.22, 0.18) if shards else 1.0
    result = jax.random.normal(stream_key, shape, jnp.float32) * scale * gain
    return jnp.minimum(jnp.maximum(result, -limit), limit).astype(held_as)


def setup_inputs(seed: int = 0) -> dict:
    arg_keys = jax.random.split(jax.random.key(seed), 23)
    return {
        "latents": bell_draw(arg_keys[0], (ITEMS, LAT, D), 1.0, 6.0, ((0, 8), (1, 4)), jnp.float32),
        "media": bell_draw(arg_keys[1], (ITEMS, CAP, D), 1.0, 6.0, ((0, 8), (1, 4))),
        "frames": draw_frames(jax.random.fold_in(arg_keys[22], 71), 0),
        "cotangent": draw_cotangent(jax.random.fold_in(arg_keys[22], 71), 0),
        "qkv_master": bell_draw(arg_keys[4], (3, D, D), D ** -0.5, 0.15625, ((1, 8), (2, 4)), jnp.float32),
        "qkv_momentum": bell_draw(arg_keys[5], (3, D, D), (4 * D * D) ** -0.5, 0.001953125, ((1, 8), (2, 4)), jnp.float32),
        "qkv_average": bell_draw(arg_keys[6], (3, D, D), D ** -0.5, 0.15625, ((1, 8), (2, 4)), jnp.float32),
        "out_master": draw_out_master(jax.random.fold_in(arg_keys[22], 71), 0),
        "out_momentum": bell_draw(arg_keys[8], (D, D), (300 * D * D) ** -0.5, 0.00024414062, ((0, 4), (1, 8)), jnp.float32),
        "out_average": bell_draw(arg_keys[9], (D, D), (max(2, D * D // (16 * (LAT + CAP)))) ** -0.5, 0.75, ((0, 4), (1, 8)), jnp.float32),
        "up_master": draw_up_master(jax.random.fold_in(arg_keys[22], 71), 0),
        "up_momentum": bell_draw(arg_keys[11], (D, FF), (16 * D * FF) ** -0.5, 0.00048828125, ((0, 8), (1, 4)), jnp.float32),
        "up_average": bell_draw(arg_keys[12], (D, FF), D ** -0.5, 0.15625, ((0, 8), (1, 4)), jnp.float32),
        "down_master": draw_down_master(jax.random.fold_in(arg_keys[22], 71), 0),
        "down_momentum": bell_draw(arg_keys[14], (FF, D), (6 * FF * D) ** -0.5, 0.0008544922, ((0, 4), (1, 8)), jnp.float32),
        "down_average": bell_draw(arg_keys[15], (FF, D), FF ** -0.5, 0.078125, ((0, 4), (1, 8)), jnp.float32),
        "norm_params": draw_norm_params(jax.random.fold_in(arg_keys[22], 71), 0),
        "norm_momentum": bell_draw(arg_keys[17], (6, D), (9000 * D) ** -0.5, 0.0017089844, (), jnp.float32),
        "norm_average": jnp.clip(1.0 + 0.1 * jax.random.normal(arg_keys[18], (6, D), jnp.float32), 0.5, 1.5),
        "time_table": bell_draw(arg_keys[19], (FRAMES, D), 0.5, 3.0, (), jnp.float32),
        "time_momentum": bell_draw(arg_keys[20], (FRAMES, D), (5000 * FRAMES * D) ** -0.5, 0.0007324219, (), jnp.float32),
        "time_average": bell_draw(arg_keys[21], (FRAMES, D), 0.5, 3.0, (), jnp.float32),
    }


EPS = 1e-05
MOMENT = 0.9
STEP_RATES = (30.0, 1200.0, 120.0, 40.0, 1000.0, 1200.0)
DECAY_AVG = 0.75
HIGH = lax.Precision.HIGHEST

@jax.custom_vjp
def low(v):
    return lax.optimization_barrier(v.astype(jnp.bfloat16)).astype(jnp.float32)

@jax.custom_vjp
def low_back(v):
    return v

def low_keep(v):
    return (low(v), None)

def low_pass(kept, grad):
    return (grad,)

def back_keep(v):
    return (v, None)

def back_low(kept, grad):
    return (low(grad),)
low.defvjp(low_keep, low_pass)
low_back.defvjp(back_keep, back_low)

def layer_norm(values, factor, offset):
    centered = values - lax.optimization_barrier(jnp.mean(values, axis=-1, keepdims=True))
    variance = lax.optimization_barrier(jnp.mean(centered * centered, axis=-1, keepdims=True))
    return centered * lax.rsqrt(variance + EPS) * factor + offset

def square_sum(arrays):
    running = jnp.zeros((), jnp.float32)
    for member in arrays:
        running = running + jnp.sum(member * member)
    return running

def advance(gradient, master, momentum, average, clip_factor, rate):
    clipped = gradient * clip_factor
    moment_new = MOMENT * momentum + clipped
    master_new = master - rate * (clipped + MOMENT * moment_new)
    average_new = DECAY_AVG * average + (1.0 - DECAY_AVG) * master_new
    return (clipped, master_new, moment_new, average_new)

def item_forward(weights, norm_rows, time_rows, latent, media_item, frame_count):
    w_query, w_key, w_value, w_out, w_up, w_down = weights
    slot_ids = jnp.arange(FRAMES * PATCHES)
    frame_ids = slot_ids // PATCHES
    onehot = (frame_ids[:, None] == jnp.arange(FRAMES)[None, :]).astype(jnp.float32)
    media_in = media_item + jnp.dot(onehot, time_rows, precision=HIGH)
    media_norm = low(layer_norm(media_in, norm_rows[0], norm_rows[1]))
    latent_norm = low(layer_norm(latent, norm_rows[2], norm_rows[3]))
    source = jnp.concatenate([media_norm, latent_norm], axis=0)
    queries = low(low_back(jnp.dot(latent_norm, w_query, precision=HIGH)))
    keys_all = low(low_back(jnp.dot(source, w_key, precision=HIGH)))
    values_all = low(low_back(jnp.dot(source, w_value, precision=HIGH)))
    queries_h = queries.reshape(LAT, HEADS, HEAD_DIM)
    keys_h = keys_all.reshape(-1, HEADS, HEAD_DIM)
    values_h = values_all.reshape(-1, HEADS, HEAD_DIM)
    raw_scores = jnp.einsum('qhd,khd->hqk', queries_h, keys_h, precision=HIGH)
    scores = low_back(raw_scores) * HEAD_DIM ** (-0.5)
    keep_mask = jnp.concatenate([frame_ids < frame_count, jnp.ones((LAT,), jnp.bool_)])
    scores = jnp.where(keep_mask[None, None, :], scores, -1e+30)
    prob_low = low(jax.nn.softmax(scores, axis=-1))
    mixed_heads = jnp.einsum('hqk,khd->qhd', prob_low, values_h, precision=HIGH).reshape(LAT, D)
    mixed_heads = low(low_back(mixed_heads))
    after_attn = latent + low_back(jnp.dot(mixed_heads, w_out, precision=HIGH))
    ffn_norm = low(layer_norm(after_attn, norm_rows[4], norm_rows[5]))
    pre_act = low_back(jnp.dot(ffn_norm, w_up, precision=HIGH))
    hidden = low(jax.nn.gelu(pre_act, approximate=False))
    return after_attn + low_back(jnp.dot(hidden, w_down, precision=HIGH))

def reference(latents, media, frames, cotangent, qkv_master, qkv_momentum, qkv_average, out_master, out_momentum, out_average, up_master, up_momentum, up_average, down_master, down_momentum, down_average, norm_params, norm_momentum, norm_average, time_table, time_momentum, time_average):

    def forward(latent_all, media_all, qkv_weight, out_weight, up_weight, down_weight, norm_rows, time_rows):
        weights = (low(qkv_weight[0]), low(qkv_weight[1]), low(qkv_weight[2]), low(out_weight), low(up_weight), low(down_weight))

        def one_item(packed):
            latent, media_item, frame_count = packed
            return item_forward(weights, norm_rows, time_rows, latent, media_item, frame_count)
        return lax.map(jax.checkpoint(one_item), (latent_all, media_all, frames))
    latents_out, pullback = jax.vjp(forward, latents, media.astype(jnp.float32), qkv_master, out_master, up_master, down_master, norm_params, time_table)
    latents_grad, media_grad, qkv_raw, out_raw, up_raw, down_raw, norm_raw, time_raw = pullback(cotangent)
    grad_norm = jnp.sqrt(square_sum((qkv_raw, out_raw, up_raw, down_raw, norm_raw, time_raw)))
    clip_factor = 1.0 / jnp.maximum(grad_norm, 1.0)
    qkv_grad, qkv_new, qkv_momentum_new, qkv_average_new = advance(qkv_raw, qkv_master, qkv_momentum, qkv_average, clip_factor, STEP_RATES[0])
    out_grad, out_new, out_momentum_new, out_average_new = advance(out_raw, out_master, out_momentum, out_average, clip_factor, STEP_RATES[1])
    up_grad, up_new, up_momentum_new, up_average_new = advance(up_raw, up_master, up_momentum, up_average, clip_factor, STEP_RATES[2])
    down_grad, down_new, down_momentum_new, down_average_new = advance(down_raw, down_master, down_momentum, down_average, clip_factor, STEP_RATES[3])
    norm_grad, norm_new, norm_momentum_new, norm_average_new = advance(norm_raw, norm_params, norm_momentum, norm_average, clip_factor, STEP_RATES[4])
    time_grad, time_new, time_momentum_new, time_average_new = advance(time_raw, time_table, time_momentum, time_average, clip_factor, STEP_RATES[5])
    return (latents_out, latents_grad, media_grad, grad_norm, qkv_grad, qkv_new, qkv_momentum_new, qkv_average_new, out_grad, out_new, out_momentum_new, out_average_new, up_grad, up_new, up_momentum_new, up_average_new, down_grad, down_new, down_momentum_new, down_average_new, norm_grad, norm_new, norm_momentum_new, norm_average_new, time_grad, time_new, time_momentum_new, time_average_new, qkv_new.astype(jnp.bfloat16), out_new.astype(jnp.bfloat16), up_new.astype(jnp.bfloat16), down_new.astype(jnp.bfloat16))
```

```python
import functools
import math

import jax
import jax.numpy as jnp
from jax import lax
from jax.experimental import pallas as pl
from jax.experimental.pallas import tpu as pltpu
from jax.sharding import PartitionSpec as P

HEAD_DIM = 96
FRAMES = 8
PATCHES = 256


EPS = 1e-05
MOMENT = 0.9
STEP_RATES = (30.0, 1200.0, 120.0, 40.0, 1000.0, 1200.0)
DECAY_AVG = 0.75
HIGH = lax.Precision.HIGHEST
NEGATIVE = -1e30
ROWS_IN_VMEM = 5 * 1024 * 1024


def layer_norm(values, factor, offset):
    centered = values - jnp.mean(values, axis=-1, keepdims=True)
    variance = jnp.mean(centered * centered, axis=-1, keepdims=True)
    return centered * lax.rsqrt(variance + EPS) * factor + offset


def exact_gelu(values):
    return jax.nn.gelu(values, approximate=False)


def square_sum(arrays):
    running = jnp.zeros((), jnp.float32)
    for member in arrays:
        running = running + jnp.sum(member * member)
    return running


def advance(gradient, master, momentum, average, clip_factor, rate):
    clipped = gradient * clip_factor
    moment_new = MOMENT * momentum + clipped
    master_new = master - rate * (clipped + MOMENT * moment_new)
    average_new = DECAY_AVG * average + (1.0 - DECAY_AVG) * master_new
    return (clipped, master_new, moment_new, average_new)


class Place:
    def __init__(self, dp_count, mp_count):
        z_count = 4 if dp_count % 4 == 0 else 1
        c_count = 2 if mp_count % 2 == 0 else 1
        self.size = {
            "z": z_count,
            "x": dp_count // z_count,
            "y": mp_count // c_count,
            "c": c_count,
        }
        self.count = {"dp": dp_count, "mp": mp_count}

    def mine(self):
        dp, mp = lax.axis_index("dp"), lax.axis_index("mp")
        x_count, c_count = self.size["x"], self.size["c"]
        return {
            "z": lax.div(dp, x_count),
            "x": lax.rem(dp, x_count),
            "y": lax.div(mp, c_count),
            "c": lax.rem(mp, c_count),
        }

    def shifted(self, me, axis, step):
        return {**me, axis: lax.rem(me[axis] + step, self.size[axis])}

    def device(self, at):
        return {
            "dp": at["z"] * self.size["x"] + at["x"],
            "mp": at["y"] * self.size["c"] + at["c"],
        }


def region(ref, at, chunk, whole):
    def pick(axis):
        return slice(None) if axis in whole else at[axis]

    return ref.at[pick("y"), pick("c"), chunk[0], pick("z"), pick("x"), chunk[1]]


def remote(src, dst, send, recv, device):
    return pltpu.make_async_remote_copy(
        src_ref=src,
        dst_ref=dst,
        send_sem=send,
        recv_sem=recv,
        device_id=device,
        device_id_type=pl.DeviceIdType.MESH,
    )


def greet(devices):
    barrier = pltpu.get_barrier_semaphore()
    for device in devices:
        pl.semaphore_signal(
            barrier, inc=1, device_id=device, device_id_type=pl.DeviceIdType.MESH
        )
    pl.semaphore_wait(barrier, len(devices))


class Swap:
    def __init__(self, place, axis, spread, value, late=0):
        self.place, self.axis, self.spread, self.value = place, axis, spread, value
        self.late = late
        self.n = place.count[axis]
        shape = value.shape if spread else (self.n,) + value.shape
        self.out = jax.ShapeDtypeStruct(shape, value.dtype)
        self.scratch = [
            pltpu.SemaphoreType.DMA((self.n,)),
            pltpu.SemaphoreType.DMA((self.n,)),
        ]

    def peers(self):
        rank = lax.axis_index(self.axis)
        return [{self.axis: lax.rem(rank + k, self.n)} for k in range(1, self.n)]

    def begin(self, refs):
        self.refs = refs

    def steps(self):
        return self.late + 1

    def own(self):
        src, dst, send, _ = self.refs
        rank = lax.axis_index(self.axis)
        return pltpu.make_async_copy(
            src.at[rank] if self.spread else src, dst.at[rank], send.at[0]
        )

    def copies(self, receive):
        src, dst, send, recv = self.refs
        rank = lax.axis_index(self.axis)
        for k in range(1, self.n):
            there, here = lax.rem(rank + k, self.n), lax.rem(rank + self.n - k, self.n)
            yield remote(
                src.at[there] if self.spread else src,
                dst.at[here if receive else rank],
                send.at[k],
                recv.at[k],
                {self.axis: there},
            )

    def step(self, time):
        if time == self.late:
            self.own().start()
            for copy in self.copies(False):
                copy.start()

    def finish(self):
        self.own().wait()
        for copy in self.copies(False):
            copy.wait_send()
        for copy in self.copies(True):
            copy.wait_recv()


def pair_at(index, chunks):
    return [n for n in (2 * index, 2 * index + 1) if 0 <= n < len(chunks)]


GATHER_STAGES = (0, 2, 1, 3, 4)
REDUCE_STAGES = (4, 3, 2, 1, 0)
ORDERS = (("z", "x", "y", "c"), ("z", "y", "x", "c"))


class Gather:
    def __init__(self, place, value, late=0):
        self.place, self.value, self.late = place, value, late
        s = place.size
        t, h = value.shape[:2]
        self.chunks = [(a, b) for a in range(t) for b in range(h)]
        self.out = jax.ShapeDtypeStruct(
            (s["y"], s["c"], t, s["z"], s["x"], h) + value.shape[2:], value.dtype
        )
        self.most = max(s.values())
        sems = pltpu.SemaphoreType.DMA((len(self.chunks), 5, self.most))
        self.scratch = [sems, sems]

    def peers(self):
        me = self.place.mine()
        return [
            self.place.device(self.place.shifted(me, a, k))
            for a in "zxyc"
            for k in range(1, self.place.size[a])
        ]

    def copies(self, n, stage, receive):
        src, dst, send, recv = self.refs
        order = ORDERS[n % 2]
        axis, whole = order[stage], order[:stage]
        me = self.me
        for k in range(1, self.place.size[axis]):
            there = self.place.shifted(me, axis, k)
            here = self.place.shifted(me, axis, self.place.size[axis] - k)
            at = here if receive else me
            block = (
                src.at[self.chunks[n][0], self.chunks[n][1]]
                if stage == 0
                else region(dst, me, self.chunks[n], whole)
            )
            yield remote(
                block,
                region(dst, at, self.chunks[n], whole),
                send.at[n, stage, k],
                recv.at[n, stage, k],
                self.place.device(there),
            )

    def begin(self, refs):
        self.refs, self.me = refs, self.place.mine()

    def own(self, n):
        src, dst, send, _ = self.refs
        chunk = self.chunks[n]
        return pltpu.make_async_copy(
            src.at[chunk[0], chunk[1]], region(dst, self.me, chunk, ()), send.at[n, 4, 0]
        )

    def steps(self):
        return self.late + pl.cdiv(len(self.chunks), 2) + 4

    def step(self, time):
        for stage in GATHER_STAGES:
            for n in pair_at(time - self.late - stage, self.chunks):
                if stage == 0:
                    self.own(n).start()
                if stage == 1:
                    self.own(n).wait()
                if stage > 0:
                    for copy in self.copies(n, stage - 1, True):
                        copy.wait_recv()
                if stage < 4:
                    for copy in self.copies(n, stage, False):
                        copy.start()

    def finish(self):
        for n in range(len(self.chunks)):
            for stage in range(4):
                for copy in self.copies(n, stage, False):
                    copy.wait_send()


BACK_ORDERS = (("c", "y", "x", "z"), ("c", "x", "y", "z"))
LAYOUT = ("y", "z", "x")


class Reduce:
    def __init__(self, place, value, late=0, starts=None, kept=None):
        self.place, self.value = place, value
        s = place.size
        t, h = value.shape[2], value.shape[5]
        tail = value.shape[6:]
        self.chunks = [(a, b) for a in range(t) for b in range(h)]
        self.out = jax.ShapeDtypeStruct((t, h) + tail, jnp.float32)
        count = len(self.chunks)
        pairs = pl.cdiv(count, 2)
        self.starts = [late + k for k in range(pairs)] if starts is None else starts
        self.kept = count if kept is None else min(kept, count)
        sems = pltpu.SemaphoreType.DMA((count, 5, max(s.values())))
        full = tuple(s[a] for a in LAYOUT)
        held = pltpu.VMEM((self.kept,) + full + tail, value.dtype)
        self.scratch = [sems, sems, held, held]
        self.spots = {}
        for parity in range(min(2, count)):
            mine = (count + 1 - parity) // 2
            left = list(LAYOUT)
            for stage, axis in list(enumerate(BACK_ORDERS[parity]))[1:]:
                left.remove(axis)
                shape = (mine, max(s[axis] - 1, 1)) + tuple(s[a] for a in left) + tail
                self.spots[parity, stage] = len(self.scratch)
                self.scratch.append(pltpu.VMEM(shape, value.dtype))
        self.out_spot = len(self.scratch)
        self.scratch.append(pltpu.VMEM((t, h) + tail, jnp.float32))
        self.scratch.append(pltpu.SemaphoreType.DMA((1,)))
        self.scratch.append(pltpu.SemaphoreType.REGULAR)

    peers = Gather.peers

    def part(self, n, stage, at):
        order = BACK_ORDERS[n % 2]
        if stage == 0:
            t, h = self.chunks[n]
            return self.src.at[:, at, t, :, :, h]
        index = tuple(
            at if a == order[stage] else self.me[a] if a in order[:stage] else slice(None)
            for a in LAYOUT
        )
        return self.scr[2].at[(n % self.kept,) + index]

    def into(self, n, stage):
        if stage == 0:
            return self.scr[3].at[pl.ds(n % self.kept, 1)]
        return self.scr[self.spots[n % 2, stage]].at[n // 2]

    def copies(self, n, stage):
        axis = BACK_ORDERS[n % 2][stage]
        for k in range(1, self.place.size[axis]):
            there = self.place.shifted(self.me, axis, k)
            yield remote(
                self.part(n, stage, there[axis]),
                self.into(n, stage).at[k - 1],
                self.scr[0].at[n, stage, k],
                self.scr[1].at[n, stage, k],
                self.place.device(there),
            )

    def own(self, n):
        t, h = self.chunks[n]
        return pltpu.make_async_copy(
            self.src.at[:, self.me["c"], t, :, :, h],
            self.scr[2].at[n % self.kept],
            self.scr[0].at[n, 4, 0],
        )

    def begin(self, refs):
        self.src, self.dst, self.scr = refs[0], refs[1], refs[2:]
        self.me = self.place.mine()

    def steps(self):
        return self.starts[-1] + 5

    def add(self, n, stage):
        order = BACK_ORDERS[n % 2]
        axis = order[stage]
        count = self.place.size[axis] - 1
        into = self.into(n, stage)
        sizes = [self.place.size[a] for a in LAYOUT if a not in order[: stage + 1]]
        if stage == 0:
            base = target = self.scr[2].at[n % self.kept]
        else:
            base = target = self.part(n, stage, self.me[axis])
        if stage == 3:
            target = self.scr[self.out_spot].at[self.chunks[n][0], self.chunks[n][1]]

        def one(flat, carry):
            index = []
            rest = flat
            for size in reversed(sizes):
                index.insert(0, lax.rem(rest, size))
                rest = lax.div(rest, size)
            index = tuple(index) + (Ellipsis,)
            if count == 1 and target.dtype == base.dtype:
                target[index] = base[index] + into[(0,) + index]
                return carry
            value = base[index].astype(jnp.float32)
            for k in range(count):
                value = value + into[(k,) + index].astype(jnp.float32)
            target[index] = value.astype(target.dtype)
            return carry

        total = math.prod(sizes)
        if total == 1:
            one(jnp.int32(0), 0)
        else:
            lax.fori_loop(0, total, one, 0)

    def step(self, time):
        for stage in REDUCE_STAGES:
            for pair, start in enumerate(self.starts):
                if start + stage == time:
                    self.advance(pair, stage)

    def advance(self, pair, stage):
        sibling = self.place.device(self.place.shifted(self.me, "c", 1))
        reused = len(self.chunks) > self.kept and self.place.size["c"] > 1
        for n in pair_at(pair, self.chunks):
            if stage == 0:
                if n >= self.kept:
                    for old in range(4):
                        for copy in self.copies(n - self.kept, old):
                            copy.wait_send()
                    if reused:
                        pl.semaphore_wait(self.scr[-1], 1)
                self.own(n).start()
            if stage == 1:
                self.own(n).wait()
            if stage > 0:
                for copy in self.copies(n, stage - 1):
                    copy.wait_recv()
                self.add(n, stage - 1)
            if stage == 1 and reused and n + self.kept < len(self.chunks):
                pl.semaphore_signal(
                    self.scr[-1],
                    inc=1,
                    device_id=sibling,
                    device_id_type=pl.DeviceIdType.MESH,
                )
            if stage < 4:
                for copy in self.copies(n, stage):
                    copy.start()

    def finish(self):
        out = pltpu.make_async_copy(self.scr[self.out_spot], self.dst, self.scr[-2].at[0])
        out.start()
        for n in range(max(0, len(self.chunks) - self.kept), len(self.chunks)):
            for stage in range(4):
                for copy in self.copies(n, stage):
                    copy.wait_send()
        out.wait()


class Total:
    AXES = ("c", "y", "x", "z")

    def __init__(self, place, value):
        self.place, self.value = place, value
        self.out = jax.ShapeDtypeStruct(value.shape, value.dtype)
        sems = pltpu.SemaphoreType.DMA((4, max(place.size.values())))
        self.scratch = [sems, sems] + [
            pltpu.VMEM((place.size[a],) + value.shape, value.dtype) for a in self.AXES
        ]

    peers = Gather.peers

    def begin(self, refs):
        self.src, self.dst, self.send, self.recv = refs[:4]
        self.bufs = refs[4:]
        self.me = self.place.mine()

    def copies(self, stage, receive):
        axis = self.AXES[stage]
        size = self.place.size[axis]
        buf, me = self.bufs[stage], self.me
        for k in range(1, size):
            there = self.place.shifted(me, axis, k)
            here = self.place.shifted(me, axis, size - k)
            yield remote(
                buf.at[me[axis]],
                buf.at[here[axis] if receive else me[axis]],
                self.send.at[stage, k],
                self.recv.at[stage, k],
                self.place.device(there),
            )

    def advance(self, stage):
        if stage == 0:
            value = self.src[...]
        else:
            for copy in self.copies(stage - 1, True):
                copy.wait_recv()
            for copy in self.copies(stage - 1, False):
                copy.wait_send()
            value = self.bufs[stage - 1][0]
            for k in range(1, self.place.size[self.AXES[stage - 1]]):
                value = value + self.bufs[stage - 1][k]
        if stage == 4:
            self.dst[...] = value
            return
        self.bufs[stage][self.me[self.AXES[stage]]] = value
        for copy in self.copies(stage, False):
            copy.start()


def norm_back(value, factor, pulled):
    centered = value - jnp.mean(value, axis=-1, keepdims=True)
    variance = jnp.mean(centered * centered, axis=-1, keepdims=True)
    scale = lax.rsqrt(variance + EPS)
    unit = centered * scale
    inner = pulled * factor
    back = scale * (
        inner
        - jnp.mean(inner, axis=-1, keepdims=True)
        - unit * jnp.mean(inner * unit, axis=-1, keepdims=True)
    )
    return (
        back,
        jnp.sum(pulled * unit, axis=0, keepdims=True),
        jnp.sum(pulled, axis=0, keepdims=True),
    )


def communicate(label, number, parts):
    count = len(parts)

    def kernel(*refs):
        ins, outs, rest = refs[:count], refs[count : 2 * count], refs[2 * count :]
        devices, seen = [], set()
        for part in parts:
            kind = part.axis if isinstance(part, Swap) else "grid"
            if kind not in seen:
                seen.add(kind)
                devices += part.peers()
        greet(devices)
        spot = 0
        for part, src, dst in zip(parts, ins, outs):
            size = len(part.scratch)
            part.begin((src, dst) + tuple(rest[spot : spot + size]))
            spot += size
        staged = parts
        for time in range(max([part.steps() for part in staged], default=0)):
            for part in staged:
                part.step(time)
        for part in parts:
            part.finish()

    return pl.pallas_call(
        kernel,
        out_shape=[part.out for part in parts],
        in_specs=[pl.BlockSpec(memory_space=pl.ANY)] * count,
        out_specs=[pl.BlockSpec(memory_space=pl.ANY)] * count,
        scratch_shapes=[s for part in parts for s in part.scratch],
        compiler_params=pltpu.CompilerParams(
            collective_id=number, has_side_effects=True, vmem_limit_bytes=58 * 1024 * 1024
        ),
        name=label,
    )(*[part.value for part in parts])


def product(left, right, dims):
    return lax.dot_general(left, right, (dims, ((), ())), preferred_element_type=jnp.float32)


NN, NT, TN = ((1,), (0,)), ((1,), (1,)), ((0,), (0,))


def spread_heads(rows, heads):
    owner = lax.broadcasted_iota(jnp.int32, rows.shape, 1)
    kept = [
        jnp.where((owner >= h * HEAD_DIM) & (owner < (h + 1) * HEAD_DIM), rows, 0)
        for h in range(heads)
    ]
    return jnp.concatenate(kept, axis=0)


def fold_heads(wide, heads):
    rows = wide.shape[0] // heads
    owner = lax.broadcasted_iota(jnp.int32, (rows, wide.shape[1]), 1)
    out = wide[:rows]
    for h in range(1, heads):
        out = jnp.where(owner >= h * HEAD_DIM, wide[h * rows : (h + 1) * rows], out)
    return out


def as_row(column):
    wide = jnp.broadcast_to(column, (column.shape[0], 128))
    return jnp.transpose(wide)[:1]


def as_column(row):
    return jnp.transpose(jnp.broadcast_to(row, (128, row.shape[1])))[:, :1]


def front_kernel(place, heads, scale, halves_w, parts, *refs):
    half, f32 = jnp.bfloat16, jnp.float32
    own_w, cot, lat_in, media, keep, time_rows, norms = refs[:7]
    w_o, back_o, src_o, lat_o, q_o, p_o, blend_o, mixed_o, stat_o = refs[7:16]
    w_vm, lat_vm, src_vm, q_vm, p_vm, blend_vm, mixed_vm, stat_vm, sems = refs[16:25]
    rest = list(refs[25:])
    gather_w, gather_c, lat_swap, mixed_swap, stat_swap = parts
    ends = (
        (own_w, w_vm),
        (cot, back_o),
        (lat_in, lat_vm),
        (mixed_vm, mixed_o),
        (stat_vm, stat_o),
    )
    for part, end in zip(parts, ends):
        size = len(part.scratch)
        part.begin(end + tuple(rest[:size]))
        rest = rest[size:]
    items, slots, width = media.shape
    lat_own = lat_in.shape[1]
    blocks, block = q_vm.shape[0], q_vm.shape[3]
    lat_total = blocks * lat_own
    c_count = place.size["c"]
    mp_rank = lax.axis_index("mp")
    greet(gather_w.peers() + lat_swap.peers())
    clock = [0]

    def run_to(time):
        while clock[0] <= time:
            for part in (lat_swap, gather_w, gather_c):
                part.step(clock[0])
            clock[0] += 1

    def arrived(t):
        return 4 + ((t + 1) * halves_w - 1) // 2

    def weight(j, t):
        return w_vm[lax.div(j, c_count), lax.rem(j, c_count), t].reshape(width, block)

    kept = []

    def keep_copy(src, dst):
        copy = pltpu.make_async_copy(src, dst, sems.at[len(kept)])
        copy.start()
        kept.append(copy)

    run_to(0)
    step_rows = math.gcd(64, slots)
    per_item = slots // step_rows

    def norm_media(k, carry):
        item, first = lax.div(k, per_item), lax.rem(k, per_item) * step_rows
        first = pl.multiple_of(first, step_rows)
        frame = lax.div(mp_rank * slots + first, PATCHES)
        value = media[item, pl.ds(first, step_rows)].astype(f32) + time_rows[pl.ds(frame, 1)]
        value = layer_norm(value, norms[0:1], norms[1:2])
        src_vm[item, pl.ds(first, step_rows)] = value.astype(half)
        return carry

    lax.fori_loop(0, items * per_item, norm_media, 0)
    src_vm[:, slots:] = lat_in[...]
    keep_copy(src_vm, src_o)
    run_to(3)
    lat_swap.finish()
    keep_copy(lat_vm, lat_o)
    run_to(arrived(0))

    def ask(j, carry):
        rows = jnp.concatenate(
            [lat_vm[:, n].reshape(lat_total, width) for n in range(items)], axis=0
        )
        query = product(rows, weight(j, 0), NN).astype(half)
        q_vm[j] = query.reshape(items, lat_total, block)
        return carry

    lax.fori_loop(0, blocks, ask, 0)
    keep_copy(q_vm, q_o)
    run_to(arrived(1))

    def score(k, carry):
        j, n = lax.div(k, items), lax.rem(k, items)
        source = src_vm[n]
        reach = product(spread_heads(q_vm[j, n], heads), weight(j, 1), NT).astype(half)
        value = product(reach, source, NT) * scale
        value = jnp.where(keep[n] > 0, value, NEGATIVE)
        peak = jnp.max(value, axis=1, keepdims=True)
        raised = jnp.exp(value - peak)
        total = jnp.sum(raised, axis=1, keepdims=True)
        low = raised.astype(half)
        p_vm[j, n] = low
        blend_vm[j, n] = product(low, source, NN).astype(half)
        stat_vm[j, n, 0:1] = as_row(peak)
        stat_vm[j, n, 1:2] = as_row(total)
        return carry

    lax.fori_loop(0, blocks * items // 2, score, 0)
    run_to(max(arrived(1) + 1, arrived(2)))
    lax.fori_loop(blocks * items // 2, blocks * items, score, 0)
    keep_copy(p_vm, p_o)
    keep_copy(blend_vm, blend_o)

    def mix(k, carry):
        j, n = lax.div(k, items), lax.rem(k, items)
        value = fold_heads(product(blend_vm[j, n], weight(j, 2), NN), heads)
        mixed_vm[:, j, n] = value.reshape(blocks, lat_own, block)
        return carry

    lax.fori_loop(0, blocks * items, mix, 0)
    mixed_swap.step(0)
    stat_swap.step(0)
    run_to(arrived(3))
    keep_copy(w_vm, w_o)
    run_to(gather_c.steps())
    for part in parts:
        if part is not lat_swap:
            part.finish()
    for copy in kept:
        copy.wait()


def front(
    place, own_weights, cot, latent_norm, media, keep, time_rows, norms, heads, scale
):
    half, f32 = jnp.bfloat16, jnp.float32
    items, slots, width = media.shape
    lat_own = latent_norm.shape[1]
    blocks, block = place.count["mp"], own_weights.shape[3]
    lat, keys = blocks * lat_own, slots + lat_own
    rows = heads * lat
    halves_w = own_weights.shape[1]
    late = 2 * halves_w
    mixed = jax.ShapeDtypeStruct((blocks, blocks, items, lat_own, block), f32)
    stats = jax.ShapeDtypeStruct((blocks, items, 2, rows), f32)
    parts = [
        Gather(place, own_weights),
        Gather(place, cot, late),
        Swap(place, "mp", False, latent_norm),
        Swap(place, "mp", True, mixed),
        Swap(place, "mp", False, stats),
    ]
    shapes = [
        parts[0].out,
        parts[2].out,
        jax.ShapeDtypeStruct((items, keys, width), half),
        jax.ShapeDtypeStruct((blocks, items, lat, block), half),
        jax.ShapeDtypeStruct((blocks, items, rows, keys), half),
        jax.ShapeDtypeStruct((blocks, items, rows, width), half),
        mixed,
        stats,
    ]
    scratch = [pltpu.VMEM(shape.shape, shape.dtype) for shape in shapes]
    scratch.append(pltpu.SemaphoreType.DMA((8,)))
    for part in parts:
        scratch += part.scratch
    whole = pl.BlockSpec(memory_space=pltpu.VMEM)
    hbm = pl.BlockSpec(memory_space=pl.ANY)
    return pl.pallas_call(
        functools.partial(front_kernel, place, heads, scale, halves_w, parts),
        in_specs=[hbm, hbm, whole, whole, whole, whole, whole],
        out_specs=[hbm] * 9,
        out_shape=[
            parts[0].out,
            parts[1].out,
            shapes[2],
            parts[2].out,
            shapes[3],
            shapes[4],
            shapes[5],
            parts[3].out,
            parts[4].out,
        ],
        scratch_shapes=scratch,
        compiler_params=pltpu.CompilerParams(
            collective_id=1, has_side_effects=True, vmem_limit_bytes=64 * 1024 * 1024 - 65536
        ),
        name="front",
    )(own_weights, cot, latent_norm, media, keep, time_rows, norms)


def feed_kernel(place, parts, *refs):
    half, f32 = jnp.bfloat16, jnp.float32
    own_rows, up_in, down_in, back_rows, after_attn, cot, mixed, norms, weights = refs[:9]
    (norm_o, ffn_o, up_o, down_o, back_o, term_o, after_o, low_o, sums_o) = refs[9:18]
    (rows_vm, up_vm, down_vm, share_a, share_b, up_give, down_give, w_out) = refs[18:26]
    (hid_vm, pre_vm, mixed_vm, term_vm, sem) = refs[26:31]
    rest = list(refs[31:])
    gather, up_swap, down_swap, first, second, up_back, down_back, back_swap, term_swap = parts
    ends = (
        (own_rows, rows_vm),
        (up_in, up_vm),
        (down_in, down_vm),
        (share_a, norm_o),
        (share_b, ffn_o),
        (up_give, up_o),
        (down_give, down_o),
        (mixed_vm, back_o),
        (term_vm, term_o),
    )
    for part, end in zip(parts, ends):
        size = len(part.scratch)
        part.begin(end + tuple(rest[:size]))
        rest = rest[size:]
    c_count, blocks = place.size["c"], place.count["mp"]
    width, units = norms.shape[1], hid_vm.shape[2]
    greet(gather.peers() + up_swap.peers() + back_swap.peers())
    out_weight = pltpu.make_async_copy(weights.at[:, 3], w_out, sem.at[0])
    gather.step(0)
    up_swap.step(0)
    down_swap.step(0)
    out_weight.start()
    for time in range(1, gather.steps()):
        gather.step(time)
    up_swap.finish()
    down_swap.finish()

    def inner(m, carry):
        y, c = lax.div(m, c_count), lax.rem(m, c_count)
        w_up, w_down = up_vm[...].reshape(width, units), down_vm[...].reshape(width, units)
        rows = rows_vm[y, c].reshape(-1, width)
        pre = product(rows, w_up, NN)
        pulled = product(back_rows[y, c].reshape(-1, width), w_down, NN)
        chance = 0.5 * (1.0 + lax.erf(pre * math.sqrt(0.5)))
        slope = chance + pre * jnp.exp(-0.5 * pre * pre) * math.sqrt(0.5 / math.pi)
        hid_vm[m] = (pre * chance).astype(half)
        pre_back = (pulled * slope).astype(half)
        pre_vm[m] = pre_back
        share = product(pre_back, w_up, NT).astype(half)
        share_a[y, c] = share.reshape(share_a.shape[2:])
        return carry

    lax.fori_loop(0, blocks, inner, 0)
    first.step(0)

    def outer(m, carry):
        y, c = lax.div(m, c_count), lax.rem(m, c_count)
        share = product(hid_vm[m], down_vm[...].reshape(width, units), NT).astype(half)
        share_b[y, c] = share.reshape(share_b.shape[2:])
        return carry

    lax.fori_loop(0, blocks, outer, 0)
    first.step(1)
    second.step(0)
    give = product(rows_vm[...].reshape(-1, width), pre_vm[...].reshape(-1, units), TN)
    up_give[...] = give.astype(half).reshape(up_give.shape)
    give = product(back_rows[...].reshape(-1, width), hid_vm[...].reshape(-1, units), TN)
    down_give[...] = give.astype(half).reshape(down_give.shape)
    first.step(2)
    second.step(1)
    up_back.step(0)
    down_back.step(0)
    first.step(3)
    second.step(2)
    first.step(4)
    pulled = first.scr[first.out_spot]
    factors = jnp.zeros((1, width), f32)
    offsets = jnp.zeros((1, width), f32)
    for t in range(after_attn.shape[0]):
        value, factor, offset = norm_back(after_attn[t], norms[4:5], pulled[t, 0])
        value = cot[t] + value
        after_o[t] = value
        low_o[t] = value.astype(half)
        factors += factor
        offsets += offset
    sums_o[0:1] = factors
    sums_o[1:2] = offsets
    out_weight.wait()
    low = low_o[...].reshape(-1, width)
    heads = term_vm.shape[2]
    for j in range(blocks):
        back = product(low, w_out[j].reshape(width, -1), NN).astype(half)
        mixed_vm[j] = back
        both = mixed[j] * back.astype(f32)
        owner = lax.broadcasted_iota(jnp.int32, both.shape, 1)
        place_of = lax.broadcasted_iota(jnp.int32, (both.shape[0], heads), 1)
        terms = jnp.zeros((both.shape[0], heads), f32)
        for h in range(heads):
            mine = (owner >= h * HEAD_DIM) & (owner < (h + 1) * HEAD_DIM)
            term = jnp.sum(jnp.where(mine, both, 0.0), axis=1, keepdims=True)
            terms = jnp.where(place_of == h, term, terms)
        term_vm[j] = terms
    back_swap.step(0)
    term_swap.step(0)
    second.step(3)
    second.step(4)
    for part in (gather, first, second, up_back, down_back, back_swap, term_swap):
        part.finish()


def feed(place, own_rows, up_pieces, down_pieces, back_rows, after_attn, cot, mixed, norms, weights):
    half, f32 = jnp.bfloat16, jnp.float32
    gather = Gather(place, own_rows)
    rows = gather.out
    width = norms.shape[1]
    blocks, flat, block = mixed.shape
    heads = block // HEAD_DIM
    units = up_pieces.shape[2]
    per = math.prod(rows.shape[2:7])
    mixed_back = jax.ShapeDtypeStruct(mixed.shape, half)
    terms = jax.ShapeDtypeStruct((blocks, flat, heads), f32)
    parts = [
        gather,
        Swap(place, "dp", True, up_pieces),
        Swap(place, "dp", True, down_pieces),
        Reduce(place, rows),
        Reduce(place, rows),
        Swap(place, "dp", True, up_pieces),
        Swap(place, "dp", True, down_pieces),
        Swap(place, "mp", False, mixed_back),
        Swap(place, "mp", False, terms),
    ]
    scratch = [
        pltpu.VMEM(rows.shape, half),
        pltpu.VMEM(up_pieces.shape, half),
        pltpu.VMEM(down_pieces.shape, half),
        pltpu.VMEM(rows.shape, half),
        pltpu.VMEM(rows.shape, half),
        pltpu.VMEM(up_pieces.shape, half),
        pltpu.VMEM(down_pieces.shape, half),
        pltpu.VMEM(weights.shape[:1] + weights.shape[2:], half),
        pltpu.VMEM((blocks, per, units), half),
        pltpu.VMEM((blocks, per, units), half),
        pltpu.VMEM(mixed.shape, half),
        pltpu.VMEM(terms.shape, f32),
        pltpu.SemaphoreType.DMA((1,)),
    ]
    for part in parts:
        scratch += part.scratch
    whole = pl.BlockSpec(memory_space=pltpu.VMEM)
    hbm = pl.BlockSpec(memory_space=pl.ANY)
    return pl.pallas_call(
        functools.partial(feed_kernel, place, parts),
        in_specs=[hbm, hbm, hbm] + [whole] * 5 + [hbm],
        out_specs=[hbm] * 6 + [whole] * 3,
        out_shape=[part.out for part in parts[3:]]
        + [
            jax.ShapeDtypeStruct(after_attn.shape, f32),
            jax.ShapeDtypeStruct(after_attn.shape, half),
            jax.ShapeDtypeStruct((2, width), f32),
        ],
        scratch_shapes=scratch,
        compiler_params=pltpu.CompilerParams(
            collective_id=3, has_side_effects=True, vmem_limit_bytes=60 * 1024 * 1024
        ),
        name="feed",
    )(own_rows, up_pieces, down_pieces, back_rows, after_attn, cot, mixed, norms, weights)


def feed_apart(place, own_rows, up_pieces, down_pieces, back_rows, after_attn, cot, mixed, norms, weights):
    half, f32 = jnp.bfloat16, jnp.float32
    width, units = norms.shape[1], up_pieces.shape[2]
    dot = functools.partial(jnp.einsum, preferred_element_type=f32)
    ffn_rows, up_pieces, down_pieces = communicate(
        "rows",
        3,
        [
            Gather(place, own_rows),
            Swap(place, "dp", True, up_pieces, 1),
            Swap(place, "dp", True, down_pieces, 1),
        ],
    )
    shape, pieces_shape = ffn_rows.shape, up_pieces.shape
    w_up, w_down = up_pieces.reshape(width, units), down_pieces.reshape(width, units)
    ffn_rows, back_rows = ffn_rows.reshape(-1, width), back_rows.reshape(-1, width)
    pre_act = dot("rd,df->rf", ffn_rows, w_up)
    hidden = exact_gelu(pre_act).astype(half)
    hidden_back = dot("rd,df->rf", back_rows, w_down)
    pre_back = jax.vjp(exact_gelu, pre_act)[1](hidden_back)[0].astype(half)
    norm_part = dot("rf,df->rd", pre_back, w_up).astype(half)
    ffn_part = dot("rf,df->rd", hidden, w_down).astype(half)
    down_part = dot("rd,rf->df", back_rows, hidden).astype(half)
    up_part = dot("rd,rf->df", ffn_rows, pre_back).astype(half)
    norm_pulled, ffn_out, up_owned, down_owned = communicate(
        "ffn",
        4,
        [
            Reduce(place, norm_part.reshape(shape)),
            Reduce(place, ffn_part.reshape(shape)),
            Swap(place, "dp", True, up_part.reshape(pieces_shape), 1),
            Swap(place, "dp", True, down_part.reshape(pieces_shape), 1),
        ],
    )
    pull = jax.vjp(layer_norm, after_attn, norms[4], norms[5])[1]
    through, factor, offset = pull(norm_pulled.reshape(after_attn.shape))
    after_back = cot + through
    low = after_back.astype(half)
    mixed_back = dot("ld,jde->jle", low.reshape(-1, width), weights[:, 3]).astype(half)
    terms = jnp.sum(
        (mixed * mixed_back.astype(f32)).reshape(*mixed.shape[:2], -1, HEAD_DIM), axis=-1
    )
    mixed_rows, terms = communicate(
        "back", 5, [Swap(place, "mp", False, mixed_back), Swap(place, "mp", False, terms)]
    )
    sums = jnp.stack([factor, offset])
    return (
        norm_pulled,
        ffn_out,
        up_owned,
        down_owned,
        mixed_rows,
        terms,
        after_back,
        low,
        sums,
    )


def attend_back_kernel(place, heads, scale, reduce, latent_swap, totals, *refs):
    half, f32 = jnp.bfloat16, jnp.float32
    (src, lat, q, p, blend, back, mix, low, row, wq, wk, wv, up_vm, down_vm) = refs[:14]
    (media, time_rows, norms, latents, after_back, ffn_sums) = refs[14:20]
    (grad_o, media_o, owned_o, latents_o, small_o, square_o) = refs[20:26]
    (acc, lat_acc, lat_vm, kept, stage_a, stage_b, small, square, stage_sem) = refs[26:35]
    rest = list(refs[35:])
    phase, block = pl.program_id(0), pl.program_id(1)
    blocks = pl.num_programs(1)
    items = src.shape[0]
    lat_total = lat.shape[1]
    width = src.shape[2]
    for part, give, out in (
        (reduce, grad_o, owned_o),
        (latent_swap, lat_acc, lat_vm),
        (totals[0], small, small_o),
        (totals[1], square, square_o),
    ):
        size = len(part.scratch)
        part.begin((give, out) + tuple(rest[:size]))
        rest = rest[size:]

    def at(number, index, action):
        pl.when((phase == number) & (block == index))(action)

    last = place.count["mp"] - 1
    plan, moves_1, moves_2 = reduce_plan(len(reduce.chunks), place.count["mp"], items)
    c_count = place.size["c"]
    y_of, c_of = lax.div(block, c_count), lax.rem(block, c_count)

    def staged(t, buffer, number):
        return pltpu.make_async_copy(buffer, grad_o.at[y_of, c_of, t], stage_sem.at[number])

    def hand_over(first, first_value, second, second_value):
        @pl.when(block > 0)
        def _():
            staged(first, stage_a, 0).wait()
            staged(second, stage_b, 1).wait()

        stage_a[...] = first_value.astype(half).reshape(stage_a.shape)
        stage_b[...] = second_value.astype(half).reshape(stage_b.shape)
        staged(first, stage_a, 0).start()
        staged(second, stage_b, 1).start()

        @pl.when(block == last)
        def _():
            staged(first, stage_a, 0).wait()
            staged(second, stage_b, 1).wait()

    def column(item, which):
        return as_column(row[0, item, which : which + 1])

    at(0, 0, lambda: greet(latent_swap.peers() + reduce.peers()))

    @pl.when(phase == 0)
    def _():
        back_s = jnp.concatenate(
            [
                (spread_heads(back[0, n], heads) * column(n, 0)).astype(half)
                for n in range(items)
            ],
            axis=0,
        )
        value_grad = product(blend[0].reshape(back_s.shape[0], width), back_s, TN)
        out_grad = product(
            low[...].reshape(-1, width), mix[0].reshape(-1, mix.shape[3]), TN
        )
        hand_over(3, out_grad, 2, value_grad)

    def events(number, half_step):
        for (where, point), moves in plan.items():
            if where == number and point % items == half_step:

                def carry_out(moves=moves):
                    for move in moves:
                        reduce.advance(*move)

                at(where, point // items, carry_out)

    at(1, 0, lambda: reduce.advance(0, 0))

    @pl.when(phase == 1)
    def _():
        turns, queries, query_backs = [], [], []
        for n in range(items):
            back_s = spread_heads(back[0, n], heads)
            pull = product(back_s, wv[0, 0], NT).astype(half)
            prob_back = product(pull, src[n], NT)
            score_back = (
                p[0, n].astype(jnp.float32) * (column(n, 0) * scale) * (prob_back - column(n, 1))
            ).astype(half)
            kept[block, n] = score_back
            turn = product(score_back, src[n], NN).astype(half)
            query_back = fold_heads(product(turn, wk[0, 0], NN), heads).astype(half)
            latent_back = product(query_back, wq[0, 0], NT)
            latent_back = latent_back.reshape(lat_acc.shape[0], -1, width)

            @pl.when(block == 0)
            def _():
                lat_acc[:, n] = latent_back

            @pl.when(block > 0)
            def _():
                lat_acc[:, n] += latent_back

            turns.append(turn)
            queries.append(spread_heads(q[0, n], heads))
            query_backs.append(query_back)
            if n + 1 < items:
                events(1, n)
        key_grad = product(
            jnp.concatenate(turns, axis=0), jnp.concatenate(queries, axis=0), TN
        )
        query_grad = product(
            lat[...].reshape(items * lat_total, width), jnp.concatenate(query_backs, axis=0), TN
        )
        hand_over(1, key_grad, 0, query_grad)

    events(1, items - 1)
    at(1, last, lambda: latent_swap.step(0))

    @pl.when(phase == 2)
    def _():
        for n in range(items):
            pull = product(spread_heads(back[0, n], heads), wv[0, 0], NT)
            reach = product(spread_heads(q[0, n], heads), wk[0, 0], NT)
            value = product(
                jnp.concatenate([kept[block, n], p[0, n]], axis=0),
                jnp.concatenate([reach.astype(half), (pull * column(n, 0)).astype(half)], axis=0),
                TN,
            )

            @pl.when(block == 0)
            def _():
                acc[n] = value

            @pl.when(block > 0)
            def _():
                acc[n] += value

            if n + 1 < items:
                events(2, n)

    events(2, items - 1)

    slots = media.shape[1]
    step_rows = math.gcd(64, slots)
    per_item = slots // step_rows
    mp_rank = lax.axis_index("mp")

    def media_back(k, carry):
        item, first = lax.div(k, per_item), lax.rem(k, per_item) * step_rows
        first = pl.multiple_of(first, step_rows)
        frame = lax.div(mp_rank * slots + first, PATCHES)
        value = media[item, pl.ds(first, step_rows)].astype(f32) + time_rows[pl.ds(frame, 1)]
        back, factor, offset = norm_back(
            value, norms[0:1], acc[item, pl.ds(first, step_rows)]
        )
        acc[item, pl.ds(first, step_rows)] = back
        small[0:1] += factor
        small[1:2] += offset
        small[pl.ds(6 + frame, 1)] += jnp.sum(back, axis=0, keepdims=True)
        return carry

    def end():
        small[...] = jnp.zeros_like(small)
        half_way = items * per_item // 2
        lax.fori_loop(0, half_way, media_back, 0)
        for move in moves_1:
            reduce.advance(*move)
        lax.fori_loop(half_way, items * per_item, media_back, 0)
        out = pltpu.make_async_copy(acc.at[:, pl.ds(0, slots)], media_o, stage_sem.at[0])
        out.start()
        latent_swap.finish()
        for n in range(items):
            pulled = acc[n, slots:]
            for k in range(lat_vm.shape[0]):
                pulled = pulled + lat_vm[k, n]
            value, factor, offset = norm_back(latents[n], norms[2:3], pulled)
            latents_o[n] = after_back[n] + value
            small[2:3] += factor
            small[3:4] += offset
        small[4:6] = ffn_sums[...]
        totals[0].advance(0)
        totals[0].advance(1)
        reduce.advance(*moves_2[0])
        totals[0].advance(2)
        for move in moves_2[1:-1]:
            reduce.advance(*move)
        totals[0].advance(3)
        sums = jnp.zeros((1, 1), f32)
        for buffer in (up_vm, down_vm):
            for k in range(buffer.shape[0]):
                value = buffer[k].astype(f32)
                sums = sums + jnp.sum(value * value, keepdims=True)
        reduce.advance(*moves_2[-1])
        totals[0].advance(4)
        owned = reduce.scr[reduce.out_spot]
        for t in range(owned.shape[0]):
            for h in range(owned.shape[1]):
                value = owned[t, h]
                sums = sums + jnp.sum(value * value, keepdims=True)
        square[...] = jnp.broadcast_to(sums, square.shape)
        totals[1].advance(0)
        reduce.finish()
        for stage in range(1, 5):
            totals[1].advance(stage)
        out.wait()

    at(2, last, end)


def attend_back(
    place,
    source,
    latent_rows,
    query,
    chance,
    blend,
    back,
    mixed,
    low,
    rows_in,
    weights,
    owned_ffn,
    rows_end,
    weight_halves,
    heads,
    scale,
):
    items, keys, width = source.shape
    lat = latent_rows.shape[1]
    own = low.shape[1]
    blocks, block = weights.shape[0], weights.shape[3]
    rows = heads * lat
    half, f32 = jnp.bfloat16, jnp.float32
    s = place.size
    part = width // (s["z"] * s["x"] * weight_halves)
    inner = (s["z"], s["x"], weight_halves, part, block)
    grad = jax.ShapeDtypeStruct((s["y"], s["c"], 4) + inner, half)
    lat_shares = jax.ShapeDtypeStruct((blocks, items, own, width), f32)
    order = [3, 2, 1, 0]
    reduce = Reduce(place, grad, kept=6 if weight_halves == 2 else 2)
    reduce.chunks = [(t, h) for t in order for h in range(weight_halves)]
    latent_swap = Swap(place, "mp", True, lat_shares)
    small = jax.ShapeDtypeStruct((16, width), f32)
    square = jax.ShapeDtypeStruct((8, 128), f32)
    totals = [Total(place, small), Total(place, square)]
    slots = keys - own

    def weight(t, first):
        return pl.BlockSpec(
            (1, 1, width, block), lambda ph, j: (j * jnp.minimum(ph // first, 1), t, 0, 0)
        )

    def per(*shape):
        return pl.BlockSpec((1, items) + shape, lambda ph, j: (j,) + (0,) * (1 + len(shape)))

    def early(*shape):
        return pl.BlockSpec(
            (1, items) + shape,
            lambda ph, j: (j + (blocks - 1 - j) * jnp.minimum(ph, 1),) + (0,) * (1 + len(shape)),
        )

    def late(*shape):
        return pl.BlockSpec(
            (1, items) + shape,
            lambda ph, j: (j * jnp.minimum(ph, 1),) + (0,) * (1 + len(shape)),
        )

    whole = pl.BlockSpec(memory_space=pltpu.VMEM)
    hbm = pl.BlockSpec(memory_space=pl.ANY)
    scratch = [
        pltpu.VMEM((items, keys, width), f32),
        pltpu.VMEM(lat_shares.shape, f32),
        pltpu.VMEM(lat_shares.shape, f32),
        pltpu.VMEM((blocks, items, rows, keys), half),
        pltpu.VMEM(inner, half),
        pltpu.VMEM(inner, half),
        pltpu.VMEM(small.shape, f32),
        pltpu.VMEM(square.shape, f32),
        pltpu.SemaphoreType.DMA((2,)),
    ]
    for member in [reduce, latent_swap] + totals:
        scratch += member.scratch
    return pl.pallas_call(
        functools.partial(
            attend_back_kernel, place, heads, scale, reduce, latent_swap, totals
        ),
        grid=(3, blocks),
        in_specs=[
            whole,
            whole,
            late(lat, block),
            late(rows, keys),
            early(rows, width),
            per(lat, block),
            early(own, block),
            whole,
            per(2, rows),
            weight(0, 1),
            weight(1, 1),
            weight(2, 1),
        ]
        + [whole] * 8,
        out_specs=[hbm] * 3 + [whole] * 3,
        out_shape=[
            grad,
            jax.ShapeDtypeStruct((items, slots, width), f32),
            reduce.out,
            jax.ShapeDtypeStruct((items, own, width), f32),
            small,
            square,
        ],
        scratch_shapes=scratch,
        compiler_params=pltpu.CompilerParams(
            collective_id=6, has_side_effects=True, vmem_limit_bytes=64 * 1024 * 1024 - 65536
        ),
        name="attend_back",
    )(
        source,
        latent_rows,
        query,
        chance,
        blend,
        back,
        mixed,
        low,
        rows_in,
        weights,
        weights,
        weights,
        *owned_ffn,
        *rows_end,
    )


def reduce_plan(chunks, blocks, items):
    points = blocks * items
    if chunks == 8:
        eighths = {
            (1, 0): [(0, 1), (1, 0)],
            (1, 3): [(0, 2), (1, 1)],
            (1, 6): [(0, 3), (1, 2)],
            (1, 7): [(2, 0)],
            (2, 0): [(2, 1), (1, 3)],
            (2, 2): [(0, 4), (3, 0)],
            (2, 4): [(3, 1)],
            (2, 6): [(2, 2)],
        }
    else:
        eighths = {
            (1, 0): [(0, 1)],
            (1, 3): [(0, 2)],
            (1, 6): [(0, 3)],
            (1, 7): [(0, 4), (1, 0)],
            (2, 0): [(1, 1)],
        }
    plan = {
        (phase, (eighth + 1) * points // 8 - 1): moves for (phase, eighth), moves in eighths.items()
    }
    if chunks == 8:
        return plan, ((1, 4), (3, 2), (2, 3)), ((3, 3), (2, 4), (3, 4))
    return plan, ((1, 2),), ((1, 3), (1, 4))


def refresh_kernel(rates, *refs):
    f32 = jnp.float32
    count = len(rates)
    square, small = refs[:2]
    ins, outs = refs[2 : 2 + 4 * count], refs[2 + 4 * count :]
    total = square[0:1, 0:1] + jnp.sum(small[...] * small[...], keepdims=True)
    norm = jnp.sqrt(total)
    outs[0][...] = norm
    clip = 1.0 / jnp.maximum(norm, 1.0)
    spot = 1
    for n, rate in enumerate(rates):
        grad, master, momentum, average = ins[4 * n : 4 * n + 4]
        with_copy = n < 4
        into = outs[spot : spot + (5 if with_copy else 4)]
        spot += len(into)
        rows = grad.shape[0]
        step = math.gcd(rows, 32)

        def update(at):
            done = advance(
                grad[at].astype(f32), master[at], momentum[at], average[at], clip, rate
            )
            for ref, value in zip(into, done):
                ref[at] = value
            if with_copy:
                into[4][at] = done[1].astype(jnp.bfloat16)

        if step < 16:
            update(Ellipsis)
        else:

            def one(k, carry):
                update(pl.ds(pl.multiple_of(k * step, step), step))
                return carry

            lax.fori_loop(0, rows // step, one, 0)


def refresh(square, small, groups):
    f32 = jnp.float32
    whole = pl.BlockSpec(memory_space=pltpu.VMEM)
    shapes = [jax.ShapeDtypeStruct((1, 1), f32)]
    for n, (rate, grad, *_) in enumerate(groups):
        shapes += [jax.ShapeDtypeStruct(grad.shape, f32)] * 4
        if n < 4:
            shapes.append(jax.ShapeDtypeStruct(grad.shape, jnp.bfloat16))
    arrays = [array for _, *four in groups for array in four]
    return pl.pallas_call(
        functools.partial(refresh_kernel, [rate for rate, *_ in groups]),
        in_specs=[whole] * (2 + len(arrays)),
        out_specs=[whole] * len(shapes),
        out_shape=shapes,
        compiler_params=pltpu.CompilerParams(vmem_limit_bytes=60 * 1024 * 1024),
        name="refresh",
    )(square, small, *arrays)


def halves(rows):
    return 2 if rows % 32 == 0 else 1


def shards(
    latents,
    media,
    frames,
    cotangent,
    qkv_master,
    qkv_momentum,
    qkv_average,
    out_master,
    out_momentum,
    out_average,
    up_master,
    up_momentum,
    up_average,
    down_master,
    down_momentum,
    down_average,
    norm_params,
    norm_momentum,
    norm_average,
    time_table,
    time_momentum,
    time_average,
):
    f32 = jnp.float32
    half = jnp.bfloat16
    mp_rank = lax.axis_index("mp")
    mp_count = lax.axis_size("mp")
    dp_count = lax.axis_size("dp")
    place = Place(dp_count, mp_count)
    items, lat_own, width = latents.shape
    lat_total = lat_own * mp_count
    slots = media.shape[1]
    block = qkv_master.shape[2]
    rows_d = qkv_master.shape[1]
    heads = block // HEAD_DIM
    hidden_block = up_master.shape[1]
    units = hidden_block // dp_count
    own_rows = items * lat_own
    all_rows = dp_count * mp_count * own_rows
    scale_factor = HEAD_DIM ** (-0.5)
    dot = functools.partial(jnp.einsum, preferred_element_type=f32)

    def as_chunks(rows):
        t = halves(own_rows)
        return rows.reshape(t, 1, own_rows // t, width)

    weight_halves = halves(rows_d)
    own_weights = jnp.concatenate(
        [qkv_master.astype(half), out_master.astype(half).T[None]], axis=0
    ).reshape(4, weight_halves, rows_d // weight_halves, block)
    latent_norm = layer_norm(latents, norm_params[2], norm_params[3]).astype(half)

    def as_pieces(wide):
        return wide.reshape(rows_d, dp_count, units).transpose(1, 0, 2)

    def from_pieces(pieces):
        return pieces.transpose(1, 0, 2).reshape(rows_d, hidden_block)

    up_pieces = as_pieces(up_master.astype(half))
    down_pieces = as_pieces(down_master.T.astype(half))
    slot_ids = mp_rank * slots + jnp.arange(slots)
    frame_ids = slot_ids // PATCHES
    keep = jnp.concatenate(
        [frame_ids[None, :] < frames[:, None], jnp.ones((items, lat_own), jnp.bool_)], axis=1
    )
    (
        weights,
        back_rows,
        source,
        latent_rows,
        queries,
        chances,
        blends,
        mixed_blocks,
        stats,
    ) = front(
        place,
        own_weights,
        as_chunks(cotangent.astype(half)),
        latent_norm,
        media,
        keep.astype(f32)[:, None],
        time_table,
        norm_params,
        heads,
        scale_factor,
    )
    weights = weights.reshape(mp_count, 4, width, block)
    w_out = weights[:, 3]
    latent_rows = latent_rows.transpose(1, 0, 2, 3).reshape(items, lat_total, width)
    part_peaks, part_sums = stats[:, :, :, 0], stats[:, :, :, 1]
    grow = jnp.exp(part_peaks - jnp.max(part_peaks, axis=0))
    shares = grow / jnp.sum(part_sums * grow, axis=0)
    share = lax.dynamic_index_in_dim(shares, mp_rank, 0, keepdims=False)
    own_shares = lax.dynamic_slice_in_dim(
        shares.reshape(mp_count, mp_count, items, heads, lat_total), mp_rank * lat_own, lat_own, 4
    )
    own_shares = jnp.repeat(own_shares.transpose(0, 1, 2, 4, 3), HEAD_DIM, axis=-1)
    mixed_full = jnp.sum(mixed_blocks * own_shares, axis=0)
    mixed_j = mixed_full.astype(half)
    after_attn = latents + dot("jile,jde->ild", mixed_j, w_out)
    ffn_norm = layer_norm(after_attn, norm_params[4], norm_params[5]).astype(half)
    t = halves(own_rows)
    by_chunk = (t, own_rows // t, width)
    (
        _,
        ffn_out,
        up_owned,
        down_owned,
        mixed_back_rows,
        row_terms,
        after_back,
        attn_low,
        ffn_sums,
    ) = (feed if 2 * all_rows * width <= ROWS_IN_VMEM else feed_apart)(
        place,
        as_chunks(ffn_norm),
        up_pieces,
        down_pieces,
        back_rows,
        after_attn.reshape(by_chunk),
        cotangent.reshape(by_chunk),
        mixed_full.reshape(mp_count, own_rows, block),
        norm_params,
        weights,
    )
    latents_out = after_attn + ffn_out.reshape(latents.shape)
    after_back, attn_low = after_back.reshape(latents.shape), attn_low.reshape(latents.shape)
    row_terms = row_terms.reshape(mp_count, mp_count, items, lat_own, heads)
    row_terms = row_terms.transpose(1, 2, 4, 0, 3).reshape(mp_count, items, heads * lat_total)
    back_j = (
        mixed_back_rows.reshape(mp_count, mp_count, items, lat_own, block)
        .transpose(1, 2, 0, 3, 4)
        .reshape(mp_count, items, lat_total, block)
    )
    _, media_grad, owned, latents_grad, small, square = attend_back(
        place,
        source,
        latent_rows,
        queries,
        chances,
        blends,
        back_j,
        mixed_j,
        attn_low,
        jnp.stack([share, row_terms], axis=2),
        weights,
        [up_owned, down_owned],
        [media, time_table, norm_params, latents, after_back, ffn_sums],
        weight_halves,
        heads,
        scale_factor,
    )
    owned = owned.reshape(4, rows_d, block)
    qkv_shape = (3 * rows_d, block)
    groups = [
        (
            STEP_RATES[0],
            owned[:3].reshape(qkv_shape),
            qkv_master.reshape(qkv_shape),
            qkv_momentum.reshape(qkv_shape),
            qkv_average.reshape(qkv_shape),
        ),
        (STEP_RATES[1], owned[3], out_master.T, out_momentum.T, out_average.T),
        (STEP_RATES[2], from_pieces(up_owned), up_master, up_momentum, up_average),
        (
            STEP_RATES[3],
            from_pieces(down_owned),
            down_master.T,
            down_momentum.T,
            down_average.T,
        ),
        (STEP_RATES[4], small[:6], norm_params, norm_momentum, norm_average),
        (STEP_RATES[5], small[6:14], time_table, time_momentum, time_average),
    ]
    (
        grad_norm,
        qkv_grad,
        qkv_new,
        qkv_momentum_new,
        qkv_average_new,
        qkv_copy,
        out_grad,
        out_new,
        out_momentum_new,
        out_average_new,
        out_copy,
        up_grad,
        up_new,
        up_momentum_new,
        up_average_new,
        up_copy,
        down_grad,
        down_new,
        down_momentum_new,
        down_average_new,
        down_copy,
        norm_grad,
        norm_new,
        norm_momentum_new,
        norm_average_new,
        time_grad,
        time_new,
        time_momentum_new,
        time_average_new,
    ) = refresh(square, small, groups)
    grad_norm = grad_norm.reshape(())
    out_grad, out_new, out_momentum_new, out_average_new, out_copy = (
        value.T for value in (out_grad, out_new, out_momentum_new, out_average_new, out_copy)
    )
    down_grad, down_new, down_momentum_new, down_average_new, down_copy = (
        value.T for value in (down_grad, down_new, down_momentum_new, down_average_new, down_copy)
    )
    qkv_grad, qkv_new, qkv_momentum_new, qkv_average_new, qkv_copy = (
        value.reshape(qkv_master.shape)
        for value in (qkv_grad, qkv_new, qkv_momentum_new, qkv_average_new, qkv_copy)
    )
    return (
        latents_out,
        latents_grad,
        media_grad,
        grad_norm,
        qkv_grad,
        qkv_new,
        qkv_momentum_new,
        qkv_average_new,
        out_grad,
        out_new,
        out_momentum_new,
        out_average_new,
        up_grad,
        up_new,
        up_momentum_new,
        up_average_new,
        down_grad,
        down_new,
        down_momentum_new,
        down_average_new,
        norm_grad,
        norm_new,
        norm_momentum_new,
        norm_average_new,
        time_grad,
        time_new,
        time_momentum_new,
        time_average_new,
        qkv_copy,
        out_copy,
        up_copy,
        down_copy,
    )


def solution(mesh):
    placed = (
        P("dp", "mp", None),
        P("dp", "mp", None),
        P("dp"),
        P("dp", "mp", None),
        P(None, "dp", "mp"),
        P(None, "dp", "mp"),
        P(None, "dp", "mp"),
        P("mp", "dp"),
        P("mp", "dp"),
        P("mp", "dp"),
        P("dp", "mp"),
        P("dp", "mp"),
        P("dp", "mp"),
        P("mp", "dp"),
        P("mp", "dp"),
        P("mp", "dp"),
        P(),
        P(),
        P(),
        P(),
        P(),
        P(),
    )
    return jax.shard_map(
        shards,
        mesh=mesh,
        in_specs=placed,
        out_specs=(
            P("dp", "mp", None),
            P("dp", "mp", None),
            P("dp", "mp", None),
            P(),
            P(None, "dp", "mp"),
            P(None, "dp", "mp"),
            P(None, "dp", "mp"),
            P(None, "dp", "mp"),
            P("mp", "dp"),
            P("mp", "dp"),
            P("mp", "dp"),
            P("mp", "dp"),
            P("dp", "mp"),
            P("dp", "mp"),
            P("dp", "mp"),
            P("dp", "mp"),
            P("mp", "dp"),
            P("mp", "dp"),
            P("mp", "dp"),
            P("mp", "dp"),
            P(),
            P(),
            P(),
            P(),
            P(),
            P(),
            P(),
            P(),
            P(None, "dp", "mp"),
            P("mp", "dp"),
            P("dp", "mp"),
            P("mp", "dp"),
        ),
        check_vma=False,
    )
```

```python
import functools
import math

import jax
import jax.numpy as jnp
from jax import lax
from jax.experimental import pallas as pl
from jax.experimental.pallas import tpu as pltpu
from jax.sharding import PartitionSpec as P

HEAD_DIM = 96
FRAMES = 8
PATCHES = 256


EPS = 1e-05
MOMENT = 0.9
STEP_RATES = (30.0, 1200.0, 120.0, 40.0, 1000.0, 1200.0)
DECAY_AVG = 0.75
HIGH = lax.Precision.HIGHEST
NEGATIVE = -1e30
SWAP_AT = 5
ROWS_IN_VMEM = 5 * 1024 * 1024


def layer_norm(values, factor, offset):
    centered = values - jnp.mean(values, axis=-1, keepdims=True)
    variance = jnp.mean(centered * centered, axis=-1, keepdims=True)
    return centered * lax.rsqrt(variance + EPS) * factor + offset


def exact_gelu(values):
    return jax.nn.gelu(values, approximate=False)


def square_sum(arrays):
    running = jnp.zeros((), jnp.float32)
    for member in arrays:
        running = running + jnp.sum(member * member)
    return running


def advance(gradient, master, momentum, average, clip_factor, rate):
    clipped = gradient * clip_factor
    moment_new = MOMENT * momentum + clipped
    master_new = master - rate * (clipped + MOMENT * moment_new)
    average_new = DECAY_AVG * average + (1.0 - DECAY_AVG) * master_new
    return (clipped, master_new, moment_new, average_new)


class Place:
    def __init__(self, dp_count, mp_count):
        z_count = 4 if dp_count % 4 == 0 else 1
        c_count = 2 if mp_count % 2 == 0 else 1
        self.size = {
            "z": z_count,
            "x": dp_count // z_count,
            "y": mp_count // c_count,
            "c": c_count,
        }
        self.count = {"dp": dp_count, "mp": mp_count}

    def mine(self):
        dp, mp = lax.axis_index("dp"), lax.axis_index("mp")
        x_count, c_count = self.size["x"], self.size["c"]
        return {
            "z": lax.div(dp, x_count),
            "x": lax.rem(dp, x_count),
            "y": lax.div(mp, c_count),
            "c": lax.rem(mp, c_count),
        }

    def shifted(self, me, axis, step):
        return {**me, axis: lax.rem(me[axis] + step, self.size[axis])}

    def device(self, at):
        return {
            "dp": at["z"] * self.size["x"] + at["x"],
            "mp": at["y"] * self.size["c"] + at["c"],
        }


def region(ref, at, chunk, whole):
    def pick(axis):
        return slice(None) if axis in whole else at[axis]

    return ref.at[pick("y"), pick("c"), chunk[0], pick("z"), pick("x"), chunk[1]]


def remote(src, dst, send, recv, device):
    return pltpu.make_async_remote_copy(
        src_ref=src,
        dst_ref=dst,
        send_sem=send,
        recv_sem=recv,
        device_id=device,
        device_id_type=pl.DeviceIdType.MESH,
    )


def greet(devices):
    barrier = pltpu.get_barrier_semaphore()
    for device in devices:
        pl.semaphore_signal(
            barrier, inc=1, device_id=device, device_id_type=pl.DeviceIdType.MESH
        )
    pl.semaphore_wait(barrier, len(devices))


class Swap:
    def __init__(self, place, axis, spread, value, late=0):
        self.place, self.axis, self.spread, self.value = place, axis, spread, value
        self.late = late
        self.n = place.count[axis]
        shape = value.shape if spread else (self.n,) + value.shape
        self.out = jax.ShapeDtypeStruct(shape, value.dtype)
        self.scratch = [
            pltpu.SemaphoreType.DMA((self.n,)),
            pltpu.SemaphoreType.DMA((self.n,)),
        ]

    def peers(self):
        rank = lax.axis_index(self.axis)
        return [{self.axis: lax.rem(rank + k, self.n)} for k in range(1, self.n)]

    def begin(self, refs):
        self.refs = refs

    def steps(self):
        return self.late + 1

    def own(self):
        src, dst, send, _ = self.refs
        rank = lax.axis_index(self.axis)
        return pltpu.make_async_copy(
            src.at[rank] if self.spread else src, dst.at[rank], send.at[0]
        )

    def copies(self, receive):
        src, dst, send, recv = self.refs
        rank = lax.axis_index(self.axis)
        for k in range(1, self.n):
            there, here = lax.rem(rank + k, self.n), lax.rem(rank + self.n - k, self.n)
            yield remote(
                src.at[there] if self.spread else src,
                dst.at[here if receive else rank],
                send.at[k],
                recv.at[k],
                {self.axis: there},
            )

    def step(self, time):
        if time == self.late:
            self.own().start()
            for copy in self.copies(False):
                copy.start()

    def finish(self):
        self.own().wait()
        for copy in self.copies(False):
            copy.wait_send()
        for copy in self.copies(True):
            copy.wait_recv()


def pair_at(index, chunks):
    return [n for n in (2 * index, 2 * index + 1) if 0 <= n < len(chunks)]


GATHER_STAGES = (0, 2, 1, 3, 4)
REDUCE_STAGES = (4, 3, 2, 1, 0)
ORDERS = (("z", "x", "y", "c"), ("z", "y", "x", "c"))


class Gather:
    def __init__(self, place, value, late=0):
        self.place, self.value, self.late = place, value, late
        s = place.size
        t, h = value.shape[:2]
        self.chunks = [(a, b) for a in range(t) for b in range(h)]
        self.out = jax.ShapeDtypeStruct(
            (s["y"], s["c"], t, s["z"], s["x"], h) + value.shape[2:], value.dtype
        )
        self.most = max(s.values())
        sems = pltpu.SemaphoreType.DMA((len(self.chunks), 5, self.most))
        self.scratch = [sems, sems]

    def peers(self):
        me = self.place.mine()
        return [
            self.place.device(self.place.shifted(me, a, k))
            for a in "zxyc"
            for k in range(1, self.place.size[a])
        ]

    def copies(self, n, stage, receive):
        src, dst, send, recv = self.refs
        order = ORDERS[n % 2]
        axis, whole = order[stage], order[:stage]
        me = self.me
        for k in range(1, self.place.size[axis]):
            there = self.place.shifted(me, axis, k)
            here = self.place.shifted(me, axis, self.place.size[axis] - k)
            at = here if receive else me
            block = (
                src.at[self.chunks[n][0], self.chunks[n][1]]
                if stage == 0
                else region(dst, me, self.chunks[n], whole)
            )
            yield remote(
                block,
                region(dst, at, self.chunks[n], whole),
                send.at[n, stage, k],
                recv.at[n, stage, k],
                self.place.device(there),
            )

    def begin(self, refs):
        self.refs, self.me = refs, self.place.mine()

    def own(self, n):
        src, dst, send, _ = self.refs
        chunk = self.chunks[n]
        return pltpu.make_async_copy(
            src.at[chunk[0], chunk[1]], region(dst, self.me, chunk, ()), send.at[n, 4, 0]
        )

    def steps(self):
        return self.late + pl.cdiv(len(self.chunks), 2) + 4

    def step(self, time):
        for stage in GATHER_STAGES:
            for n in pair_at(time - self.late - stage, self.chunks):
                if stage == 0:
                    self.own(n).start()
                if stage == 1:
                    self.own(n).wait()
                if stage > 0:
                    for copy in self.copies(n, stage - 1, True):
                        copy.wait_recv()
                if stage < 4:
                    for copy in self.copies(n, stage, False):
                        copy.start()

    def finish(self):
        for n in range(len(self.chunks)):
            for stage in range(4):
                for copy in self.copies(n, stage, False):
                    copy.wait_send()


BACK_ORDERS = (("c", "y", "x", "z"), ("c", "x", "y", "z"))
LAYOUT = ("y", "z", "x")


class Reduce:
    def __init__(self, place, value, late=0, starts=None, kept=None):
        self.place, self.value = place, value
        s = place.size
        t, h = value.shape[2], value.shape[5]
        tail = value.shape[6:]
        self.chunks = [(a, b) for a in range(t) for b in range(h)]
        self.out = jax.ShapeDtypeStruct((t, h) + tail, jnp.float32)
        count = len(self.chunks)
        pairs = pl.cdiv(count, 2)
        self.starts = [late + k for k in range(pairs)] if starts is None else starts
        self.kept = count if kept is None else min(kept, count)
        sems = pltpu.SemaphoreType.DMA((count, 5, max(s.values())))
        full = tuple(s[a] for a in LAYOUT)
        held = pltpu.VMEM((self.kept,) + full + tail, value.dtype)
        self.scratch = [sems, sems, held, held]
        self.spots = {}
        for parity in range(min(2, count)):
            mine = (count + 1 - parity) // 2
            left = list(LAYOUT)
            for stage, axis in list(enumerate(BACK_ORDERS[parity]))[1:]:
                left.remove(axis)
                shape = (mine, max(s[axis] - 1, 1)) + tuple(s[a] for a in left) + tail
                self.spots[parity, stage] = len(self.scratch)
                self.scratch.append(pltpu.VMEM(shape, value.dtype))
        self.out_spot = len(self.scratch)
        self.scratch.append(pltpu.VMEM((t, h) + tail, jnp.float32))
        self.scratch.append(pltpu.SemaphoreType.DMA((1,)))
        self.scratch.append(pltpu.SemaphoreType.REGULAR)

    peers = Gather.peers

    def part(self, n, stage, at):
        order = BACK_ORDERS[n % 2]
        if stage == 0:
            t, h = self.chunks[n]
            return self.src.at[:, at, t, :, :, h]
        index = tuple(
            at if a == order[stage] else self.me[a] if a in order[:stage] else slice(None)
            for a in LAYOUT
        )
        return self.scr[2].at[(n % self.kept,) + index]

    def into(self, n, stage):
        if stage == 0:
            return self.scr[3].at[pl.ds(n % self.kept, 1)]
        return self.scr[self.spots[n % 2, stage]].at[n // 2]

    def copies(self, n, stage):
        axis = BACK_ORDERS[n % 2][stage]
        for k in range(1, self.place.size[axis]):
            there = self.place.shifted(self.me, axis, k)
            yield remote(
                self.part(n, stage, there[axis]),
                self.into(n, stage).at[k - 1],
                self.scr[0].at[n, stage, k],
                self.scr[1].at[n, stage, k],
                self.place.device(there),
            )

    def own(self, n):
        t, h = self.chunks[n]
        return pltpu.make_async_copy(
            self.src.at[:, self.me["c"], t, :, :, h],
            self.scr[2].at[n % self.kept],
            self.scr[0].at[n, 4, 0],
        )

    def begin(self, refs):
        self.src, self.dst, self.scr = refs[0], refs[1], refs[2:]
        self.me = self.place.mine()

    def steps(self):
        return self.starts[-1] + 5

    def add(self, n, stage):
        order = BACK_ORDERS[n % 2]
        axis = order[stage]
        count = self.place.size[axis] - 1
        into = self.into(n, stage)
        sizes = [self.place.size[a] for a in LAYOUT if a not in order[: stage + 1]]
        if stage == 0:
            base = target = self.scr[2].at[n % self.kept]
        else:
            base = target = self.part(n, stage, self.me[axis])
        if stage == 3:
            target = self.scr[self.out_spot].at[self.chunks[n][0], self.chunks[n][1]]

        def one(flat, carry):
            index = []
            rest = flat
            for size in reversed(sizes):
                index.insert(0, lax.rem(rest, size))
                rest = lax.div(rest, size)
            index = tuple(index) + (Ellipsis,)
            if count == 1 and target.dtype == base.dtype:
                target[index] = base[index] + into[(0,) + index]
                return carry
            value = base[index].astype(jnp.float32)
            for k in range(count):
                value = value + into[(k,) + index].astype(jnp.float32)
            target[index] = value.astype(target.dtype)
            return carry

        total = math.prod(sizes)
        if total == 1:
            one(jnp.int32(0), 0)
        else:
            lax.fori_loop(0, total, one, 0)

    def step(self, time):
        for stage in REDUCE_STAGES:
            for pair, start in enumerate(self.starts):
                if start + stage == time:
                    self.advance(pair, stage)

    def advance(self, pair, stage):
        sibling = self.place.device(self.place.shifted(self.me, "c", 1))
        reused = len(self.chunks) > self.kept and self.place.size["c"] > 1
        for n in pair_at(pair, self.chunks):
            if stage == 0:
                if n >= self.kept:
                    for old in range(4):
                        for copy in self.copies(n - self.kept, old):
                            copy.wait_send()
                    if reused:
                        pl.semaphore_wait(self.scr[-1], 1)
                self.own(n).start()
            if stage == 1:
                self.own(n).wait()
            if stage > 0:
                for copy in self.copies(n, stage - 1):
                    copy.wait_recv()
                self.add(n, stage - 1)
            if stage == 1 and reused and n + self.kept < len(self.chunks):
                pl.semaphore_signal(
                    self.scr[-1],
                    inc=1,
                    device_id=sibling,
                    device_id_type=pl.DeviceIdType.MESH,
                )
            if stage < 4:
                for copy in self.copies(n, stage):
                    copy.start()

    def finish(self):
        out = pltpu.make_async_copy(self.scr[self.out_spot], self.dst, self.scr[-2].at[0])
        out.start()
        for n in range(max(0, len(self.chunks) - self.kept), len(self.chunks)):
            for stage in range(4):
                for copy in self.copies(n, stage):
                    copy.wait_send()
        out.wait()


class Total:
    AXES = ("c", "y", "x", "z")

    def __init__(self, place, value):
        self.place, self.value = place, value
        self.out = jax.ShapeDtypeStruct(value.shape, value.dtype)
        sems = pltpu.SemaphoreType.DMA((4, max(place.size.values())))
        self.scratch = [sems, sems] + [
            pltpu.VMEM((place.size[a],) + value.shape, value.dtype) for a in self.AXES
        ]

    peers = Gather.peers

    def begin(self, refs):
        self.src, self.dst, self.send, self.recv = refs[:4]
        self.bufs = refs[4:]
        self.me = self.place.mine()

    def copies(self, stage, receive):
        axis = self.AXES[stage]
        size = self.place.size[axis]
        buf, me = self.bufs[stage], self.me
        for k in range(1, size):
            there = self.place.shifted(me, axis, k)
            here = self.place.shifted(me, axis, size - k)
            yield remote(
                buf.at[me[axis]],
                buf.at[here[axis] if receive else me[axis]],
                self.send.at[stage, k],
                self.recv.at[stage, k],
                self.place.device(there),
            )

    def advance(self, stage):
        if stage == 0:
            value = self.src[...]
        else:
            for copy in self.copies(stage - 1, True):
                copy.wait_recv()
            for copy in self.copies(stage - 1, False):
                copy.wait_send()
            value = self.bufs[stage - 1][0]
            for k in range(1, self.place.size[self.AXES[stage - 1]]):
                value = value + self.bufs[stage - 1][k]
        if stage == 4:
            self.dst[...] = value
            return
        self.bufs[stage][self.me[self.AXES[stage]]] = value
        for copy in self.copies(stage, False):
            copy.start()


def norm_back(value, factor, pulled):
    centered = value - jnp.mean(value, axis=-1, keepdims=True)
    variance = jnp.mean(centered * centered, axis=-1, keepdims=True)
    scale = lax.rsqrt(variance + EPS)
    unit = centered * scale
    inner = pulled * factor
    back = scale * (
        inner
        - jnp.mean(inner, axis=-1, keepdims=True)
        - unit * jnp.mean(inner * unit, axis=-1, keepdims=True)
    )
    return (
        back,
        jnp.sum(pulled * unit, axis=0, keepdims=True),
        jnp.sum(pulled, axis=0, keepdims=True),
    )


def communicate(label, number, parts):
    count = len(parts)

    def kernel(*refs):
        ins, outs, rest = refs[:count], refs[count : 2 * count], refs[2 * count :]
        devices, seen = [], set()
        for part in parts:
            kind = part.axis if isinstance(part, Swap) else "grid"
            if kind not in seen:
                seen.add(kind)
                devices += part.peers()
        greet(devices)
        spot = 0
        for part, src, dst in zip(parts, ins, outs):
            size = len(part.scratch)
            part.begin((src, dst) + tuple(rest[spot : spot + size]))
            spot += size
        staged = parts
        for time in range(max([part.steps() for part in staged], default=0)):
            for part in staged:
                part.step(time)
        for part in parts:
            part.finish()

    return pl.pallas_call(
        kernel,
        out_shape=[part.out for part in parts],
        in_specs=[pl.BlockSpec(memory_space=pl.ANY)] * count,
        out_specs=[pl.BlockSpec(memory_space=pl.ANY)] * count,
        scratch_shapes=[s for part in parts for s in part.scratch],
        compiler_params=pltpu.CompilerParams(
            collective_id=number, has_side_effects=True, vmem_limit_bytes=58 * 1024 * 1024
        ),
        name=label,
    )(*[part.value for part in parts])


def product(left, right, dims):
    return lax.dot_general(left, right, (dims, ((), ())), preferred_element_type=jnp.float32)


NN, NT, TN = ((1,), (0,)), ((1,), (1,)), ((0,), (0,))


def spread_heads(rows, heads):
    owner = lax.broadcasted_iota(jnp.int32, rows.shape, 1)
    kept = [
        jnp.where((owner >= h * HEAD_DIM) & (owner < (h + 1) * HEAD_DIM), rows, 0)
        for h in range(heads)
    ]
    return jnp.concatenate(kept, axis=0)


def fold_heads(wide, heads):
    rows = wide.shape[0] // heads
    owner = lax.broadcasted_iota(jnp.int32, (rows, wide.shape[1]), 1)
    out = wide[:rows]
    for h in range(1, heads):
        out = jnp.where(owner >= h * HEAD_DIM, wide[h * rows : (h + 1) * rows], out)
    return out


def as_row(column):
    wide = jnp.broadcast_to(column, (column.shape[0], 128))
    return jnp.transpose(wide)[:1]


def as_column(row):
    return jnp.transpose(jnp.broadcast_to(row, (128, row.shape[1])))[:, :1]


def front_kernel(place, heads, scale, halves_w, parts, *refs):
    half, f32 = jnp.bfloat16, jnp.float32
    qkv, out_t, cot_in, latents, ffn_in, media, keep, time_rows, norms = refs[:9]
    w_o, back_o, src_o, lat_o, q_o, p_o, blend_o, mixed_o, stat_o, ffn_o = refs[9:19]
    w_vm, lat_vm, src_vm, q_vm, p_vm, blend_vm, mixed_vm, stat_vm, sems = refs[19:28]
    own_w, cot, lat_in = refs[28:31]
    rest = list(refs[31:])
    gather_w, gather_c, lat_swap, mixed_swap, stat_swap, ffn_swap = parts
    ends = (
        (own_w, w_vm),
        (cot, back_o),
        (lat_in, lat_vm),
        (mixed_vm, mixed_o),
        (stat_vm, stat_o),
        (ffn_in, ffn_o),
    )
    for part, end in zip(parts, ends):
        size = len(part.scratch)
        part.begin(end + tuple(rest[:size]))
        rest = rest[size:]
    items, slots, width = media.shape
    lat_own = latents.shape[1]
    blocks, block = q_vm.shape[0], q_vm.shape[3]
    lat_total = blocks * lat_own
    c_count = place.size["c"]
    mp_rank = lax.axis_index("mp")
    greet(gather_w.peers() + lat_swap.peers() + ffn_swap.peers())
    clock = [0]

    def run_to(time):
        while clock[0] <= time:
            for part in (lat_swap, gather_w, gather_c, ffn_swap):
                part.step(clock[0])
            clock[0] += 1

    def arrived(t):
        return 4 + ((t + 1) * halves_w - 1) // 2

    def weight(j, t):
        return w_vm[lax.div(j, c_count), lax.rem(j, c_count), t].reshape(width, block)

    kept = []

    def keep_copy(src, dst):
        copy = pltpu.make_async_copy(src, dst, sems.at[len(kept)])
        copy.start()
        kept.append(copy)

    for n in range(items):
        lat_in[n] = layer_norm(latents[n], norms[2:3], norms[3:4]).astype(half)
    for t in range(4):
        value = qkv[t] if t < 3 else out_t[...]
        own_w[t] = value.astype(half).reshape(own_w.shape[1:])
    run_to(0)
    cot[...] = cot_in[...].astype(half)
    step_rows = math.gcd(64, slots)
    per_item = slots // step_rows

    def norm_media(k, carry):
        item, first = lax.div(k, per_item), lax.rem(k, per_item) * step_rows
        first = pl.multiple_of(first, step_rows)
        frame = lax.div(mp_rank * slots + first, PATCHES)
        value = media[item, pl.ds(first, step_rows)].astype(f32) + time_rows[pl.ds(frame, 1)]
        value = layer_norm(value, norms[0:1], norms[1:2])
        src_vm[item, pl.ds(first, step_rows)] = value.astype(half)
        return carry

    lax.fori_loop(0, items * per_item, norm_media, 0)
    src_vm[:, slots:] = lat_in[...]
    keep_copy(src_vm, src_o)
    run_to(3)
    lat_swap.finish()
    keep_copy(lat_vm, lat_o)
    run_to(arrived(0))

    def ask(j, carry):
        rows = jnp.concatenate(
            [lat_vm[:, n].reshape(lat_total, width) for n in range(items)], axis=0
        )
        query = product(rows, weight(j, 0), NN).astype(half)
        q_vm[j] = query.reshape(items, lat_total, block)
        return carry

    lax.fori_loop(0, blocks, ask, 0)
    keep_copy(q_vm, q_o)
    run_to(arrived(1))

    def score(k, carry):
        j, n = lax.div(k, items), lax.rem(k, items)
        source = src_vm[n]
        reach = product(spread_heads(q_vm[j, n], heads), weight(j, 1), NT).astype(half)
        value = product(reach, source, NT) * scale
        value = jnp.where(keep[n] > 0, value, NEGATIVE)
        peak = jnp.max(value, axis=1, keepdims=True)
        raised = jnp.exp(value - peak)
        total = jnp.sum(raised, axis=1, keepdims=True)
        low = raised.astype(half)
        p_vm[j, n] = low
        blend_vm[j, n] = product(low, source, NN).astype(half)
        stat_vm[j, n, 0:1] = as_row(peak)
        stat_vm[j, n, 1:2] = as_row(total)
        return carry

    lax.fori_loop(0, blocks * items // 2, score, 0)
    run_to(max(arrived(1) + 1, arrived(2)))
    lax.fori_loop(blocks * items // 2, blocks * items, score, 0)
    keep_copy(p_vm, p_o)
    keep_copy(blend_vm, blend_o)

    def mix(k, carry):
        j, n = lax.div(k, items), lax.rem(k, items)
        value = fold_heads(product(blend_vm[j, n], weight(j, 2), NN), heads)
        mixed_vm[:, j, n] = value.reshape(blocks, lat_own, block)
        return carry

    lax.fori_loop(0, blocks * items, mix, 0)
    mixed_swap.step(0)
    stat_swap.step(0)
    run_to(arrived(3))
    keep_copy(w_vm, w_o)
    run_to(gather_c.steps())
    for part in parts:
        if part is not lat_swap:
            part.finish()
    for copy in kept:
        copy.wait()


def front(
    place, qkv, out_t, cot, latents, ffn_pieces, media, keep, time_rows, norms, halves_w, heads, scale
):
    half, f32 = jnp.bfloat16, jnp.float32
    items, slots, width = media.shape
    lat_own = latents.shape[1]
    rows_d, block = out_t.shape
    blocks = place.count["mp"]
    own_weights = jax.ShapeDtypeStruct((4, halves_w, rows_d // halves_w, block), half)
    low_cot = jax.ShapeDtypeStruct(cot.shape, half)
    latent_norm = jax.ShapeDtypeStruct(latents.shape, half)
    lat, keys = blocks * lat_own, slots + lat_own
    rows = heads * lat
    late = 2 * halves_w
    mixed = jax.ShapeDtypeStruct((blocks, blocks, items, lat_own, block), f32)
    stats = jax.ShapeDtypeStruct((blocks, items, 2, rows), f32)
    parts = [
        Gather(place, own_weights),
        Gather(place, low_cot, late),
        Swap(place, "mp", False, latent_norm),
        Swap(place, "mp", True, mixed),
        Swap(place, "mp", False, stats),
        Swap(place, "dp", True, ffn_pieces, SWAP_AT),
    ]
    shapes = [
        parts[0].out,
        parts[2].out,
        jax.ShapeDtypeStruct((items, keys, width), half),
        jax.ShapeDtypeStruct((blocks, items, lat, block), half),
        jax.ShapeDtypeStruct((blocks, items, rows, keys), half),
        jax.ShapeDtypeStruct((blocks, items, rows, width), half),
        mixed,
        stats,
    ]
    scratch = [pltpu.VMEM(shape.shape, shape.dtype) for shape in shapes]
    scratch.append(pltpu.SemaphoreType.DMA((8,)))
    scratch += [pltpu.VMEM(v.shape, half) for v in (own_weights, low_cot, latent_norm)]
    for part in parts:
        scratch += part.scratch
    whole = pl.BlockSpec(memory_space=pltpu.VMEM)
    hbm = pl.BlockSpec(memory_space=pl.ANY)
    return pl.pallas_call(
        functools.partial(front_kernel, place, heads, scale, halves_w, parts),
        in_specs=[whole] * 4 + [hbm] + [whole] * 4,
        out_specs=[hbm] * 10,
        out_shape=[
            parts[0].out,
            parts[1].out,
            shapes[2],
            parts[2].out,
            shapes[3],
            shapes[4],
            shapes[5],
            parts[3].out,
            parts[4].out,
            parts[5].out,
        ],
        scratch_shapes=scratch,
        compiler_params=pltpu.CompilerParams(
            collective_id=1, has_side_effects=True, vmem_limit_bytes=64 * 1024 * 1024 - 65536
        ),
        name="front",
    )(qkv, out_t, cot, latents, ffn_pieces, media, keep, time_rows, norms)


def feed_kernel(place, parts, *refs):
    half, f32 = jnp.bfloat16, jnp.float32
    own_rows, pieces, back_rows, after_attn, cot, mixed, norms, weights = refs[:8]
    (norm_o, ffn_o, back_o, term_o, give_o, after_o, low_o, sums_o) = refs[8:16]
    (rows_vm, up_vm, down_vm, share_a, share_b, w_out) = refs[16:22]
    (hid_vm, pre_vm, mixed_vm, term_vm, sem) = refs[22:27]
    rest = list(refs[27:])
    gather, first, second, back_swap, term_swap = parts
    ends = (
        (own_rows, rows_vm),
        (share_a, norm_o),
        (share_b, ffn_o),
        (mixed_vm, back_o),
        (term_vm, term_o),
    )
    for part, end in zip(parts, ends):
        size = len(part.scratch)
        part.begin(end + tuple(rest[:size]))
        rest = rest[size:]
    c_count, blocks = place.size["c"], place.count["mp"]
    width, units = norms.shape[1], hid_vm.shape[2]
    greet(gather.peers() + back_swap.peers())
    out_weight = pltpu.make_async_copy(weights.at[:, 3], w_out, sem.at[0])
    gather.step(0)
    out_weight.start()
    up_vm[...] = pieces[:, :, :units].reshape(width, units)
    down_vm[...] = pieces[:, :, units:].reshape(width, units)
    for time in range(1, gather.steps()):
        gather.step(time)

    def inner(m, carry):
        y, c = lax.div(m, c_count), lax.rem(m, c_count)
        w_up, w_down = up_vm[...], down_vm[...]
        rows = rows_vm[y, c].reshape(-1, width)
        pre = product(rows, w_up, NN)
        pulled = product(back_rows[y, c].reshape(-1, width), w_down, NN)
        chance = 0.5 * (1.0 + lax.erf(pre * math.sqrt(0.5)))
        slope = chance + pre * jnp.exp(-0.5 * pre * pre) * math.sqrt(0.5 / math.pi)
        hid_vm[m] = (pre * chance).astype(half)
        pre_back = (pulled * slope).astype(half)
        pre_vm[m] = pre_back
        share = product(pre_back, w_up, NT).astype(half)
        share_a[y, c] = share.reshape(share_a.shape[2:])
        return carry

    lax.fori_loop(0, blocks, inner, 0)
    first.step(0)

    def outer(m, carry):
        y, c = lax.div(m, c_count), lax.rem(m, c_count)
        share = product(hid_vm[m], down_vm[...], NT).astype(half)
        share_b[y, c] = share.reshape(share_b.shape[2:])
        return carry

    lax.fori_loop(0, blocks, outer, 0)
    first.step(1)
    second.step(0)
    give = product(rows_vm[...].reshape(-1, width), pre_vm[...].reshape(-1, units), TN)
    half_shape = give_o.shape[:2] + (units,)
    give_o[:, :, :units] = give.astype(half).reshape(half_shape)
    give = product(back_rows[...].reshape(-1, width), hid_vm[...].reshape(-1, units), TN)
    give_o[:, :, units:] = give.astype(half).reshape(half_shape)
    first.step(2)
    second.step(1)
    first.step(3)
    second.step(2)
    first.step(4)
    pulled = first.scr[first.out_spot]
    factors = jnp.zeros((1, width), f32)
    offsets = jnp.zeros((1, width), f32)
    for t in range(after_attn.shape[0]):
        value, factor, offset = norm_back(after_attn[t], norms[4:5], pulled[t, 0])
        value = cot[t] + value
        after_o[t] = value
        low_o[t] = value.astype(half)
        factors += factor
        offsets += offset
    sums_o[0:1] = factors
    sums_o[1:2] = offsets
    out_weight.wait()
    low = low_o[...].reshape(-1, width)
    heads = term_vm.shape[0] // blocks
    for j in range(blocks):
        back = product(low, w_out[j].reshape(width, -1), NN).astype(half)
        mixed_vm[j] = back
        both = mixed[j] * back.astype(f32)
        owner = lax.broadcasted_iota(jnp.int32, both.shape, 1)
        for h in range(heads):
            mine = (owner >= h * HEAD_DIM) & (owner < (h + 1) * HEAD_DIM)
            term = jnp.sum(jnp.where(mine, both, 0.0), axis=1, keepdims=True)
            term_vm[j * heads + h : j * heads + h + 1] = as_row(term)
    back_swap.step(0)
    term_swap.step(0)
    second.step(3)
    second.step(4)
    for part in parts:
        part.finish()


def feed(place, own_rows, pieces, back_rows, after_attn, cot, mixed, norms, weights):
    half, f32 = jnp.bfloat16, jnp.float32
    gather = Gather(place, own_rows)
    rows = gather.out
    width = norms.shape[1]
    blocks, flat, block = mixed.shape
    heads = block // HEAD_DIM
    units = pieces.shape[2] // 2
    per = math.prod(rows.shape[2:7])
    mixed_back = jax.ShapeDtypeStruct(mixed.shape, half)
    terms = jax.ShapeDtypeStruct((blocks * heads, flat), f32)
    parts = [
        gather,
        Reduce(place, rows),
        Reduce(place, rows),
        Swap(place, "mp", False, mixed_back),
        Swap(place, "mp", False, terms),
    ]
    scratch = [
        pltpu.VMEM(rows.shape, half),
        pltpu.VMEM((width, units), half),
        pltpu.VMEM((width, units), half),
        pltpu.VMEM(rows.shape, half),
        pltpu.VMEM(rows.shape, half),
        pltpu.VMEM(weights.shape[:1] + weights.shape[2:], half),
        pltpu.VMEM((blocks, per, units), half),
        pltpu.VMEM((blocks, per, units), half),
        pltpu.VMEM(mixed.shape, half),
        pltpu.VMEM(terms.shape, f32),
        pltpu.SemaphoreType.DMA((1,)),
    ]
    for part in parts:
        scratch += part.scratch
    whole = pl.BlockSpec(memory_space=pltpu.VMEM)
    hbm = pl.BlockSpec(memory_space=pl.ANY)
    return pl.pallas_call(
        functools.partial(feed_kernel, place, parts),
        in_specs=[hbm] + [whole] * 6 + [hbm],
        out_specs=[hbm] * 4 + [whole] * 4,
        out_shape=[part.out for part in parts[1:]]
        + [
            jax.ShapeDtypeStruct(pieces.shape, half),
            jax.ShapeDtypeStruct(after_attn.shape, f32),
            jax.ShapeDtypeStruct(after_attn.shape, half),
            jax.ShapeDtypeStruct((2, width), f32),
        ],
        scratch_shapes=scratch,
        compiler_params=pltpu.CompilerParams(
            collective_id=3, has_side_effects=True, vmem_limit_bytes=60 * 1024 * 1024
        ),
        name="feed",
    )(own_rows, pieces, back_rows, after_attn, cot, mixed, norms, weights)


def feed_apart(place, own_rows, pieces, back_rows, after_attn, cot, mixed, norms, weights):
    half, f32 = jnp.bfloat16, jnp.float32
    width, units = norms.shape[1], pieces.shape[2] // 2
    dot = functools.partial(jnp.einsum, preferred_element_type=f32)
    (ffn_rows,) = communicate("rows", 3, [Gather(place, own_rows)])
    shape, half_shape = ffn_rows.shape, pieces.shape[:2] + (units,)
    w_up, w_down = (
        part.reshape(width, units) for part in (pieces[:, :, :units], pieces[:, :, units:])
    )
    ffn_rows, back_rows = ffn_rows.reshape(-1, width), back_rows.reshape(-1, width)
    pre_act = dot("rd,df->rf", ffn_rows, w_up)
    hidden = exact_gelu(pre_act).astype(half)
    hidden_back = dot("rd,df->rf", back_rows, w_down)
    pre_back = jax.vjp(exact_gelu, pre_act)[1](hidden_back)[0].astype(half)
    norm_part = dot("rf,df->rd", pre_back, w_up).astype(half)
    ffn_part = dot("rf,df->rd", hidden, w_down).astype(half)
    down_part = dot("rd,rf->df", back_rows, hidden).astype(half)
    up_part = dot("rd,rf->df", ffn_rows, pre_back).astype(half)
    norm_pulled, ffn_out = communicate(
        "ffn",
        4,
        [Reduce(place, norm_part.reshape(shape)), Reduce(place, ffn_part.reshape(shape))],
    )
    pull = jax.vjp(layer_norm, after_attn, norms[4], norms[5])[1]
    through, factor, offset = pull(norm_pulled.reshape(after_attn.shape))
    after_back = cot + through
    low = after_back.astype(half)
    mixed_back = dot("ld,jde->jle", low.reshape(-1, width), weights[:, 3]).astype(half)
    terms = jnp.sum(
        (mixed * mixed_back.astype(f32)).reshape(*mixed.shape[:2], -1, HEAD_DIM), axis=-1
    )
    terms = terms.transpose(0, 2, 1).reshape(-1, mixed.shape[1])
    mixed_rows, terms = communicate(
        "back", 5, [Swap(place, "mp", False, mixed_back), Swap(place, "mp", False, terms)]
    )
    sums = jnp.stack([factor, offset])
    return (
        norm_pulled,
        ffn_out,
        mixed_rows,
        terms,
        jnp.concatenate([up_part.reshape(half_shape), down_part.reshape(half_shape)], axis=2),
        after_back,
        low,
        sums,
    )


def attend_back_kernel(place, heads, scale, reduce, swap, latent_swap, totals, *refs):
    half, f32 = jnp.bfloat16, jnp.float32
    (src, lat, q, p, blend, back, mix, low, row, wq, wk, wv, give) = refs[:13]
    (media, time_rows, norms, latents, after_back, ffn_sums) = refs[13:19]
    (grad_o, media_o, owned_o, ffn_o, latents_o, small_o, square_o) = refs[19:26]
    (acc, lat_acc, lat_vm, kept, stage_a, stage_b, small, square, ffn_vm, joined, stage_sem) = refs[
        26:37
    ]
    rest = list(refs[37:])
    phase, block = pl.program_id(0), pl.program_id(1)
    blocks = pl.num_programs(1)
    items = src.shape[0]
    lat_total = lat.shape[1]
    width = src.shape[2]
    for part, give, out in (
        (reduce, grad_o, owned_o),
        (swap, give, ffn_vm),
        (latent_swap, lat_acc, lat_vm),
        (totals[0], small, small_o),
        (totals[1], square, square_o),
    ):
        size = len(part.scratch)
        part.begin((give, out) + tuple(rest[:size]))
        rest = rest[size:]

    def at(number, index, action):
        pl.when((phase == number) & (block == index))(action)

    last = place.count["mp"] - 1
    plan, moves_1, moves_2 = reduce_plan(len(reduce.chunks), place.count["mp"], items)
    c_count = place.size["c"]
    y_of, c_of = lax.div(block, c_count), lax.rem(block, c_count)

    def staged(t, buffer, number):
        return pltpu.make_async_copy(buffer, grad_o.at[y_of, c_of, t], stage_sem.at[number])

    def hand_over(first, first_value, second, second_value):
        @pl.when(block > 0)
        def _():
            staged(first, stage_a, 0).wait()
            staged(second, stage_b, 1).wait()

        stage_a[...] = first_value.astype(half).reshape(stage_a.shape)
        stage_b[...] = second_value.astype(half).reshape(stage_b.shape)
        staged(first, stage_a, 0).start()
        staged(second, stage_b, 1).start()

        @pl.when(block == last)
        def _():
            staged(first, stage_a, 0).wait()
            staged(second, stage_b, 1).wait()

    def column(item, which):
        return as_column(row[0, item, which : which + 1])

    def start():
        greet(swap.peers() + latent_swap.peers() + reduce.peers())
        swap.step(0)

    at(0, 0, start)

    @pl.when(phase == 0)
    def _():
        back_s = jnp.concatenate(
            [
                (spread_heads(back[0, n], heads) * column(n, 0)).astype(half)
                for n in range(items)
            ],
            axis=0,
        )
        value_grad = product(blend[0].reshape(back_s.shape[0], width), back_s, TN)
        out_grad = product(
            low[...].reshape(-1, width), mix[0].reshape(-1, mix.shape[3]), TN
        )
        hand_over(3, out_grad, 2, value_grad)

    def events(number, half_step):
        for (where, point), moves in plan.items():
            if where == number and point % items == half_step:

                def carry_out(moves=moves):
                    for move in moves:
                        reduce.advance(*move)

                at(where, point // items, carry_out)

    at(1, 0, lambda: reduce.advance(0, 0))

    @pl.when(phase == 1)
    def _():
        turns = []
        queries = jnp.concatenate([spread_heads(q[0, n], heads) for n in range(items)], axis=0)
        back_s = jnp.concatenate([spread_heads(back[0, n], heads) for n in range(items)], axis=0)
        pulls = product(back_s, wv[0, 0], NT).astype(half)
        rows = pulls.shape[0] // items
        for n in range(items):
            prob_back = product(pulls[n * rows : (n + 1) * rows], src[n], NT)
            score_back = (
                p[0, n].astype(jnp.float32) * (column(n, 0) * scale) * (prob_back - column(n, 1))
            ).astype(half)
            kept[block, n] = score_back
            turns.append(product(score_back, src[n], NN).astype(half))
            if n + 1 < items:
                events(1, n)
        turns = jnp.concatenate(turns, axis=0)
        key_turns = product(turns, wk[0, 0], NN)
        query_backs = jnp.concatenate(
            [fold_heads(key_turns[n * rows : (n + 1) * rows], heads) for n in range(items)], axis=0
        ).astype(half)
        latent_back = product(query_backs, wq[0, 0], NT)
        latent_back = latent_back.reshape(items, lat_acc.shape[0], -1, width)

        @pl.when(block == 0)
        def _():
            for n in range(items):
                lat_acc[:, n] = latent_back[n]

        @pl.when(block > 0)
        def _():
            for n in range(items):
                lat_acc[:, n] += latent_back[n]

        key_grad = product(turns, queries, TN)
        query_grad = product(lat[...].reshape(items * lat_total, width), query_backs, TN)
        hand_over(1, key_grad, 0, query_grad)

    events(1, items - 1)
    at(1, last, lambda: latent_swap.step(0))

    @pl.when(phase == 2)
    def _():
        queries = jnp.concatenate([spread_heads(q[0, n], heads) for n in range(items)], axis=0)
        back_s = jnp.concatenate([spread_heads(back[0, n], heads) for n in range(items)], axis=0)
        pulls = product(back_s, wv[0, 0], NT)
        reach = product(queries, wk[0, 0], NT).astype(half)
        rows = pulls.shape[0] // items
        for n in range(items):
            mine = slice(n * rows, (n + 1) * rows)
            value = product(
                jnp.concatenate([kept[block, n], p[0, n]], axis=0),
                jnp.concatenate([reach[mine], (pulls[mine] * column(n, 0)).astype(half)], axis=0),
                TN,
            )

            @pl.when(block == 0)
            def _():
                acc[n] = value

            @pl.when(block > 0)
            def _():
                acc[n] += value

            if n + 1 < items:
                events(2, n)

    events(2, items - 1)

    slots = media.shape[1]
    step_rows = math.gcd(64, slots)
    per_item = slots // step_rows
    mp_rank = lax.axis_index("mp")

    def media_back(k, carry):
        item, first = lax.div(k, per_item), lax.rem(k, per_item) * step_rows
        first = pl.multiple_of(first, step_rows)
        frame = lax.div(mp_rank * slots + first, PATCHES)
        value = media[item, pl.ds(first, step_rows)].astype(f32) + time_rows[pl.ds(frame, 1)]
        back, factor, offset = norm_back(
            value, norms[0:1], acc[item, pl.ds(first, step_rows)]
        )
        acc[item, pl.ds(first, step_rows)] = back
        small[0:1] += factor
        small[1:2] += offset
        small[pl.ds(6 + frame, 1)] += jnp.sum(back, axis=0, keepdims=True)
        return carry

    def end():
        small[...] = jnp.zeros_like(small)
        half_way = items * per_item // 2
        lax.fori_loop(0, half_way, media_back, 0)
        for move in moves_1:
            reduce.advance(*move)
        lax.fori_loop(half_way, items * per_item, media_back, 0)
        out = pltpu.make_async_copy(acc.at[:, pl.ds(0, slots)], media_o, stage_sem.at[0])
        out.start()
        latent_swap.finish()
        for n in range(items):
            pulled = acc[n, slots:]
            for k in range(lat_vm.shape[0]):
                pulled = pulled + lat_vm[k, n]
            value, factor, offset = norm_back(latents[n], norms[2:3], pulled)
            latents_o[n] = after_back[n] + value
            small[2:3] += factor
            small[3:4] += offset
        small[4:6] = ffn_sums[...]
        totals[0].advance(0)
        totals[0].advance(1)
        reduce.advance(*moves_2[0])
        totals[0].advance(2)
        for move in moves_2[1:-1]:
            reduce.advance(*move)
        totals[0].advance(3)
        swap.finish()
        units = ffn_vm.shape[2] // 2
        sums = jnp.zeros((1, 1), f32)
        for k in range(ffn_vm.shape[0]):
            piece = ffn_vm[k]
            joined[0, :, k * units : (k + 1) * units] = piece[:, :units]
            joined[1, :, k * units : (k + 1) * units] = piece[:, units:]
            value = piece.astype(f32)
            sums = sums + jnp.sum(value * value, keepdims=True)
        ffn_out = pltpu.make_async_copy(joined, ffn_o, stage_sem.at[1])
        ffn_out.start()
        reduce.advance(*moves_2[-1])
        totals[0].advance(4)
        owned = reduce.scr[reduce.out_spot]
        for t in range(owned.shape[0]):
            for h in range(owned.shape[1]):
                value = owned[t, h]
                sums = sums + jnp.sum(value * value, keepdims=True)
        square[...] = jnp.broadcast_to(sums, square.shape)
        totals[1].advance(0)
        reduce.finish()
        for stage in range(1, 5):
            totals[1].advance(stage)
        ffn_out.wait()
        out.wait()

    at(2, last, end)


def attend_back(
    place,
    source,
    latent_rows,
    query,
    chance,
    blend,
    back,
    mixed,
    low,
    rows_in,
    weights,
    give,
    rows_end,
    weight_halves,
    heads,
    scale,
):
    items, keys, width = source.shape
    lat = latent_rows.shape[1]
    own = low.shape[1]
    blocks, block = weights.shape[0], weights.shape[3]
    rows = heads * lat
    half, f32 = jnp.bfloat16, jnp.float32
    s = place.size
    part = width // (s["z"] * s["x"] * weight_halves)
    inner = (s["z"], s["x"], weight_halves, part, block)
    grad = jax.ShapeDtypeStruct((s["y"], s["c"], 4) + inner, half)
    lat_shares = jax.ShapeDtypeStruct((blocks, items, own, width), f32)
    order = [3, 2, 1, 0]
    reduce = Reduce(place, grad, kept=6 if weight_halves == 2 else 2)
    reduce.chunks = [(t, h) for t in order for h in range(weight_halves)]
    latent_swap = Swap(place, "mp", True, lat_shares)
    swap = Swap(place, "dp", True, give)
    joined = jax.ShapeDtypeStruct((2, give.shape[1], give.shape[0] * give.shape[2] // 2), half)
    small = jax.ShapeDtypeStruct((16, width), f32)
    square = jax.ShapeDtypeStruct((8, 128), f32)
    totals = [Total(place, small), Total(place, square)]
    slots = keys - own

    def weight(t, first):
        return pl.BlockSpec(
            (1, 1, width, block), lambda ph, j: (j * jnp.minimum(ph // first, 1), t, 0, 0)
        )

    def per(*shape):
        return pl.BlockSpec((1, items) + shape, lambda ph, j: (j,) + (0,) * (1 + len(shape)))

    def early(*shape):
        return pl.BlockSpec(
            (1, items) + shape,
            lambda ph, j: (j + (blocks - 1 - j) * jnp.minimum(ph, 1),) + (0,) * (1 + len(shape)),
        )

    def late(*shape):
        return pl.BlockSpec(
            (1, items) + shape,
            lambda ph, j: (j * jnp.minimum(ph, 1),) + (0,) * (1 + len(shape)),
        )

    whole = pl.BlockSpec(memory_space=pltpu.VMEM)
    hbm = pl.BlockSpec(memory_space=pl.ANY)
    scratch = [
        pltpu.VMEM((items, keys, width), f32),
        pltpu.VMEM(lat_shares.shape, f32),
        pltpu.VMEM(lat_shares.shape, f32),
        pltpu.VMEM((blocks, items, rows, keys), half),
        pltpu.VMEM(inner, half),
        pltpu.VMEM(inner, half),
        pltpu.VMEM(small.shape, f32),
        pltpu.VMEM(square.shape, f32),
        pltpu.VMEM(give.shape, half),
        pltpu.VMEM(joined.shape, half),
        pltpu.SemaphoreType.DMA((2,)),
    ]
    for member in [reduce, swap, latent_swap] + totals:
        scratch += member.scratch
    return pl.pallas_call(
        functools.partial(
            attend_back_kernel, place, heads, scale, reduce, swap, latent_swap, totals
        ),
        grid=(3, blocks),
        in_specs=[
            whole,
            whole,
            late(lat, block),
            late(rows, keys),
            early(rows, width),
            per(lat, block),
            early(own, block),
            whole,
            per(2, rows),
            weight(0, 1),
            weight(1, 1),
            weight(2, 1),
            hbm,
        ]
        + [whole] * 6,
        out_specs=[hbm] * 4 + [whole] * 3,
        out_shape=[
            grad,
            jax.ShapeDtypeStruct((items, slots, width), f32),
            reduce.out,
            joined,
            jax.ShapeDtypeStruct((items, own, width), f32),
            small,
            square,
        ],
        scratch_shapes=scratch,
        compiler_params=pltpu.CompilerParams(
            collective_id=6, has_side_effects=True, vmem_limit_bytes=64 * 1024 * 1024 - 65536
        ),
        name="attend_back",
    )(
        source,
        latent_rows,
        query,
        chance,
        blend,
        back,
        mixed,
        low,
        rows_in,
        weights,
        weights,
        weights,
        give,
        *rows_end,
    )


def reduce_plan(chunks, blocks, items):
    points = blocks * items
    if chunks == 8:
        eighths = {
            (1, 1): [(0, 1), (1, 0)],
            (1, 4): [(0, 2), (1, 1)],
            (1, 7): [(2, 0), (0, 3), (1, 2)],
            (2, 0): [(2, 1)],
            (2, 3): [(0, 4), (3, 0), (1, 3)],
            (2, 4): [(3, 1)],
            (2, 6): [(2, 2)],
        }
    else:
        eighths = {
            (1, 0): [(0, 1)],
            (1, 3): [(0, 2)],
            (1, 6): [(0, 3)],
            (1, 7): [(0, 4), (1, 0)],
            (2, 0): [(1, 1)],
        }
    plan = {
        (phase, (eighth + 1) * points // 8 - 1): moves for (phase, eighth), moves in eighths.items()
    }
    if chunks == 8:
        return plan, ((1, 4), (3, 2), (2, 3)), ((3, 3), (2, 4), (3, 4))
    return plan, ((1, 2),), ((1, 3), (1, 4))


def refresh_kernel(*refs):
    f32 = jnp.float32
    square, small, owned, ffn, media_in = refs[:5]
    groups = [refs[5 + 3 * n : 8 + 3 * n] for n in range(6)]
    norm_o, media_o = refs[23:25]
    outs = [refs[25 + 5 * n : 30 + 5 * n] for n in range(4)]
    outs += [refs[45 + 4 * n : 49 + 4 * n] for n in range(2)]
    media_come = pltpu.make_async_copy(media_in, refs[53], refs[54].at[0])
    media_come.start()
    total = square[0:1, 0:1] + jnp.sum(small[...] * small[...], keepdims=True)
    norm = jnp.sqrt(total)
    norm_o[...] = norm
    clip = 1.0 / jnp.maximum(norm, 1.0)

    def update(number, at, gradient):
        master, momentum, average = groups[number]
        done = advance(
            gradient.astype(f32),
            master[at],
            momentum[at],
            average[at],
            clip,
            STEP_RATES[number],
        )
        for ref, value in zip(outs[number], done):
            ref[at] = value
        if number < 4:
            outs[number][4][at] = done[1].astype(jnp.bfloat16)

    parts, rows = owned.shape[1:3]
    for h in range(parts):
        for t in range(3):
            update(0, (t, pl.ds(h * rows, rows)), owned[t, h])
        update(1, pl.ds(h * rows, rows), owned[3, h])
    media_come.wait()
    media_go = pltpu.make_async_copy(refs[53], media_o, refs[54].at[1])
    media_go.start()
    step = math.gcd(ffn.shape[1], 16)

    def one(k, carry):
        at = pl.ds(pl.multiple_of(k * step, step), step)
        for n in range(2):
            update(2 + n, at, ffn[n, at])
        return carry

    lax.fori_loop(0, ffn.shape[1] // step, one, 0)
    update(4, Ellipsis, small[0:6])
    update(5, Ellipsis, small[6 : 6 + FRAMES])
    media_go.wait()


def refresh(square, small, owned, ffn, media_grad, groups):
    f32 = jnp.float32
    whole = pl.BlockSpec(memory_space=pltpu.VMEM)
    hbm = pl.BlockSpec(memory_space=pl.ANY)
    shapes = [
        jax.ShapeDtypeStruct((1, 1), f32),
        jax.ShapeDtypeStruct(media_grad.shape, f32),
    ]
    for n, group in enumerate(groups):
        shapes += [jax.ShapeDtypeStruct(group[0].shape, f32)] * 4
        if n < 4:
            shapes.append(jax.ShapeDtypeStruct(group[0].shape, jnp.bfloat16))
    arrays = [array for group in groups for array in group]
    return pl.pallas_call(
        refresh_kernel,
        in_specs=[whole] * 4 + [hbm] + [whole] * len(arrays),
        out_specs=[whole, hbm] + [whole] * (len(shapes) - 2),
        out_shape=shapes,
        scratch_shapes=[
            pltpu.VMEM(media_grad.shape, f32),
            pltpu.SemaphoreType.DMA((2,)),
        ],
        compiler_params=pltpu.CompilerParams(vmem_limit_bytes=60 * 1024 * 1024),
        name="refresh",
    )(square, small, owned, ffn, media_grad, *arrays)


def halves(rows):
    return 2 if rows % 32 == 0 else 1


def shards(
    latents,
    media,
    frames,
    cotangent,
    qkv_master,
    qkv_momentum,
    qkv_average,
    out_master,
    out_momentum,
    out_average,
    up_master,
    up_momentum,
    up_average,
    down_master,
    down_momentum,
    down_average,
    norm_params,
    norm_momentum,
    norm_average,
    time_table,
    time_momentum,
    time_average,
):
    f32 = jnp.float32
    half = jnp.bfloat16
    mp_rank = lax.axis_index("mp")
    mp_count = lax.axis_size("mp")
    dp_count = lax.axis_size("dp")
    place = Place(dp_count, mp_count)
    items, lat_own, width = latents.shape
    lat_total = lat_own * mp_count
    slots = media.shape[1]
    block = qkv_master.shape[2]
    rows_d = qkv_master.shape[1]
    heads = block // HEAD_DIM
    hidden_block = up_master.shape[1]
    units = hidden_block // dp_count
    own_rows = items * lat_own
    all_rows = dp_count * mp_count * own_rows
    scale_factor = HEAD_DIM ** (-0.5)
    dot = functools.partial(jnp.einsum, preferred_element_type=f32)

    def as_chunks(rows):
        t = halves(own_rows)
        return rows.reshape(t, 1, own_rows // t, width)

    weight_halves = halves(rows_d)
    def as_pieces(wide):
        return wide.reshape(rows_d, dp_count, units).transpose(1, 0, 2)

    ffn_pieces = jnp.concatenate(
        [as_pieces(up_master.astype(half)), as_pieces(down_master.T.astype(half))], axis=2
    )
    slot_ids = mp_rank * slots + jnp.arange(slots)
    frame_ids = slot_ids // PATCHES
    keep = jnp.concatenate(
        [frame_ids[None, :] < frames[:, None], jnp.ones((items, lat_own), jnp.bool_)], axis=1
    )
    (
        weights,
        back_rows,
        source,
        latent_rows,
        queries,
        chances,
        blends,
        mixed_blocks,
        stats,
        ffn_pieces,
    ) = front(
        place,
        qkv_master,
        out_master.T,
        as_chunks(cotangent),
        latents,
        ffn_pieces,
        media,
        keep.astype(f32)[:, None],
        time_table,
        norm_params,
        weight_halves,
        heads,
        scale_factor,
    )
    weights = weights.reshape(mp_count, 4, width, block)
    w_out = weights[:, 3]
    latent_rows = latent_rows.transpose(1, 0, 2, 3).reshape(items, lat_total, width)
    part_peaks, part_sums = stats[:, :, :, 0], stats[:, :, :, 1]
    grow = jnp.exp(part_peaks - jnp.max(part_peaks, axis=0))
    shares = grow / jnp.sum(part_sums * grow, axis=0)
    share = lax.dynamic_index_in_dim(shares, mp_rank, 0, keepdims=False)
    own_shares = lax.dynamic_slice_in_dim(
        shares.reshape(mp_count, mp_count, items, heads, lat_total), mp_rank * lat_own, lat_own, 4
    )
    own_shares = jnp.repeat(own_shares.transpose(0, 1, 2, 4, 3), HEAD_DIM, axis=-1)
    mixed_full = jnp.sum(mixed_blocks * own_shares, axis=0)
    mixed_j = mixed_full.astype(half)
    after_attn = latents + dot("jile,jde->ild", mixed_j, w_out)
    ffn_norm = layer_norm(after_attn, norm_params[4], norm_params[5]).astype(half)
    t = halves(own_rows)
    by_chunk = (t, own_rows // t, width)
    (
        _,
        ffn_out,
        mixed_back_rows,
        row_terms,
        give,
        after_back,
        attn_low,
        ffn_sums,
    ) = (feed if 2 * all_rows * width <= ROWS_IN_VMEM else feed_apart)(
        place,
        as_chunks(ffn_norm),
        ffn_pieces,
        back_rows,
        after_attn.reshape(by_chunk),
        cotangent.reshape(by_chunk),
        mixed_full.reshape(mp_count, own_rows, block),
        norm_params,
        weights,
    )
    latents_out = after_attn + ffn_out.reshape(latents.shape)
    after_back, attn_low = after_back.reshape(latents.shape), attn_low.reshape(latents.shape)
    row_terms = row_terms.reshape(mp_count, mp_count, heads, items, lat_own)
    row_terms = row_terms.transpose(1, 3, 2, 0, 4).reshape(mp_count, items, heads * lat_total)
    back_j = (
        mixed_back_rows.reshape(mp_count, mp_count, items, lat_own, block)
        .transpose(1, 2, 0, 3, 4)
        .reshape(mp_count, items, lat_total, block)
    )
    _, media_grad, owned, ffn_owned, latents_grad, small, square = attend_back(
        place,
        source,
        latent_rows,
        queries,
        chances,
        blends,
        back_j,
        mixed_j,
        attn_low,
        jnp.stack([share, row_terms], axis=2),
        weights,
        give,
        [media, time_table, norm_params, latents, after_back, ffn_sums],
        weight_halves,
        heads,
        scale_factor,
    )
    groups = [
        (qkv_master, qkv_momentum, qkv_average),
        (out_master.T, out_momentum.T, out_average.T),
        (up_master, up_momentum, up_average),
        (down_master.T, down_momentum.T, down_average.T),
        (norm_params, norm_momentum, norm_average),
        (time_table, time_momentum, time_average),
    ]
    (
        grad_norm,
        media_grad,
        qkv_grad,
        qkv_new,
        qkv_momentum_new,
        qkv_average_new,
        qkv_copy,
        out_grad,
        out_new,
        out_momentum_new,
        out_average_new,
        out_copy,
        up_grad,
        up_new,
        up_momentum_new,
        up_average_new,
        up_copy,
        down_grad,
        down_new,
        down_momentum_new,
        down_average_new,
        down_copy,
        norm_grad,
        norm_new,
        norm_momentum_new,
        norm_average_new,
        time_grad,
        time_new,
        time_momentum_new,
        time_average_new,
    ) = refresh(square, small, owned, ffn_owned, media_grad, groups)
    grad_norm = grad_norm.reshape(())
    out_grad, out_new, out_momentum_new, out_average_new, out_copy = (
        value.T for value in (out_grad, out_new, out_momentum_new, out_average_new, out_copy)
    )
    down_grad, down_new, down_momentum_new, down_average_new, down_copy = (
        value.T for value in (down_grad, down_new, down_momentum_new, down_average_new, down_copy)
    )
    return (
        latents_out,
        latents_grad,
        media_grad,
        grad_norm,
        qkv_grad,
        qkv_new,
        qkv_momentum_new,
        qkv_average_new,
        out_grad,
        out_new,
        out_momentum_new,
        out_average_new,
        up_grad,
        up_new,
        up_momentum_new,
        up_average_new,
        down_grad,
        down_new,
        down_momentum_new,
        down_average_new,
        norm_grad,
        norm_new,
        norm_momentum_new,
        norm_average_new,
        time_grad,
        time_new,
        time_momentum_new,
        time_average_new,
        qkv_copy,
        out_copy,
        up_copy,
        down_copy,
    )


def solution(mesh):
    placed = (
        P("dp", "mp", None),
        P("dp", "mp", None),
        P("dp"),
        P("dp", "mp", None),
        P(None, "dp", "mp"),
        P(None, "dp", "mp"),
        P(None, "dp", "mp"),
        P("mp", "dp"),
        P("mp", "dp"),
        P("mp", "dp"),
        P("dp", "mp"),
        P("dp", "mp"),
        P("dp", "mp"),
        P("mp", "dp"),
        P("mp", "dp"),
        P("mp", "dp"),
        P(),
        P(),
        P(),
        P(),
        P(),
        P(),
    )
    return jax.shard_map(
        shards,
        mesh=mesh,
        in_specs=placed,
        out_specs=(
            P("dp", "mp", None),
            P("dp", "mp", None),
            P("dp", "mp", None),
            P(),
            P(None, "dp", "mp"),
            P(None, "dp", "mp"),
            P(None, "dp", "mp"),
            P(None, "dp", "mp"),
            P("mp", "dp"),
            P("mp", "dp"),
            P("mp", "dp"),
            P("mp", "dp"),
            P("dp", "mp"),
            P("dp", "mp"),
            P("dp", "mp"),
            P("dp", "mp"),
            P("mp", "dp"),
            P("mp", "dp"),
            P("mp", "dp"),
            P("mp", "dp"),
            P(),
            P(),
            P(),
            P(),
            P(),
            P(),
            P(),
            P(),
            P(None, "dp", "mp"),
            P("mp", "dp"),
            P("dp", "mp"),
            P("mp", "dp"),
        ),
        check_vma=False,
    )
```

```python
import functools
import math

import jax
import jax.numpy as jnp
from jax import lax
from jax.experimental import pallas as pl
from jax.experimental.pallas import tpu as pltpu
from jax.sharding import PartitionSpec as P

HEAD_DIM = 96
FRAMES = 8
PATCHES = 256


EPS = 1e-05
MOMENT = 0.9
STEP_RATES = (30.0, 1200.0, 120.0, 40.0, 1000.0, 1200.0)
DECAY_AVG = 0.75
HIGH = lax.Precision.HIGHEST
NEGATIVE = -1e30
SWAP_AT = 5
ROWS_IN_VMEM = 5 * 1024 * 1024


def layer_norm(values, factor, offset):
    centered = values - jnp.mean(values, axis=-1, keepdims=True)
    variance = jnp.mean(centered * centered, axis=-1, keepdims=True)
    return centered * lax.rsqrt(variance + EPS) * factor + offset


def exact_gelu(values):
    return jax.nn.gelu(values, approximate=False)


def square_sum(arrays):
    running = jnp.zeros((), jnp.float32)
    for member in arrays:
        running = running + jnp.sum(member * member)
    return running


def advance(gradient, master, momentum, average, clip_factor, rate):
    clipped = gradient * clip_factor
    moment_new = MOMENT * momentum + clipped
    master_new = master - rate * (clipped + MOMENT * moment_new)
    average_new = DECAY_AVG * average + (1.0 - DECAY_AVG) * master_new
    return (clipped, master_new, moment_new, average_new)


class Place:
    def __init__(self, dp_count, mp_count):
        z_count = 4 if dp_count % 4 == 0 else 1
        c_count = 2 if mp_count % 2 == 0 else 1
        self.size = {
            "z": z_count,
            "x": dp_count // z_count,
            "y": mp_count // c_count,
            "c": c_count,
        }
        self.count = {"dp": dp_count, "mp": mp_count}

    def mine(self):
        dp, mp = lax.axis_index("dp"), lax.axis_index("mp")
        x_count, c_count = self.size["x"], self.size["c"]
        return {
            "z": lax.div(dp, x_count),
            "x": lax.rem(dp, x_count),
            "y": lax.div(mp, c_count),
            "c": lax.rem(mp, c_count),
        }

    def shifted(self, me, axis, step):
        return {**me, axis: lax.rem(me[axis] + step, self.size[axis])}

    def device(self, at):
        return {
            "dp": at["z"] * self.size["x"] + at["x"],
            "mp": at["y"] * self.size["c"] + at["c"],
        }


def region(ref, at, chunk, whole):
    def pick(axis):
        return slice(None) if axis in whole else at[axis]

    return ref.at[pick("y"), pick("c"), chunk[0], pick("z"), pick("x"), chunk[1]]


def remote(src, dst, send, recv, device):
    return pltpu.make_async_remote_copy(
        src_ref=src,
        dst_ref=dst,
        send_sem=send,
        recv_sem=recv,
        device_id=device,
        device_id_type=pl.DeviceIdType.MESH,
    )


def greet(devices):
    barrier = pltpu.get_barrier_semaphore()
    for device in devices:
        pl.semaphore_signal(
            barrier, inc=1, device_id=device, device_id_type=pl.DeviceIdType.MESH
        )
    pl.semaphore_wait(barrier, len(devices))


class Swap:
    def __init__(self, place, axis, spread, value, late=0):
        self.place, self.axis, self.spread, self.value = place, axis, spread, value
        self.late = late
        self.n = place.count[axis]
        shape = value.shape if spread else (self.n,) + value.shape
        self.out = jax.ShapeDtypeStruct(shape, value.dtype)
        self.scratch = [
            pltpu.SemaphoreType.DMA((self.n,)),
            pltpu.SemaphoreType.DMA((self.n,)),
        ]

    def peers(self):
        rank = lax.axis_index(self.axis)
        return [{self.axis: lax.rem(rank + k, self.n)} for k in range(1, self.n)]

    def begin(self, refs):
        self.refs = refs

    def steps(self):
        return self.late + 1

    def own(self):
        src, dst, send, _ = self.refs
        rank = lax.axis_index(self.axis)
        return pltpu.make_async_copy(
            src.at[rank] if self.spread else src, dst.at[rank], send.at[0]
        )

    def copies(self, receive):
        src, dst, send, recv = self.refs
        rank = lax.axis_index(self.axis)
        for k in range(1, self.n):
            there, here = lax.rem(rank + k, self.n), lax.rem(rank + self.n - k, self.n)
            yield remote(
                src.at[there] if self.spread else src,
                dst.at[here if receive else rank],
                send.at[k],
                recv.at[k],
                {self.axis: there},
            )

    def step(self, time):
        if time == self.late:
            self.own().start()
            for copy in self.copies(False):
                copy.start()

    def finish(self):
        self.own().wait()
        for copy in self.copies(False):
            copy.wait_send()
        for copy in self.copies(True):
            copy.wait_recv()


def pair_at(index, chunks):
    return [n for n in (2 * index, 2 * index + 1) if 0 <= n < len(chunks)]


GATHER_STAGES = (0, 2, 1, 3, 4)
REDUCE_STAGES = (4, 3, 2, 1, 0)
ORDERS = (("z", "x", "y", "c"), ("z", "y", "x", "c"))


class Gather:
    def __init__(self, place, value, late=0):
        self.place, self.value, self.late = place, value, late
        s = place.size
        t, h = value.shape[:2]
        self.chunks = [(a, b) for a in range(t) for b in range(h)]
        self.out = jax.ShapeDtypeStruct(
            (s["y"], s["c"], t, s["z"], s["x"], h) + value.shape[2:], value.dtype
        )
        self.most = max(s.values())
        sems = pltpu.SemaphoreType.DMA((len(self.chunks), 5, self.most))
        self.scratch = [sems, sems]

    def peers(self):
        me = self.place.mine()
        return [
            self.place.device(self.place.shifted(me, a, k))
            for a in "zxyc"
            for k in range(1, self.place.size[a])
        ]

    def copies(self, n, stage, receive):
        src, dst, send, recv = self.refs
        order = ORDERS[n % 2]
        axis, whole = order[stage], order[:stage]
        me = self.me
        for k in range(1, self.place.size[axis]):
            there = self.place.shifted(me, axis, k)
            here = self.place.shifted(me, axis, self.place.size[axis] - k)
            at = here if receive else me
            block = (
                src.at[self.chunks[n][0], self.chunks[n][1]]
                if stage == 0
                else region(dst, me, self.chunks[n], whole)
            )
            yield remote(
                block,
                region(dst, at, self.chunks[n], whole),
                send.at[n, stage, k],
                recv.at[n, stage, k],
                self.place.device(there),
            )

    def begin(self, refs):
        self.refs, self.me = refs, self.place.mine()

    def own(self, n):
        src, dst, send, _ = self.refs
        chunk = self.chunks[n]
        return pltpu.make_async_copy(
            src.at[chunk[0], chunk[1]], region(dst, self.me, chunk, ()), send.at[n, 4, 0]
        )

    def steps(self):
        return self.late + pl.cdiv(len(self.chunks), 2) + 4

    def step(self, time):
        for stage in GATHER_STAGES:
            for n in pair_at(time - self.late - stage, self.chunks):
                if stage == 0:
                    self.own(n).start()
                if stage == 1:
                    self.own(n).wait()
                if stage > 0:
                    for copy in self.copies(n, stage - 1, True):
                        copy.wait_recv()
                if stage < 4:
                    for copy in self.copies(n, stage, False):
                        copy.start()

    def finish(self):
        for n in range(len(self.chunks)):
            for stage in range(4):
                for copy in self.copies(n, stage, False):
                    copy.wait_send()


BACK_ORDERS = (("c", "y", "x", "z"), ("c", "x", "y", "z"))
LAYOUT = ("y", "z", "x")


class Reduce:
    def __init__(self, place, value, late=0, starts=None, kept=None):
        self.place, self.value = place, value
        s = place.size
        t, h = value.shape[2], value.shape[5]
        tail = value.shape[6:]
        self.chunks = [(a, b) for a in range(t) for b in range(h)]
        self.out = jax.ShapeDtypeStruct((t, h) + tail, jnp.float32)
        count = len(self.chunks)
        pairs = pl.cdiv(count, 2)
        self.starts = [late + k for k in range(pairs)] if starts is None else starts
        self.kept = count if kept is None else min(kept, count)
        sems = pltpu.SemaphoreType.DMA((count, 5, max(s.values())))
        full = tuple(s[a] for a in LAYOUT)
        held = pltpu.VMEM((self.kept,) + full + tail, value.dtype)
        self.scratch = [sems, sems, held, held]
        self.spots = {}
        for parity in range(min(2, count)):
            mine = (count + 1 - parity) // 2
            left = list(LAYOUT)
            for stage, axis in list(enumerate(BACK_ORDERS[parity]))[1:]:
                left.remove(axis)
                shape = (mine, max(s[axis] - 1, 1)) + tuple(s[a] for a in left) + tail
                self.spots[parity, stage] = len(self.scratch)
                self.scratch.append(pltpu.VMEM(shape, value.dtype))
        self.out_spot = len(self.scratch)
        self.scratch.append(pltpu.VMEM((t, h) + tail, jnp.float32))
        self.scratch.append(pltpu.SemaphoreType.DMA((1,)))
        self.scratch.append(pltpu.SemaphoreType.REGULAR)

    peers = Gather.peers

    def part(self, n, stage, at):
        order = BACK_ORDERS[n % 2]
        if stage == 0:
            return self.source(n, at)
        index = tuple(
            at if a == order[stage] else self.me[a] if a in order[:stage] else slice(None)
            for a in LAYOUT
        )
        return self.scr[2].at[(n % self.kept,) + index]

    def into(self, n, stage):
        if stage == 0:
            return self.scr[3].at[pl.ds(n % self.kept, 1)]
        return self.scr[self.spots[n % 2, stage]].at[n // 2]

    def copies(self, n, stage):
        axis = BACK_ORDERS[n % 2][stage]
        for k in range(1, self.place.size[axis]):
            there = self.place.shifted(self.me, axis, k)
            yield remote(
                self.part(n, stage, there[axis]),
                self.into(n, stage).at[k - 1],
                self.scr[0].at[n, stage, k],
                self.scr[1].at[n, stage, k],
                self.place.device(there),
            )

    def source(self, n, at):
        t, h = self.chunks[n]
        if t in self.apart:
            return self.apart[t].at[:, at, :, :, h]
        return self.src.at[:, at, t, :, :, h]

    def own(self, n):
        return pltpu.make_async_copy(
            self.source(n, self.me["c"]),
            self.scr[2].at[n % self.kept],
            self.scr[0].at[n, 4, 0],
        )

    def begin(self, refs, apart=()):
        self.src, self.dst, self.scr = refs[0], refs[1], refs[2:]
        self.apart = dict(apart)
        self.me = self.place.mine()

    def steps(self):
        return self.starts[-1] + 5

    def add(self, n, stage):
        order = BACK_ORDERS[n % 2]
        axis = order[stage]
        count = self.place.size[axis] - 1
        into = self.into(n, stage)
        sizes = [self.place.size[a] for a in LAYOUT if a not in order[: stage + 1]]
        if stage == 0:
            base = target = self.scr[2].at[n % self.kept]
        else:
            base = target = self.part(n, stage, self.me[axis])
        if stage == 3:
            target = self.scr[self.out_spot].at[self.chunks[n][0], self.chunks[n][1]]

        def one(flat, carry):
            index = []
            rest = flat
            for size in reversed(sizes):
                index.insert(0, lax.rem(rest, size))
                rest = lax.div(rest, size)
            index = tuple(index) + (Ellipsis,)
            if count == 1 and target.dtype == base.dtype:
                target[index] = base[index] + into[(0,) + index]
                return carry
            value = base[index].astype(jnp.float32)
            for k in range(count):
                value = value + into[(k,) + index].astype(jnp.float32)
            target[index] = value.astype(target.dtype)
            return carry

        total = math.prod(sizes)
        if total == 1:
            one(jnp.int32(0), 0)
        else:
            lax.fori_loop(0, total, one, 0)

    def step(self, time):
        for stage in REDUCE_STAGES:
            for pair, start in enumerate(self.starts):
                if start + stage == time:
                    self.advance(pair, stage)

    def advance(self, pair, stage):
        sibling = self.place.device(self.place.shifted(self.me, "c", 1))
        reused = len(self.chunks) > self.kept and self.place.size["c"] > 1
        for n in pair_at(pair, self.chunks):
            if stage == 0:
                if n >= self.kept:
                    for old in range(4):
                        for copy in self.copies(n - self.kept, old):
                            copy.wait_send()
                    if reused:
                        pl.semaphore_wait(self.scr[-1], 1)
                self.own(n).start()
            if stage == 1:
                self.own(n).wait()
            if stage > 0:
                for copy in self.copies(n, stage - 1):
                    copy.wait_recv()
                self.add(n, stage - 1)
            if stage == 1 and reused and n + self.kept < len(self.chunks):
                pl.semaphore_signal(
                    self.scr[-1],
                    inc=1,
                    device_id=sibling,
                    device_id_type=pl.DeviceIdType.MESH,
                )
            if stage < 4:
                for copy in self.copies(n, stage):
                    copy.start()

    def finish(self):
        out = pltpu.make_async_copy(self.scr[self.out_spot], self.dst, self.scr[-2].at[0])
        out.start()
        for n in range(max(0, len(self.chunks) - self.kept), len(self.chunks)):
            for stage in range(4):
                for copy in self.copies(n, stage):
                    copy.wait_send()
        out.wait()


class Total:
    def __init__(self, place, value, axes=("c", "y", "x", "z"), split=False):
        self.place, self.value, self.split = place, value, split
        self.axes = axes + ("c",) if split else axes
        self.out = jax.ShapeDtypeStruct(value.shape, value.dtype)
        self.half = value.shape[0] // 2 if split else value.shape[0]
        sizes = [self.size(a) for a in self.axes]
        sems = pltpu.SemaphoreType.DMA((len(sizes), max(sizes)))
        self.scratch = [sems, sems] + [
            pltpu.VMEM(
                (size, self.half if k else value.shape[0]) + value.shape[1:], value.dtype
            )
            for k, size in enumerate(sizes)
        ]

    peers = Gather.peers

    def size(self, axis):
        return self.place.count[axis] if axis in self.place.count else self.place.size[axis]

    def spot(self, axis):
        return lax.axis_index(axis) if axis in self.place.count else self.me[axis]

    def begin(self, refs):
        self.src, self.dst, self.send, self.recv = refs[:4]
        self.bufs = refs[4:]
        self.me = self.place.mine()

    def copies(self, stage, receive):
        axis = self.axes[stage]
        size = self.size(axis)
        buf, mine = self.bufs[stage], self.spot(axis)
        for k in range(1, size):
            there = lax.rem(mine + k, size)
            here = lax.rem(mine + size - k, size)
            if axis in self.place.count:
                device = {axis: there}
            else:
                device = self.place.device({**self.me, axis: there})
            yield remote(
                buf.at[mine],
                buf.at[here if receive else mine],
                self.send.at[stage, k],
                self.recv.at[stage, k],
                device,
            )

    def advance(self, stage):
        if stage == 0:
            value = self.src[...]
        else:
            for copy in self.copies(stage - 1, True):
                copy.wait_recv()
            for copy in self.copies(stage - 1, False):
                copy.wait_send()
            buf, size = self.bufs[stage - 1], self.size(self.axes[stage - 1])
            if self.split and stage == len(self.axes):
                for k in range(size):
                    self.dst[k * self.half : (k + 1) * self.half] = buf[k]
                return
            if self.split and stage == 1:
                rows = pl.ds(pl.multiple_of(self.me["c"] * self.half, self.half), self.half)
            else:
                rows = slice(None)
            value = buf[0, rows]
            for k in range(1, size):
                value = value + buf[k, rows]
        if stage == len(self.axes):
            self.dst[...] = value
            return
        self.bufs[stage][self.spot(self.axes[stage])] = value
        for copy in self.copies(stage, False):
            copy.start()


def norm_back(value, factor, pulled):
    centered = value - jnp.mean(value, axis=-1, keepdims=True)
    variance = jnp.mean(centered * centered, axis=-1, keepdims=True)
    scale = lax.rsqrt(variance + EPS)
    unit = centered * scale
    inner = pulled * factor
    back = scale * (
        inner
        - jnp.mean(inner, axis=-1, keepdims=True)
        - unit * jnp.mean(inner * unit, axis=-1, keepdims=True)
    )
    return (
        back,
        jnp.sum(pulled * unit, axis=0, keepdims=True),
        jnp.sum(pulled, axis=0, keepdims=True),
    )


def communicate(label, number, parts):
    count = len(parts)

    def kernel(*refs):
        ins, outs, rest = refs[:count], refs[count : 2 * count], refs[2 * count :]
        devices, seen = [], set()
        for part in parts:
            kind = part.axis if isinstance(part, Swap) else "grid"
            if kind not in seen:
                seen.add(kind)
                devices += part.peers()
        greet(devices)
        spot = 0
        for part, src, dst in zip(parts, ins, outs):
            size = len(part.scratch)
            part.begin((src, dst) + tuple(rest[spot : spot + size]))
            spot += size
        staged = parts
        for time in range(max([part.steps() for part in staged], default=0)):
            for part in staged:
                part.step(time)
        for part in parts:
            part.finish()

    return pl.pallas_call(
        kernel,
        out_shape=[part.out for part in parts],
        in_specs=[pl.BlockSpec(memory_space=pl.ANY)] * count,
        out_specs=[pl.BlockSpec(memory_space=pl.ANY)] * count,
        scratch_shapes=[s for part in parts for s in part.scratch],
        compiler_params=pltpu.CompilerParams(
            collective_id=number, has_side_effects=True, vmem_limit_bytes=58 * 1024 * 1024
        ),
        name=label,
    )(*[part.value for part in parts])


def product(left, right, dims):
    return lax.dot_general(left, right, (dims, ((), ())), preferred_element_type=jnp.float32)


NN, NT, TN = ((1,), (0,)), ((1,), (1,)), ((0,), (0,))


def spread_heads(rows, heads):
    owner = lax.broadcasted_iota(jnp.int32, rows.shape, 1)
    kept = [
        jnp.where((owner >= h * HEAD_DIM) & (owner < (h + 1) * HEAD_DIM), rows, 0)
        for h in range(heads)
    ]
    return jnp.concatenate(kept, axis=0)


def fold_heads(wide, heads):
    rows = wide.shape[0] // heads
    owner = lax.broadcasted_iota(jnp.int32, (rows, wide.shape[1]), 1)
    out = wide[:rows]
    for h in range(1, heads):
        out = jnp.where(owner >= h * HEAD_DIM, wide[h * rows : (h + 1) * rows], out)
    return out


def as_row(column):
    wide = jnp.broadcast_to(column, (column.shape[0], 128))
    return jnp.transpose(wide)[:1]


def as_column(row):
    return jnp.transpose(jnp.broadcast_to(row, (128, row.shape[1])))[:, :1]


def front_kernel(place, heads, scale, halves_w, parts, *refs):
    half, f32 = jnp.bfloat16, jnp.float32
    qkv, out_t, cot_in, latents, ffn_in, media, keep, time_rows, norms = refs[:9]
    w_o, back_o, src_o, lat_o, q_o, p_o, blend_o, mixed_o, stat_o, ffn_o = refs[9:19]
    w_vm, lat_vm, src_vm, q_vm, p_vm, blend_vm, mixed_vm, stat_vm, sems = refs[19:28]
    own_w, cot, lat_in, stat_all = refs[28:32]
    rest = list(refs[32:])
    gather_w, gather_c, lat_swap, mixed_swap, stat_swap, ffn_swap = parts
    ends = (
        (own_w, w_vm),
        (cot, back_o),
        (lat_in, lat_vm),
        (mixed_vm, mixed_o),
        (stat_vm, stat_all),
        (ffn_in, ffn_o),
    )
    for part, end in zip(parts, ends):
        size = len(part.scratch)
        part.begin(end + tuple(rest[:size]))
        rest = rest[size:]
    items, slots, width = media.shape
    lat_own = latents.shape[1]
    blocks, block = q_vm.shape[0], q_vm.shape[3]
    lat_total = blocks * lat_own
    c_count = place.size["c"]
    mp_rank = lax.axis_index("mp")
    greet(gather_w.peers() + lat_swap.peers() + ffn_swap.peers())
    clock = [0]

    def run_to(time):
        while clock[0] <= time:
            for part in (lat_swap, gather_w, gather_c, ffn_swap):
                part.step(clock[0])
            clock[0] += 1

    def arrived(t):
        return 4 + ((t + 1) * halves_w - 1) // 2

    def weight(j, t):
        return w_vm[lax.div(j, c_count), lax.rem(j, c_count), t].reshape(width, block)

    kept = []

    def keep_copy(src, dst):
        copy = pltpu.make_async_copy(src, dst, sems.at[len(kept)])
        copy.start()
        kept.append(copy)

    for n in range(items):
        lat_in[n] = layer_norm(latents[n], norms[2:3], norms[3:4]).astype(half)
    for t in range(4):
        value = qkv[t] if t < 3 else out_t[...]
        own_w[t] = value.astype(half).reshape(own_w.shape[1:])
    run_to(0)
    cot[...] = cot_in[...].astype(half)
    step_rows = math.gcd(64, slots)
    per_item = slots // step_rows

    def norm_media(k, carry):
        item, first = lax.div(k, per_item), lax.rem(k, per_item) * step_rows
        first = pl.multiple_of(first, step_rows)
        frame = lax.div(mp_rank * slots + first, PATCHES)
        value = media[item, pl.ds(first, step_rows)].astype(f32) + time_rows[pl.ds(frame, 1)]
        value = layer_norm(value, norms[0:1], norms[1:2])
        src_vm[item, pl.ds(first, step_rows)] = value.astype(half)
        return carry

    lax.fori_loop(0, items * per_item, norm_media, 0)
    src_vm[:, slots:] = lat_in[...]
    keep_copy(src_vm, src_o)
    run_to(3)
    lat_swap.finish()
    keep_copy(lat_vm, lat_o)
    run_to(arrived(0))

    def ask(j, carry):
        rows = jnp.concatenate(
            [lat_vm[:, n].reshape(lat_total, width) for n in range(items)], axis=0
        )
        query = product(rows, weight(j, 0), NN).astype(half)
        q_vm[j] = query.reshape(items, lat_total, block)
        return carry

    lax.fori_loop(0, blocks, ask, 0)
    keep_copy(q_vm, q_o)
    run_to(arrived(1))

    def score(k, carry):
        j, n = lax.div(k, items), lax.rem(k, items)
        source = src_vm[n]
        reach = product(spread_heads(q_vm[j, n], heads), weight(j, 1), NT).astype(half)
        value = product(reach, source, NT) * scale
        value = jnp.where(keep[n] > 0, value, NEGATIVE)
        peak = jnp.max(value, axis=1, keepdims=True)
        raised = jnp.exp(value - peak)
        total = jnp.sum(raised, axis=1, keepdims=True)
        low = raised.astype(half)
        p_vm[j, n] = low
        blend_vm[j, n] = product(low, source, NN).astype(half)
        stat_vm[j, n, 0:1] = as_row(peak)
        stat_vm[j, n, 1:2] = as_row(total)
        return carry

    lax.fori_loop(0, blocks * items // 2, score, 0)
    run_to(max(arrived(1) + 1, arrived(2)))
    lax.fori_loop(blocks * items // 2, blocks * items, score, 0)
    keep_copy(p_vm, p_o)
    keep_copy(blend_vm, blend_o)

    def mix(k, carry):
        j, n = lax.div(k, items), lax.rem(k, items)
        value = fold_heads(product(blend_vm[j, n], weight(j, 2), NN), heads)
        mixed_vm[:, j, n] = value.reshape(blocks, lat_own, block)
        return carry

    lax.fori_loop(0, blocks * items, mix, 0)
    mixed_swap.step(0)
    stat_swap.step(0)
    run_to(arrived(3))
    keep_copy(w_vm, w_o)
    run_to(gather_c.steps())
    for part in parts:
        if part is not lat_swap:
            part.finish()
    peaks = [stat_all[k, :, :, 0] for k in range(blocks)]
    top = functools.reduce(jnp.maximum, peaks)
    grow = [jnp.exp(peak - top) for peak in peaks]
    total = sum(stat_all[k, :, :, 1] * grow[k] for k in range(blocks))
    for k in range(blocks):
        stat_o[k] = grow[k] / total
    for copy in kept:
        copy.wait()


def front(
    place, qkv, out_t, cot, latents, ffn_pieces, media, keep, time_rows, norms, halves_w, heads, scale
):
    half, f32 = jnp.bfloat16, jnp.float32
    items, slots, width = media.shape
    lat_own = latents.shape[1]
    rows_d, block = out_t.shape
    blocks = place.count["mp"]
    own_weights = jax.ShapeDtypeStruct((4, halves_w, rows_d // halves_w, block), half)
    low_cot = jax.ShapeDtypeStruct(cot.shape, half)
    latent_norm = jax.ShapeDtypeStruct(latents.shape, half)
    lat, keys = blocks * lat_own, slots + lat_own
    rows = heads * lat
    late = 2 * halves_w
    mixed = jax.ShapeDtypeStruct((blocks, blocks, items, lat_own, block), f32)
    stats = jax.ShapeDtypeStruct((blocks, items, 2, rows), f32)
    parts = [
        Gather(place, own_weights),
        Gather(place, low_cot, late),
        Swap(place, "mp", False, latent_norm),
        Swap(place, "mp", True, mixed),
        Swap(place, "mp", False, stats),
        Swap(place, "dp", True, ffn_pieces, SWAP_AT),
    ]
    shapes = [
        parts[0].out,
        parts[2].out,
        jax.ShapeDtypeStruct((items, keys, width), half),
        jax.ShapeDtypeStruct((blocks, items, lat, block), half),
        jax.ShapeDtypeStruct((blocks, items, rows, keys), half),
        jax.ShapeDtypeStruct((blocks, items, rows, width), half),
        mixed,
        stats,
    ]
    scratch = [pltpu.VMEM(shape.shape, shape.dtype) for shape in shapes]
    scratch.append(pltpu.SemaphoreType.DMA((8,)))
    scratch += [pltpu.VMEM(v.shape, half) for v in (own_weights, low_cot, latent_norm)]
    scratch.append(pltpu.VMEM(parts[4].out.shape, f32))
    for part in parts:
        scratch += part.scratch
    whole = pl.BlockSpec(memory_space=pltpu.VMEM)
    hbm = pl.BlockSpec(memory_space=pl.ANY)
    return pl.pallas_call(
        functools.partial(front_kernel, place, heads, scale, halves_w, parts),
        in_specs=[whole] * 4 + [hbm] + [whole] * 4,
        out_specs=[hbm] * 8 + [whole, hbm],
        out_shape=[
            parts[0].out,
            parts[1].out,
            shapes[2],
            parts[2].out,
            shapes[3],
            shapes[4],
            shapes[5],
            parts[3].out,
            jax.ShapeDtypeStruct((blocks, blocks, items, rows), f32),
            parts[5].out,
        ],
        scratch_shapes=scratch,
        compiler_params=pltpu.CompilerParams(
            collective_id=1, has_side_effects=True, vmem_limit_bytes=64 * 1024 * 1024 - 65536
        ),
        name="front",
    )(qkv, out_t, cot, latents, ffn_pieces, media, keep, time_rows, norms)


def out_grad_shape(place, width, halves_w, block):
    s = place.size
    return (s["y"], s["c"], s["z"], s["x"], halves_w, width // (s["z"] * s["x"] * halves_w), block)


def feed_kernel(place, parts, *refs):
    half, f32 = jnp.bfloat16, jnp.float32
    own_rows, pieces, back_rows, after_attn, cot, mixed, norms, weights = refs[:8]
    (norm_o, ffn_o, back_o, term_o, grad_o, give_o, after_o, low_o, sums_o, lat_o) = refs[8:18]
    (rows_vm, up_vm, down_vm, share_a, share_b, w_out) = refs[18:24]
    (hid_vm, pre_vm, mixed_vm, term_vm, grad_vm, sem) = refs[24:30]
    rest = list(refs[30:])
    gather, first, second, back_swap, term_swap = parts
    ends = (
        (own_rows, rows_vm),
        (share_a, norm_o),
        (share_b, ffn_o),
        (mixed_vm, back_o),
        (term_vm, term_o),
    )
    for part, end in zip(parts, ends):
        size = len(part.scratch)
        part.begin(end + tuple(rest[:size]))
        rest = rest[size:]
    c_count, blocks = place.size["c"], place.count["mp"]
    width, units = norms.shape[1], hid_vm.shape[2]
    greet(gather.peers() + back_swap.peers())
    out_weight = pltpu.make_async_copy(weights.at[:, 3], w_out, sem.at[0])
    gather.step(0)
    out_weight.start()
    up_vm[...] = pieces[:, :, :units].reshape(width, units)
    down_vm[...] = pieces[:, :, units:].reshape(width, units)
    for time in range(1, gather.steps()):
        gather.step(time)

    def inner(m, carry):
        y, c = lax.div(m, c_count), lax.rem(m, c_count)
        w_up, w_down = up_vm[...], down_vm[...]
        rows = rows_vm[y, c].reshape(-1, width)
        pre = product(rows, w_up, NN)
        pulled = product(back_rows[y, c].reshape(-1, width), w_down, NN)
        chance = 0.5 * (1.0 + lax.erf(pre * math.sqrt(0.5)))
        slope = chance + pre * jnp.exp(-0.5 * pre * pre) * math.sqrt(0.5 / math.pi)
        hid_vm[m] = (pre * chance).astype(half)
        pre_back = (pulled * slope).astype(half)
        pre_vm[m] = pre_back
        share = product(pre_back, w_up, NT).astype(half)
        share_a[y, c] = share.reshape(share_a.shape[2:])
        return carry

    lax.fori_loop(0, blocks, inner, 0)
    first.step(0)

    def outer(m, carry):
        y, c = lax.div(m, c_count), lax.rem(m, c_count)
        share = product(hid_vm[m], down_vm[...], NT).astype(half)
        share_b[y, c] = share.reshape(share_b.shape[2:])
        return carry

    lax.fori_loop(0, blocks, outer, 0)
    first.step(1)
    second.step(0)
    give = product(rows_vm[...].reshape(-1, width), pre_vm[...].reshape(-1, units), TN)
    half_shape = give_o.shape[:2] + (units,)
    give_o[:, :, :units] = give.astype(half).reshape(half_shape)
    give = product(back_rows[...].reshape(-1, width), hid_vm[...].reshape(-1, units), TN)
    give_o[:, :, units:] = give.astype(half).reshape(half_shape)
    first.step(2)
    second.step(1)
    first.step(3)
    second.step(2)
    first.step(4)
    pulled = first.scr[first.out_spot]
    factors = jnp.zeros((1, width), f32)
    offsets = jnp.zeros((1, width), f32)
    for t in range(after_attn.shape[0]):
        value, factor, offset = norm_back(after_attn[t], norms[4:5], pulled[t, 0])
        value = cot[t] + value
        after_o[t] = value
        low_o[t] = value.astype(half)
        factors += factor
        offsets += offset
    sums_o[0:1] = factors
    sums_o[1:2] = offsets
    out_weight.wait()
    low = low_o[...].reshape(-1, width)
    heads = term_vm.shape[0] // blocks
    for j in range(blocks):
        back = product(low, w_out[j].reshape(width, -1), NN).astype(half)
        mixed_vm[j] = back
        both = mixed[j] * back.astype(f32)
        owner = lax.broadcasted_iota(jnp.int32, both.shape, 1)
        for h in range(heads):
            mine = (owner >= h * HEAD_DIM) & (owner < (h + 1) * HEAD_DIM)
            term = jnp.sum(jnp.where(mine, both, 0.0), axis=1, keepdims=True)
            term_vm[j * heads + h : j * heads + h + 1] = as_row(term)
    back_swap.step(0)
    term_swap.step(0)
    second.step(3)
    for j in range(blocks):
        grad = product(low, mixed[j].astype(half), TN).astype(half)
        grad_vm[j // c_count, j % c_count] = grad.reshape(grad_vm.shape[2:])
    grad_copy = pltpu.make_async_copy(grad_vm, grad_o, sem.at[1])
    grad_copy.start()
    second.step(4)
    for t in range(after_attn.shape[0]):
        lat_o[t] = after_attn[t] + second.scr[second.out_spot][t, 0]
    for part in parts:
        part.finish()
    grad_copy.wait()


def feed(
    place, own_rows, pieces, back_rows, after_attn, cot, mixed, norms, weights, halves_w
):
    half, f32 = jnp.bfloat16, jnp.float32
    gather = Gather(place, own_rows)
    rows = gather.out
    width = norms.shape[1]
    blocks, flat, block = mixed.shape
    heads = block // HEAD_DIM
    units = pieces.shape[2] // 2
    per = math.prod(rows.shape[2:7])
    mixed_back = jax.ShapeDtypeStruct(mixed.shape, half)
    terms = jax.ShapeDtypeStruct((blocks * heads, flat), f32)
    grad = jax.ShapeDtypeStruct(out_grad_shape(place, width, halves_w, block), half)
    parts = [
        gather,
        Reduce(place, rows),
        Reduce(place, rows),
        Swap(place, "mp", False, mixed_back),
        Swap(place, "mp", False, terms),
    ]
    scratch = [
        pltpu.VMEM(rows.shape, half),
        pltpu.VMEM((width, units), half),
        pltpu.VMEM((width, units), half),
        pltpu.VMEM(rows.shape, half),
        pltpu.VMEM(rows.shape, half),
        pltpu.VMEM(weights.shape[:1] + weights.shape[2:], half),
        pltpu.VMEM((blocks, per, units), half),
        pltpu.VMEM((blocks, per, units), half),
        pltpu.VMEM(mixed.shape, half),
        pltpu.VMEM(terms.shape, f32),
        pltpu.VMEM(grad.shape, half),
        pltpu.SemaphoreType.DMA((2,)),
    ]
    for part in parts:
        scratch += part.scratch
    whole = pl.BlockSpec(memory_space=pltpu.VMEM)
    hbm = pl.BlockSpec(memory_space=pl.ANY)
    return pl.pallas_call(
        functools.partial(feed_kernel, place, parts),
        in_specs=[hbm] + [whole] * 6 + [hbm],
        out_specs=[hbm] * 5 + [whole] * 5,
        out_shape=[part.out for part in parts[1:]]
        + [
            grad,
            jax.ShapeDtypeStruct(pieces.shape, half),
            jax.ShapeDtypeStruct(after_attn.shape, f32),
            jax.ShapeDtypeStruct(after_attn.shape, half),
            jax.ShapeDtypeStruct((2, width), f32),
            jax.ShapeDtypeStruct(after_attn.shape, f32),
        ],
        scratch_shapes=scratch,
        compiler_params=pltpu.CompilerParams(
            collective_id=3, has_side_effects=True, vmem_limit_bytes=60 * 1024 * 1024
        ),
        name="feed",
    )(own_rows, pieces, back_rows, after_attn, cot, mixed, norms, weights)


def feed_apart(
    place, own_rows, pieces, back_rows, after_attn, cot, mixed, norms, weights, halves_w
):
    half, f32 = jnp.bfloat16, jnp.float32
    width, units = norms.shape[1], pieces.shape[2] // 2
    dot = functools.partial(jnp.einsum, preferred_element_type=f32)
    (ffn_rows,) = communicate("rows", 3, [Gather(place, own_rows)])
    shape, half_shape = ffn_rows.shape, pieces.shape[:2] + (units,)
    w_up, w_down = (
        part.reshape(width, units) for part in (pieces[:, :, :units], pieces[:, :, units:])
    )
    ffn_rows, back_rows = ffn_rows.reshape(-1, width), back_rows.reshape(-1, width)
    pre_act = dot("rd,df->rf", ffn_rows, w_up)
    hidden = exact_gelu(pre_act).astype(half)
    hidden_back = dot("rd,df->rf", back_rows, w_down)
    pre_back = jax.vjp(exact_gelu, pre_act)[1](hidden_back)[0].astype(half)
    norm_part = dot("rf,df->rd", pre_back, w_up).astype(half)
    ffn_part = dot("rf,df->rd", hidden, w_down).astype(half)
    down_part = dot("rd,rf->df", back_rows, hidden).astype(half)
    up_part = dot("rd,rf->df", ffn_rows, pre_back).astype(half)
    norm_pulled, ffn_out = communicate(
        "ffn",
        4,
        [Reduce(place, norm_part.reshape(shape)), Reduce(place, ffn_part.reshape(shape))],
    )
    pull = jax.vjp(layer_norm, after_attn, norms[4], norms[5])[1]
    through, factor, offset = pull(norm_pulled.reshape(after_attn.shape))
    after_back = cot + through
    low = after_back.astype(half)
    mixed_back = dot("ld,jde->jle", low.reshape(-1, width), weights[:, 3]).astype(half)
    terms = jnp.sum(
        (mixed * mixed_back.astype(f32)).reshape(*mixed.shape[:2], -1, HEAD_DIM), axis=-1
    )
    terms = terms.transpose(0, 2, 1).reshape(-1, mixed.shape[1])
    mixed_rows, terms = communicate(
        "back", 5, [Swap(place, "mp", False, mixed_back), Swap(place, "mp", False, terms)]
    )
    sums = jnp.stack([factor, offset])
    grad = dot("ld,jle->jde", low.reshape(-1, width), mixed.astype(half)).astype(half)
    return (
        norm_pulled,
        ffn_out,
        mixed_rows,
        terms,
        grad.reshape(out_grad_shape(place, width, halves_w, mixed.shape[2])),
        jnp.concatenate([up_part.reshape(half_shape), down_part.reshape(half_shape)], axis=2),
        after_back,
        low,
        sums,
        after_attn + ffn_out.reshape(after_attn.shape),
    )


def attend_back_kernel(place, heads, scale, reduce, swap, latent_swap, totals, *refs):
    half, f32 = jnp.bfloat16, jnp.float32
    (src, lat, q, p, blend, back, out_part, row, wq, wk, wv, give) = refs[:12]
    (media, time_rows, norms, latents, after_back, ffn_sums) = refs[12:18]
    (grad_o, media_o, owned_o, ffn_o, latents_o, small_o, square_o) = refs[18:25]
    (acc, lat_acc, lat_vm, kept, stage_a, stage_b, small, square, ffn_vm, joined, stage_sem) = refs[
        25:36
    ]
    rest = list(refs[36:])
    phase, block = pl.program_id(0), pl.program_id(1)
    blocks = pl.num_programs(1)
    items = src.shape[0]
    lat_total = lat.shape[1]
    width = src.shape[2]
    for part, give, out in (
        (reduce, grad_o, owned_o),
        (swap, give, ffn_vm),
        (latent_swap, lat_acc, lat_vm),
        (totals[0], small, small_o),
        (totals[1], square, square_o),
    ):
        size = len(part.scratch)
        if part is reduce:
            part.begin((give, out) + tuple(rest[:size]), {3: out_part})
        else:
            part.begin((give, out) + tuple(rest[:size]))
        rest = rest[size:]

    def at(number, index, action):
        pl.when((phase == number) & (block == index))(action)

    last = place.count["mp"] - 1
    plan, moves_1, moves_2 = reduce_plan(len(reduce.chunks), place.count["mp"], items)
    c_count = place.size["c"]
    y_of, c_of = lax.div(block, c_count), lax.rem(block, c_count)

    def staged(t, buffer, number):
        return pltpu.make_async_copy(buffer, grad_o.at[y_of, c_of, t], stage_sem.at[number])

    def hand_over(*shares):
        @pl.when(block > 0)
        def _():
            for k, (t, _) in enumerate(shares):
                staged(t, (stage_a, stage_b)[k], k).wait()

        for k, (t, value) in enumerate(shares):
            buffer = (stage_a, stage_b)[k]
            buffer[...] = value.astype(half).reshape(buffer.shape)
            staged(t, buffer, k).start()

        @pl.when(block == last)
        def _():
            for k, (t, _) in enumerate(shares):
                staged(t, (stage_a, stage_b)[k], k).wait()

    def of_item(ref, item):
        return ref[:, 0, item].reshape(lat_total, ref.shape[4])

    def column(item, which):
        return as_column(row[0, item, which : which + 1])

    def events(number, half_step):
        for (where, point), moves in plan.items():
            if where == number and point % items == half_step:

                def carry_out(moves=moves):
                    for move in moves:
                        reduce.advance(*move)

                at(where, point // items, carry_out)

    def start():
        greet(swap.peers() + latent_swap.peers() + reduce.peers())
        if len(reduce.chunks) == 8:
            reduce.advance(0, 0)
        swap.step(0)

    at(0, 0, start)

    @pl.when(phase == 0)
    def _():
        back_s = jnp.concatenate(
            [
                (spread_heads(of_item(back, n), heads) * column(n, 0)).astype(half)
                for n in range(items)
            ],
            axis=0,
        )
        value_grad = product(blend[0].reshape(back_s.shape[0], width), back_s, TN)
        hand_over((2, value_grad))

    events(0, items - 1)

    @pl.when(phase == 1)
    def _():
        turns = []
        queries = jnp.concatenate([spread_heads(q[0, n], heads) for n in range(items)], axis=0)
        back_s = jnp.concatenate([spread_heads(of_item(back, n), heads) for n in range(items)], axis=0)
        pulls = product(back_s, wv[0, 0], NT).astype(half)
        rows = pulls.shape[0] // items
        for n in range(items):
            prob_back = product(pulls[n * rows : (n + 1) * rows], src[n], NT)
            score_back = (
                p[0, n].astype(jnp.float32) * (column(n, 0) * scale) * (prob_back - column(n, 1))
            ).astype(half)
            kept[block, n] = score_back
            turns.append(product(score_back, src[n], NN).astype(half))
            if n + 1 < items:
                events(1, n)
        turns = jnp.concatenate(turns, axis=0)
        key_turns = product(turns, wk[0, 0], NN)
        query_backs = jnp.concatenate(
            [fold_heads(key_turns[n * rows : (n + 1) * rows], heads) for n in range(items)], axis=0
        ).astype(half)
        latent_back = product(query_backs, wq[0, 0], NT)
        latent_back = latent_back.reshape(items, lat_acc.shape[0], -1, width)

        @pl.when(block == 0)
        def _():
            for n in range(items):
                lat_acc[:, n] = latent_back[n]

        @pl.when(block > 0)
        def _():
            for n in range(items):
                lat_acc[:, n] += latent_back[n]

        key_grad = product(turns, queries, TN)
        query_grad = product(lat[...].reshape(items * lat_total, width), query_backs, TN)
        hand_over((1, key_grad), (0, query_grad))

    events(1, items - 1)
    at(1, last, lambda: latent_swap.step(0))

    @pl.when(phase == 2)
    def _():
        queries = jnp.concatenate([spread_heads(q[0, n], heads) for n in range(items)], axis=0)
        back_s = jnp.concatenate([spread_heads(of_item(back, n), heads) for n in range(items)], axis=0)
        pulls = product(back_s, wv[0, 0], NT)
        reach = product(queries, wk[0, 0], NT).astype(half)
        rows = pulls.shape[0] // items
        for n in range(items):
            mine = slice(n * rows, (n + 1) * rows)
            value = product(
                jnp.concatenate([kept[block, n], p[0, n]], axis=0),
                jnp.concatenate([reach[mine], (pulls[mine] * column(n, 0)).astype(half)], axis=0),
                TN,
            )

            @pl.when(block == 0)
            def _():
                acc[n] = value

            @pl.when(block > 0)
            def _():
                acc[n] += value

            if n + 1 < items:
                events(2, n)

    events(2, items - 1)

    slots = media.shape[1]
    step_rows = math.gcd(64, slots)
    per_item = slots // step_rows
    mp_rank = lax.axis_index("mp")

    def media_back(k, carry):
        item, first = lax.div(k, per_item), lax.rem(k, per_item) * step_rows
        first = pl.multiple_of(first, step_rows)
        frame = lax.div(mp_rank * slots + first, PATCHES)
        value = media[item, pl.ds(first, step_rows)].astype(f32) + time_rows[pl.ds(frame, 1)]
        back, factor, offset = norm_back(
            value, norms[0:1], acc[item, pl.ds(first, step_rows)]
        )
        acc[item, pl.ds(first, step_rows)] = back
        small[0:1] += factor
        small[1:2] += offset
        small[pl.ds(6 + frame, 1)] += jnp.sum(back, axis=0, keepdims=True)
        return carry

    def end():
        small[...] = jnp.zeros_like(small)
        half_way = items * per_item // 2
        lax.fori_loop(0, half_way, media_back, 0)
        for move in moves_1:
            reduce.advance(*move)
        lax.fori_loop(half_way, items * per_item, media_back, 0)
        out = pltpu.make_async_copy(acc.at[:, pl.ds(0, slots)], media_o, stage_sem.at[0])
        out.start()
        latent_swap.finish()
        for n in range(items):
            pulled = acc[n, slots:]
            for k in range(lat_vm.shape[0]):
                pulled = pulled + lat_vm[k, n]
            value, factor, offset = norm_back(latents[n], norms[2:3], pulled)
            latents_o[n] = after_back[n] + value
            small[2:3] += factor
            small[3:4] += offset
        small[4:6] = ffn_sums[...]
        totals[0].advance(0)
        totals[0].advance(1)
        reduce.advance(*moves_2[0])
        totals[0].advance(2)
        for move in moves_2[1:-1]:
            reduce.advance(*move)
        totals[0].advance(3)
        swap.finish()
        units = ffn_vm.shape[2] // 2
        sums = jnp.zeros((1, 1), f32)
        for k in range(ffn_vm.shape[0]):
            piece = ffn_vm[k]
            joined[0, :, k * units : (k + 1) * units] = piece[:, :units]
            joined[1, :, k * units : (k + 1) * units] = piece[:, units:]
            value = piece.astype(f32)
            sums = sums + jnp.sum(value * value, keepdims=True)
        ffn_out = pltpu.make_async_copy(joined, ffn_o, stage_sem.at[1])
        ffn_out.start()
        totals[0].advance(4)
        reduce.advance(*moves_2[-1])
        if totals[0].split:
            totals[0].advance(5)
        owned = reduce.scr[reduce.out_spot]
        for t in range(owned.shape[0]):
            for h in range(owned.shape[1]):
                value = owned[t, h]
                sums = sums + jnp.sum(value * value, keepdims=True)
        square[...] = jnp.broadcast_to(sums, square.shape)
        totals[1].advance(0)
        reduce.finish()
        for stage in range(1, 3):
            totals[1].advance(stage)
        ffn_out.wait()
        out.wait()

    at(2, last, end)


def attend_back(
    place,
    source,
    latent_rows,
    query,
    chance,
    blend,
    back,
    out_part,
    rows_in,
    weights,
    give,
    rows_end,
    weight_halves,
    heads,
    scale,
):
    items, keys, width = source.shape
    lat = latent_rows.shape[1]
    own = back.shape[3]
    blocks, block = weights.shape[0], weights.shape[3]
    rows = heads * lat
    half, f32 = jnp.bfloat16, jnp.float32
    s = place.size
    part = width // (s["z"] * s["x"] * weight_halves)
    inner = (s["z"], s["x"], weight_halves, part, block)
    grad = jax.ShapeDtypeStruct((s["y"], s["c"], 4) + inner, half)
    lat_shares = jax.ShapeDtypeStruct((blocks, items, own, width), f32)
    order = [3, 2, 1, 0]
    reduce = Reduce(place, grad, kept=6 if weight_halves == 2 else 2)
    reduce.chunks = [(t, h) for t in order for h in range(weight_halves)]
    latent_swap = Swap(place, "mp", True, lat_shares)
    swap = Swap(place, "dp", True, give)
    joined = jax.ShapeDtypeStruct((2, give.shape[1], give.shape[0] * give.shape[2] // 2), half)
    small = jax.ShapeDtypeStruct((16, width), f32)
    square = jax.ShapeDtypeStruct((8, 128), f32)
    totals = [
        Total(place, small, split=s["c"] == 2),
        Total(place, square, axes=("mp", "dp")),
    ]
    slots = keys - own

    def weight(t, first):
        return pl.BlockSpec(
            (1, 1, width, block), lambda ph, j: (j * jnp.minimum(ph // first, 1), t, 0, 0)
        )

    def per(*shape):
        return pl.BlockSpec((1, items) + shape, lambda ph, j: (j,) + (0,) * (1 + len(shape)))

    def early(*shape):
        return pl.BlockSpec(
            (1, items) + shape,
            lambda ph, j: (j + (blocks - 1 - j) * jnp.minimum(ph, 1),) + (0,) * (1 + len(shape)),
        )

    def late(*shape):
        return pl.BlockSpec(
            (1, items) + shape,
            lambda ph, j: (j * jnp.minimum(ph, 1),) + (0,) * (1 + len(shape)),
        )

    whole = pl.BlockSpec(memory_space=pltpu.VMEM)
    hbm = pl.BlockSpec(memory_space=pl.ANY)
    scratch = [
        pltpu.VMEM((items, keys, width), f32),
        pltpu.VMEM(lat_shares.shape, f32),
        pltpu.VMEM(lat_shares.shape, f32),
        pltpu.VMEM((blocks, items, rows, keys), half),
        pltpu.VMEM(inner, half),
        pltpu.VMEM(inner, half),
        pltpu.VMEM(small.shape, f32),
        pltpu.VMEM(square.shape, f32),
        pltpu.VMEM(give.shape, half),
        pltpu.VMEM(joined.shape, half),
        pltpu.SemaphoreType.DMA((2,)),
    ]
    for member in [reduce, swap, latent_swap] + totals:
        scratch += member.scratch
    return pl.pallas_call(
        functools.partial(
            attend_back_kernel, place, heads, scale, reduce, swap, latent_swap, totals
        ),
        grid=(3, blocks),
        in_specs=[
            whole,
            whole,
            late(lat, block),
            late(rows, keys),
            early(rows, width),
            pl.BlockSpec(
                (blocks, 1, items, own, block), lambda ph, j: (0, j, 0, 0, 0)
            ),
            hbm,
            per(2, rows),
            weight(0, 1),
            weight(1, 1),
            weight(2, 1),
            hbm,
        ]
        + [whole] * 6,
        out_specs=[hbm] * 4 + [whole] * 3,
        out_shape=[
            grad,
            jax.ShapeDtypeStruct((items, slots, width), f32),
            reduce.out,
            joined,
            jax.ShapeDtypeStruct((items, own, width), f32),
            small,
            square,
        ],
        scratch_shapes=scratch,
        compiler_params=pltpu.CompilerParams(
            collective_id=6, has_side_effects=True, vmem_limit_bytes=64 * 1024 * 1024 - 65536
        ),
        name="attend_back",
    )(
        source,
        latent_rows,
        query,
        chance,
        blend,
        back,
        out_part,
        rows_in,
        weights,
        weights,
        weights,
        give,
        *rows_end,
    )


def reduce_plan(chunks, blocks, items):
    points = blocks * items
    if chunks == 8:
        eighths = {
            (0, 1): [(0, 1)],
            (0, 7): [(1, 0)],
            (1, 2): [(0, 2), (1, 1)],
            (1, 5): [(0, 3), (1, 2)],
            (1, 7): [(2, 0)],
            (2, 0): [(2, 1), (0, 4), (3, 0)],
            (2, 3): [(1, 3)],
            (2, 4): [(3, 1)],
            (2, 6): [(2, 2)],
        }
        ends = ((1, 4), (3, 2), (2, 3)), ((3, 3), (2, 4), (3, 4))
    else:
        eighths = {
            (0, 7): [(0, 0)],
            (1, 1): [(0, 1)],
            (1, 3): [(0, 2)],
            (1, 6): [(0, 3)],
            (1, 7): [(0, 4), (1, 0)],
            (2, 0): [(1, 1)],
        }
        ends = ((1, 2),), ((1, 3), (1, 4))
    plan = {
        (phase, (eighth + 1) * points // 8 - 1): moves for (phase, eighth), moves in eighths.items()
    }
    return plan, *ends


def refresh_kernel(*refs):
    f32 = jnp.float32
    square, small, owned, ffn, media_in = refs[:5]
    groups = [refs[5 + 3 * n : 8 + 3 * n] for n in range(6)]
    norm_o, media_o = refs[23:25]
    outs = [refs[25 + 5 * n : 30 + 5 * n] for n in range(4)]
    outs += [refs[45 + 4 * n : 49 + 4 * n] for n in range(2)]
    media_come = pltpu.make_async_copy(media_in, refs[53], refs[54].at[0])
    media_come.start()
    total = square[0:1, 0:1] + jnp.sum(small[...] * small[...], keepdims=True)
    norm = jnp.sqrt(total)
    norm_o[...] = norm
    clip = 1.0 / jnp.maximum(norm, 1.0)

    def update(number, at, gradient):
        master, momentum, average = groups[number]
        done = advance(
            gradient.astype(f32),
            master[at],
            momentum[at],
            average[at],
            clip,
            STEP_RATES[number],
        )
        for ref, value in zip(outs[number], done):
            ref[at] = value
        if number < 4:
            outs[number][4][at] = done[1].astype(jnp.bfloat16)

    parts, rows = owned.shape[1:3]
    for h in range(parts):
        for t in range(3):
            update(0, (t, pl.ds(h * rows, rows)), owned[t, h])
        update(1, pl.ds(h * rows, rows), owned[3, h])
    media_come.wait()
    media_go = pltpu.make_async_copy(refs[53], media_o, refs[54].at[1])
    media_go.start()
    step = math.gcd(ffn.shape[1], 16)

    def one(k, carry):
        at = pl.ds(pl.multiple_of(k * step, step), step)
        for n in range(2):
            update(2 + n, at, ffn[n, at])
        return carry

    lax.fori_loop(0, ffn.shape[1] // step, one, 0)
    update(4, Ellipsis, small[0:6])
    update(5, Ellipsis, small[6 : 6 + FRAMES])
    media_go.wait()


def refresh(square, small, owned, ffn, media_grad, groups):
    f32 = jnp.float32
    whole = pl.BlockSpec(memory_space=pltpu.VMEM)
    hbm = pl.BlockSpec(memory_space=pl.ANY)
    shapes = [
        jax.ShapeDtypeStruct((1, 1), f32),
        jax.ShapeDtypeStruct(media_grad.shape, f32),
    ]
    for n, group in enumerate(groups):
        shapes += [jax.ShapeDtypeStruct(group[0].shape, f32)] * 4
        if n < 4:
            shapes.append(jax.ShapeDtypeStruct(group[0].shape, jnp.bfloat16))
    arrays = [array for group in groups for array in group]
    return pl.pallas_call(
        refresh_kernel,
        in_specs=[whole] * 4 + [hbm] + [whole] * len(arrays),
        out_specs=[whole, hbm] + [whole] * (len(shapes) - 2),
        out_shape=shapes,
        scratch_shapes=[
            pltpu.VMEM(media_grad.shape, f32),
            pltpu.SemaphoreType.DMA((2,)),
        ],
        compiler_params=pltpu.CompilerParams(vmem_limit_bytes=60 * 1024 * 1024),
        name="refresh",
    )(square, small, owned, ffn, media_grad, *arrays)


def halves(rows):
    return 2 if rows % 32 == 0 else 1


def shards(
    latents,
    media,
    frames,
    cotangent,
    qkv_master,
    qkv_momentum,
    qkv_average,
    out_master,
    out_momentum,
    out_average,
    up_master,
    up_momentum,
    up_average,
    down_master,
    down_momentum,
    down_average,
    norm_params,
    norm_momentum,
    norm_average,
    time_table,
    time_momentum,
    time_average,
):
    f32 = jnp.float32
    half = jnp.bfloat16
    mp_rank = lax.axis_index("mp")
    mp_count = lax.axis_size("mp")
    dp_count = lax.axis_size("dp")
    place = Place(dp_count, mp_count)
    items, lat_own, width = latents.shape
    lat_total = lat_own * mp_count
    slots = media.shape[1]
    block = qkv_master.shape[2]
    rows_d = qkv_master.shape[1]
    heads = block // HEAD_DIM
    hidden_block = up_master.shape[1]
    units = hidden_block // dp_count
    own_rows = items * lat_own
    all_rows = dp_count * mp_count * own_rows
    scale_factor = HEAD_DIM ** (-0.5)
    dot = functools.partial(jnp.einsum, preferred_element_type=f32)

    def as_chunks(rows):
        t = halves(own_rows)
        return rows.reshape(t, 1, own_rows // t, width)

    weight_halves = halves(rows_d)
    def as_pieces(wide):
        return wide.reshape(rows_d, dp_count, units).transpose(1, 0, 2)

    ffn_pieces = jnp.concatenate(
        [as_pieces(up_master.astype(half)), as_pieces(down_master.T.astype(half))], axis=2
    )
    slot_ids = mp_rank * slots + jnp.arange(slots)
    frame_ids = slot_ids // PATCHES
    keep = jnp.concatenate(
        [frame_ids[None, :] < frames[:, None], jnp.ones((items, lat_own), jnp.bool_)], axis=1
    )
    (
        weights,
        back_rows,
        source,
        latent_rows,
        queries,
        chances,
        blends,
        mixed_blocks,
        shares,
        ffn_pieces,
    ) = front(
        place,
        qkv_master,
        out_master.T,
        as_chunks(cotangent),
        latents,
        ffn_pieces,
        media,
        keep.astype(f32)[:, None],
        time_table,
        norm_params,
        weight_halves,
        heads,
        scale_factor,
    )
    weights = weights.reshape(mp_count, 4, width, block)
    w_out = weights[:, 3]
    latent_rows = latent_rows.transpose(1, 0, 2, 3).reshape(items, lat_total, width)
    share = lax.dynamic_index_in_dim(shares, mp_rank, 0, keepdims=False)
    own_shares = lax.dynamic_slice_in_dim(
        shares.reshape(mp_count, mp_count, items, heads, lat_total), mp_rank * lat_own, lat_own, 4
    )
    own_shares = jnp.repeat(own_shares.transpose(0, 1, 2, 4, 3), HEAD_DIM, axis=-1)
    mixed_full = jnp.sum(mixed_blocks * own_shares, axis=0)
    mixed_j = mixed_full.astype(half)
    after_attn = latents + dot("jile,jde->ild", mixed_j, w_out)
    ffn_norm = layer_norm(after_attn, norm_params[4], norm_params[5]).astype(half)
    t = halves(own_rows)
    by_chunk = (t, own_rows // t, width)
    (
        _,
        _,
        mixed_back_rows,
        row_terms,
        out_part,
        give,
        after_back,
        attn_low,
        ffn_sums,
        latents_out,
    ) = (feed if 2 * all_rows * width <= ROWS_IN_VMEM else feed_apart)(
        place,
        as_chunks(ffn_norm),
        ffn_pieces,
        back_rows,
        after_attn.reshape(by_chunk),
        cotangent.reshape(by_chunk),
        mixed_full.reshape(mp_count, own_rows, block),
        norm_params,
        weights,
        weight_halves,
    )
    latents_out, after_back = latents_out.reshape(latents.shape), after_back.reshape(latents.shape)
    row_terms = row_terms.reshape(mp_count, mp_count, heads, items, lat_own)
    row_terms = row_terms.transpose(1, 3, 2, 0, 4).reshape(mp_count, items, heads * lat_total)
    back_j = mixed_back_rows.reshape(mp_count, mp_count, items, lat_own, block)
    _, media_grad, owned, ffn_owned, latents_grad, small, square = attend_back(
        place,
        source,
        latent_rows,
        queries,
        chances,
        blends,
        back_j,
        out_part,
        jnp.stack([share, row_terms], axis=2),
        weights,
        give,
        [media, time_table, norm_params, latents, after_back, ffn_sums],
        weight_halves,
        heads,
        scale_factor,
    )
    groups = [
        (qkv_master, qkv_momentum, qkv_average),
        (out_master.T, out_momentum.T, out_average.T),
        (up_master, up_momentum, up_average),
        (down_master.T, down_momentum.T, down_average.T),
        (norm_params, norm_momentum, norm_average),
        (time_table, time_momentum, time_average),
    ]
    (
        grad_norm,
        media_grad,
        qkv_grad,
        qkv_new,
        qkv_momentum_new,
        qkv_average_new,
        qkv_copy,
        out_grad,
        out_new,
        out_momentum_new,
        out_average_new,
        out_copy,
        up_grad,
        up_new,
        up_momentum_new,
        up_average_new,
        up_copy,
        down_grad,
        down_new,
        down_momentum_new,
        down_average_new,
        down_copy,
        norm_grad,
        norm_new,
        norm_momentum_new,
        norm_average_new,
        time_grad,
        time_new,
        time_momentum_new,
        time_average_new,
    ) = refresh(square, small, owned, ffn_owned, media_grad, groups)
    grad_norm = grad_norm.reshape(())
    out_grad, out_new, out_momentum_new, out_average_new, out_copy = (
        value.T for value in (out_grad, out_new, out_momentum_new, out_average_new, out_copy)
    )
    down_grad, down_new, down_momentum_new, down_average_new, down_copy = (
        value.T for value in (down_grad, down_new, down_momentum_new, down_average_new, down_copy)
    )
    return (
        latents_out,
        latents_grad,
        media_grad,
        grad_norm,
        qkv_grad,
        qkv_new,
        qkv_momentum_new,
        qkv_average_new,
        out_grad,
        out_new,
        out_momentum_new,
        out_average_new,
        up_grad,
        up_new,
        up_momentum_new,
        up_average_new,
        down_grad,
        down_new,
        down_momentum_new,
        down_average_new,
        norm_grad,
        norm_new,
        norm_momentum_new,
        norm_average_new,
        time_grad,
        time_new,
        time_momentum_new,
        time_average_new,
        qkv_copy,
        out_copy,
        up_copy,
        down_copy,
    )


def solution(mesh):
    placed = (
        P("dp", "mp", None),
        P("dp", "mp", None),
        P("dp"),
        P("dp", "mp", None),
        P(None, "dp", "mp"),
        P(None, "dp", "mp"),
        P(None, "dp", "mp"),
        P("mp", "dp"),
        P("mp", "dp"),
        P("mp", "dp"),
        P("dp", "mp"),
        P("dp", "mp"),
        P("dp", "mp"),
        P("mp", "dp"),
        P("mp", "dp"),
        P("mp", "dp"),
        P(),
        P(),
        P(),
        P(),
        P(),
        P(),
    )
    return jax.shard_map(
        shards,
        mesh=mesh,
        in_specs=placed,
        out_specs=(
            P("dp", "mp", None),
            P("dp", "mp", None),
            P("dp", "mp", None),
            P(),
            P(None, "dp", "mp"),
            P(None, "dp", "mp"),
            P(None, "dp", "mp"),
            P(None, "dp", "mp"),
            P("mp", "dp"),
            P("mp", "dp"),
            P("mp", "dp"),
            P("mp", "dp"),
            P("dp", "mp"),
            P("dp", "mp"),
            P("dp", "mp"),
            P("dp", "mp"),
            P("mp", "dp"),
            P("mp", "dp"),
            P("mp", "dp"),
            P("mp", "dp"),
            P(),
            P(),
            P(),
            P(),
            P(),
            P(),
            P(),
            P(),
            P(None, "dp", "mp"),
            P("mp", "dp"),
            P("dp", "mp"),
            P("mp", "dp"),
        ),
        check_vma=False,
    )
```

```python
import functools
import math

import jax
import jax.numpy as jnp
from jax import lax
from jax.experimental import pallas as pl
from jax.experimental.pallas import tpu as pltpu
from jax.sharding import PartitionSpec as P

HEAD_DIM = 96
FRAMES = 8
PATCHES = 256


EPS = 1e-05
MOMENT = 0.9
STEP_RATES = (30.0, 1200.0, 120.0, 40.0, 1000.0, 1200.0)
DECAY_AVG = 0.75
HIGH = lax.Precision.HIGHEST
NEGATIVE = -1e30
SWAP_AT = 5
ROWS_IN_VMEM = 5 * 1024 * 1024


def layer_norm(values, factor, offset):
    centered = values - jnp.mean(values, axis=-1, keepdims=True)
    variance = jnp.mean(centered * centered, axis=-1, keepdims=True)
    return centered * lax.rsqrt(variance + EPS) * factor + offset


def exact_gelu(values):
    return jax.nn.gelu(values, approximate=False)


def square_sum(arrays):
    running = jnp.zeros((), jnp.float32)
    for member in arrays:
        running = running + jnp.sum(member * member)
    return running


def advance(gradient, master, momentum, average, clip_factor, rate):
    clipped = gradient * clip_factor
    moment_new = MOMENT * momentum + clipped
    master_new = master - rate * (clipped + MOMENT * moment_new)
    average_new = DECAY_AVG * average + (1.0 - DECAY_AVG) * master_new
    return (clipped, master_new, moment_new, average_new)


class Place:
    def __init__(self, dp_count, mp_count):
        z_count = 4 if dp_count % 4 == 0 else 1
        c_count = 2 if mp_count % 2 == 0 else 1
        self.size = {
            "z": z_count,
            "x": dp_count // z_count,
            "y": mp_count // c_count,
            "c": c_count,
        }
        self.count = {"dp": dp_count, "mp": mp_count}

    def mine(self):
        dp, mp = lax.axis_index("dp"), lax.axis_index("mp")
        x_count, c_count = self.size["x"], self.size["c"]
        return {
            "z": lax.div(dp, x_count),
            "x": lax.rem(dp, x_count),
            "y": lax.div(mp, c_count),
            "c": lax.rem(mp, c_count),
        }

    def shifted(self, me, axis, step):
        return {**me, axis: lax.rem(me[axis] + step, self.size[axis])}

    def device(self, at):
        return {
            "dp": at["z"] * self.size["x"] + at["x"],
            "mp": at["y"] * self.size["c"] + at["c"],
        }


def region(ref, at, chunk, whole):
    def pick(axis):
        return slice(None) if axis in whole else at[axis]

    return ref.at[pick("y"), pick("c"), chunk[0], pick("z"), pick("x"), chunk[1]]


def remote(src, dst, send, recv, device):
    return pltpu.make_async_remote_copy(
        src_ref=src,
        dst_ref=dst,
        send_sem=send,
        recv_sem=recv,
        device_id=device,
        device_id_type=pl.DeviceIdType.MESH,
    )


def greet(devices):
    barrier = pltpu.get_barrier_semaphore()
    for device in devices:
        pl.semaphore_signal(
            barrier, inc=1, device_id=device, device_id_type=pl.DeviceIdType.MESH
        )
    pl.semaphore_wait(barrier, len(devices))


class Swap:
    def __init__(self, place, axis, spread, value, late=0):
        self.place, self.axis, self.spread, self.value = place, axis, spread, value
        self.late = late
        self.n = place.count[axis]
        shape = value.shape if spread else (self.n,) + value.shape
        self.out = jax.ShapeDtypeStruct(shape, value.dtype)
        self.scratch = [
            pltpu.SemaphoreType.DMA((self.n,)),
            pltpu.SemaphoreType.DMA((self.n,)),
        ]

    def peers(self):
        rank = lax.axis_index(self.axis)
        return [{self.axis: lax.rem(rank + k, self.n)} for k in range(1, self.n)]

    def begin(self, refs):
        self.refs = refs

    def steps(self):
        return self.late + 1

    def own(self):
        src, dst, send, _ = self.refs
        rank = lax.axis_index(self.axis)
        return pltpu.make_async_copy(
            src.at[rank] if self.spread else src, dst.at[rank], send.at[0]
        )

    def copies(self, receive):
        src, dst, send, recv = self.refs
        rank = lax.axis_index(self.axis)
        for k in range(1, self.n):
            there, here = lax.rem(rank + k, self.n), lax.rem(rank + self.n - k, self.n)
            yield remote(
                src.at[there] if self.spread else src,
                dst.at[here if receive else rank],
                send.at[k],
                recv.at[k],
                {self.axis: there},
            )

    def step(self, time):
        if time == self.late:
            self.own().start()
            for copy in self.copies(False):
                copy.start()

    def finish(self):
        self.own().wait()
        for copy in self.copies(False):
            copy.wait_send()
        for copy in self.copies(True):
            copy.wait_recv()


def pair_at(index, chunks):
    return [n for n in (2 * index, 2 * index + 1) if 0 <= n < len(chunks)]


GATHER_STAGES = (0, 2, 1, 3, 4)
REDUCE_STAGES = (4, 3, 2, 1, 0)
ORDERS = (("z", "x", "y", "c"), ("z", "y", "x", "c"))


class Gather:
    def __init__(self, place, value, late=0):
        self.place, self.value, self.late = place, value, late
        s = place.size
        t, h = value.shape[:2]
        self.chunks = [(a, b) for a in range(t) for b in range(h)]
        self.out = jax.ShapeDtypeStruct(
            (s["y"], s["c"], t, s["z"], s["x"], h) + value.shape[2:], value.dtype
        )
        self.most = max(s.values())
        sems = pltpu.SemaphoreType.DMA((len(self.chunks), 5, self.most))
        self.scratch = [sems, sems]

    def peers(self):
        me = self.place.mine()
        return [
            self.place.device(self.place.shifted(me, a, k))
            for a in "zxyc"
            for k in range(1, self.place.size[a])
        ]

    def copies(self, n, stage, receive):
        src, dst, send, recv = self.refs
        order = ORDERS[n % 2]
        axis, whole = order[stage], order[:stage]
        me = self.me
        for k in range(1, self.place.size[axis]):
            there = self.place.shifted(me, axis, k)
            here = self.place.shifted(me, axis, self.place.size[axis] - k)
            at = here if receive else me
            block = (
                src.at[self.chunks[n][0], self.chunks[n][1]]
                if stage == 0
                else region(dst, me, self.chunks[n], whole)
            )
            yield remote(
                block,
                region(dst, at, self.chunks[n], whole),
                send.at[n, stage, k],
                recv.at[n, stage, k],
                self.place.device(there),
            )

    def begin(self, refs):
        self.refs, self.me = refs, self.place.mine()

    def own(self, n):
        src, dst, send, _ = self.refs
        chunk = self.chunks[n]
        return pltpu.make_async_copy(
            src.at[chunk[0], chunk[1]], region(dst, self.me, chunk, ()), send.at[n, 4, 0]
        )

    def steps(self):
        return self.late + pl.cdiv(len(self.chunks), 2) + 4

    def step(self, time):
        for stage in GATHER_STAGES:
            for n in pair_at(time - self.late - stage, self.chunks):
                if stage == 0:
                    self.own(n).start()
                if stage == 1:
                    self.own(n).wait()
                if stage > 0:
                    for copy in self.copies(n, stage - 1, True):
                        copy.wait_recv()
                if stage < 4:
                    for copy in self.copies(n, stage, False):
                        copy.start()

    def finish(self):
        for n in range(len(self.chunks)):
            for stage in range(4):
                for copy in self.copies(n, stage, False):
                    copy.wait_send()


BACK_ORDERS = (("c", "y", "x", "z"), ("c", "x", "y", "z"))
LAYOUT = ("y", "z", "x")


class Reduce:
    def __init__(self, place, value, late=0, starts=None, kept=None):
        self.place, self.value = place, value
        s = place.size
        t, h = value.shape[2], value.shape[5]
        tail = value.shape[6:]
        self.chunks = [(a, b) for a in range(t) for b in range(h)]
        self.out = jax.ShapeDtypeStruct((t, h) + tail, jnp.float32)
        count = len(self.chunks)
        pairs = pl.cdiv(count, 2)
        self.starts = [late + k for k in range(pairs)] if starts is None else starts
        self.kept = count if kept is None else min(kept, count)
        sems = pltpu.SemaphoreType.DMA((count, 5, max(s.values())))
        full = tuple(s[a] for a in LAYOUT)
        held = pltpu.VMEM((self.kept,) + full + tail, value.dtype)
        self.scratch = [sems, sems, held, held]
        self.spots = {}
        for parity in range(min(2, count)):
            mine = (count + 1 - parity) // 2
            left = list(LAYOUT)
            for stage, axis in list(enumerate(BACK_ORDERS[parity]))[1:]:
                left.remove(axis)
                shape = (mine, max(s[axis] - 1, 1)) + tuple(s[a] for a in left) + tail
                self.spots[parity, stage] = len(self.scratch)
                self.scratch.append(pltpu.VMEM(shape, value.dtype))
        self.out_spot = len(self.scratch)
        self.scratch.append(pltpu.VMEM((t, h) + tail, jnp.float32))
        self.scratch.append(pltpu.SemaphoreType.DMA((1,)))
        self.scratch.append(pltpu.SemaphoreType.REGULAR)

    peers = Gather.peers

    def part(self, n, stage, at):
        order = BACK_ORDERS[n % 2]
        if stage == 0:
            return self.source(n, at)
        index = tuple(
            at if a == order[stage] else self.me[a] if a in order[:stage] else slice(None)
            for a in LAYOUT
        )
        return self.scr[2].at[(n % self.kept,) + index]

    def into(self, n, stage):
        if stage == 0:
            return self.scr[3].at[pl.ds(n % self.kept, 1)]
        return self.scr[self.spots[n % 2, stage]].at[n // 2]

    def copies(self, n, stage):
        axis = BACK_ORDERS[n % 2][stage]
        for k in range(1, self.place.size[axis]):
            there = self.place.shifted(self.me, axis, k)
            yield remote(
                self.part(n, stage, there[axis]),
                self.into(n, stage).at[k - 1],
                self.scr[0].at[n, stage, k],
                self.scr[1].at[n, stage, k],
                self.place.device(there),
            )

    def source(self, n, at):
        t, h = self.chunks[n]
        if t in self.apart:
            return self.apart[t].at[:, at, :, :, h]
        return self.src.at[:, at, t, :, :, h]

    def own(self, n):
        return pltpu.make_async_copy(
            self.source(n, self.me["c"]),
            self.scr[2].at[n % self.kept],
            self.scr[0].at[n, 4, 0],
        )

    def begin(self, refs, apart=()):
        self.src, self.dst, self.scr = refs[0], refs[1], refs[2:]
        self.apart = dict(apart)
        self.me = self.place.mine()

    def steps(self):
        return self.starts[-1] + 5

    def add(self, n, stage):
        order = BACK_ORDERS[n % 2]
        axis = order[stage]
        count = self.place.size[axis] - 1
        into = self.into(n, stage)
        sizes = [self.place.size[a] for a in LAYOUT if a not in order[: stage + 1]]
        if stage == 0:
            base = target = self.scr[2].at[n % self.kept]
        else:
            base = target = self.part(n, stage, self.me[axis])
        if stage == 3:
            target = self.scr[self.out_spot].at[self.chunks[n][0], self.chunks[n][1]]

        def one(flat, carry):
            index = []
            rest = flat
            for size in reversed(sizes):
                index.insert(0, lax.rem(rest, size))
                rest = lax.div(rest, size)
            index = tuple(index) + (Ellipsis,)
            if count == 1 and target.dtype == base.dtype:
                target[index] = base[index] + into[(0,) + index]
                return carry
            value = base[index].astype(jnp.float32)
            for k in range(count):
                value = value + into[(k,) + index].astype(jnp.float32)
            target[index] = value.astype(target.dtype)
            return carry

        total = math.prod(sizes)
        if total == 1:
            one(jnp.int32(0), 0)
        else:
            lax.fori_loop(0, total, one, 0)

    def step(self, time):
        for stage in REDUCE_STAGES:
            for pair, start in enumerate(self.starts):
                if start + stage == time:
                    self.advance(pair, stage)

    def advance(self, pair, stage):
        sibling = self.place.device(self.place.shifted(self.me, "c", 1))
        reused = len(self.chunks) > self.kept and self.place.size["c"] > 1
        for n in pair_at(pair, self.chunks):
            if stage == 0:
                if n >= self.kept:
                    for old in range(4):
                        for copy in self.copies(n - self.kept, old):
                            copy.wait_send()
                    if reused:
                        pl.semaphore_wait(self.scr[-1], 1)
                self.own(n).start()
            if stage == 1:
                self.own(n).wait()
            if stage > 0:
                for copy in self.copies(n, stage - 1):
                    copy.wait_recv()
                self.add(n, stage - 1)
            if stage == 1 and reused and n + self.kept < len(self.chunks):
                pl.semaphore_signal(
                    self.scr[-1],
                    inc=1,
                    device_id=sibling,
                    device_id_type=pl.DeviceIdType.MESH,
                )
            if stage < 4:
                for copy in self.copies(n, stage):
                    copy.start()

    def finish(self):
        out = pltpu.make_async_copy(self.scr[self.out_spot], self.dst, self.scr[-2].at[0])
        out.start()
        for n in range(max(0, len(self.chunks) - self.kept), len(self.chunks)):
            for stage in range(4):
                for copy in self.copies(n, stage):
                    copy.wait_send()
        out.wait()


class Total:
    def __init__(self, place, value, axes=("c", "y", "x", "z"), split=False):
        self.place, self.value, self.split = place, value, split
        self.axes = axes + ("c",) if split else axes
        self.out = jax.ShapeDtypeStruct(value.shape, value.dtype)
        self.half = value.shape[0] // 2 if split else value.shape[0]
        sizes = [self.size(a) for a in self.axes]
        sems = pltpu.SemaphoreType.DMA((len(sizes), max(sizes)))
        self.scratch = [sems, sems] + [
            pltpu.VMEM(
                (size, self.half if k else value.shape[0]) + value.shape[1:], value.dtype
            )
            for k, size in enumerate(sizes)
        ]

    peers = Gather.peers

    def size(self, axis):
        return self.place.count[axis] if axis in self.place.count else self.place.size[axis]

    def spot(self, axis):
        return lax.axis_index(axis) if axis in self.place.count else self.me[axis]

    def begin(self, refs):
        self.src, self.dst, self.send, self.recv = refs[:4]
        self.bufs = refs[4:]
        self.me = self.place.mine()

    def copies(self, stage, receive):
        axis = self.axes[stage]
        size = self.size(axis)
        buf, mine = self.bufs[stage], self.spot(axis)
        for k in range(1, size):
            there = lax.rem(mine + k, size)
            here = lax.rem(mine + size - k, size)
            if axis in self.place.count:
                device = {axis: there}
            else:
                device = self.place.device({**self.me, axis: there})
            yield remote(
                buf.at[mine],
                buf.at[here if receive else mine],
                self.send.at[stage, k],
                self.recv.at[stage, k],
                device,
            )

    def advance(self, stage):
        if stage == 0:
            value = self.src[...]
        else:
            for copy in self.copies(stage - 1, True):
                copy.wait_recv()
            for copy in self.copies(stage - 1, False):
                copy.wait_send()
            buf, size = self.bufs[stage - 1], self.size(self.axes[stage - 1])
            if self.split and stage == len(self.axes):
                for k in range(size):
                    self.dst[k * self.half : (k + 1) * self.half] = buf[k]
                return
            if self.split and stage == 1:
                rows = pl.ds(pl.multiple_of(self.me["c"] * self.half, self.half), self.half)
            else:
                rows = slice(None)
            value = buf[0, rows]
            for k in range(1, size):
                value = value + buf[k, rows]
        if stage == len(self.axes):
            self.dst[...] = value
            return
        self.bufs[stage][self.spot(self.axes[stage])] = value
        for copy in self.copies(stage, False):
            copy.start()


def norm_back(value, factor, pulled):
    centered = value - jnp.mean(value, axis=-1, keepdims=True)
    variance = jnp.mean(centered * centered, axis=-1, keepdims=True)
    scale = lax.rsqrt(variance + EPS)
    unit = centered * scale
    inner = pulled * factor
    back = scale * (
        inner
        - jnp.mean(inner, axis=-1, keepdims=True)
        - unit * jnp.mean(inner * unit, axis=-1, keepdims=True)
    )
    return (
        back,
        jnp.sum(pulled * unit, axis=0, keepdims=True),
        jnp.sum(pulled, axis=0, keepdims=True),
    )


def communicate(label, number, parts):
    count = len(parts)

    def kernel(*refs):
        ins, outs, rest = refs[:count], refs[count : 2 * count], refs[2 * count :]
        devices, seen = [], set()
        for part in parts:
            kind = part.axis if isinstance(part, Swap) else "grid"
            if kind not in seen:
                seen.add(kind)
                devices += part.peers()
        greet(devices)
        spot = 0
        for part, src, dst in zip(parts, ins, outs):
            size = len(part.scratch)
            part.begin((src, dst) + tuple(rest[spot : spot + size]))
            spot += size
        staged = parts
        for time in range(max([part.steps() for part in staged], default=0)):
            for part in staged:
                part.step(time)
        for part in parts:
            part.finish()

    return pl.pallas_call(
        kernel,
        out_shape=[part.out for part in parts],
        in_specs=[pl.BlockSpec(memory_space=pl.ANY)] * count,
        out_specs=[pl.BlockSpec(memory_space=pl.ANY)] * count,
        scratch_shapes=[s for part in parts for s in part.scratch],
        compiler_params=pltpu.CompilerParams(
            collective_id=number, has_side_effects=True, vmem_limit_bytes=58 * 1024 * 1024
        ),
        name=label,
    )(*[part.value for part in parts])


def product(left, right, dims):
    return lax.dot_general(left, right, (dims, ((), ())), preferred_element_type=jnp.float32)


NN, NT, TN = ((1,), (0,)), ((1,), (1,)), ((0,), (0,))


def spread_heads(rows, heads):
    owner = lax.broadcasted_iota(jnp.int32, rows.shape, 1)
    kept = [
        jnp.where((owner >= h * HEAD_DIM) & (owner < (h + 1) * HEAD_DIM), rows, 0)
        for h in range(heads)
    ]
    return jnp.concatenate(kept, axis=0)


def fold_heads(wide, heads):
    rows = wide.shape[0] // heads
    owner = lax.broadcasted_iota(jnp.int32, (rows, wide.shape[1]), 1)
    out = wide[:rows]
    for h in range(1, heads):
        out = jnp.where(owner >= h * HEAD_DIM, wide[h * rows : (h + 1) * rows], out)
    return out


def as_row(column):
    wide = jnp.broadcast_to(column, (column.shape[0], 128))
    return jnp.transpose(wide)[:1]


def as_column(row):
    return jnp.transpose(jnp.broadcast_to(row, (128, row.shape[1])))[:, :1]


def front_kernel(place, heads, scale, halves_w, parts, *refs):
    half, f32 = jnp.bfloat16, jnp.float32
    qkv, out_t, cot_in, latents, ffn_in, media, keep, time_rows, norms = refs[:9]
    w_o, back_o, src_o, lat_o, q_o, p_o, blend_o, mixed_o, stat_o, ffn_o = refs[9:19]
    w_vm, lat_vm, src_vm, q_vm, p_vm, blend_vm, mixed_vm, stat_vm, sems = refs[19:28]
    own_w, cot, lat_in, stat_all = refs[28:32]
    rest = list(refs[32:])
    gather_w, gather_c, lat_swap, mixed_swap, stat_swap, ffn_swap = parts
    ends = (
        (own_w, w_vm),
        (cot, back_o),
        (lat_in, lat_vm),
        (mixed_vm, mixed_o),
        (stat_vm, stat_all),
        (ffn_in, ffn_o),
    )
    for part, end in zip(parts, ends):
        size = len(part.scratch)
        part.begin(end + tuple(rest[:size]))
        rest = rest[size:]
    items, slots, width = media.shape
    lat_own = latents.shape[1]
    blocks, block = q_vm.shape[0], q_vm.shape[3]
    lat_total = blocks * lat_own
    c_count = place.size["c"]
    mp_rank = lax.axis_index("mp")
    greet(gather_w.peers() + lat_swap.peers() + ffn_swap.peers())
    clock = [0]

    def run_to(time):
        while clock[0] <= time:
            for part in (lat_swap, gather_w, gather_c, ffn_swap):
                part.step(clock[0])
            clock[0] += 1

    def arrived(t):
        return 4 + ((t + 1) * halves_w - 1) // 2

    def weight(j, t):
        return w_vm[lax.div(j, c_count), lax.rem(j, c_count), t].reshape(width, block)

    kept = []

    def keep_copy(src, dst):
        copy = pltpu.make_async_copy(src, dst, sems.at[len(kept)])
        copy.start()
        kept.append(copy)

    for n in range(items):
        lat_in[n] = layer_norm(latents[n], norms[2:3], norms[3:4]).astype(half)
    for t in range(4):
        value = qkv[t] if t < 3 else out_t[...]
        own_w[t] = value.astype(half).reshape(own_w.shape[1:])
    run_to(0)
    cot[...] = cot_in[...].astype(half)
    step_rows = math.gcd(64, slots)
    per_item = slots // step_rows

    def norm_media(k, carry):
        item, first = lax.div(k, per_item), lax.rem(k, per_item) * step_rows
        first = pl.multiple_of(first, step_rows)
        frame = lax.div(mp_rank * slots + first, PATCHES)
        value = media[item, pl.ds(first, step_rows)].astype(f32) + time_rows[pl.ds(frame, 1)]
        value = layer_norm(value, norms[0:1], norms[1:2])
        src_vm[item, pl.ds(first, step_rows)] = value.astype(half)
        return carry

    lax.fori_loop(0, items * per_item, norm_media, 0)
    src_vm[:, slots:] = lat_in[...]
    keep_copy(src_vm, src_o)
    run_to(3)
    lat_swap.finish()
    keep_copy(lat_vm, lat_o)
    run_to(arrived(0))

    def ask(j, carry):
        rows = jnp.concatenate(
            [lat_vm[:, n].reshape(lat_total, width) for n in range(items)], axis=0
        )
        query = product(rows, weight(j, 0), NN).astype(half)
        q_vm[j] = query.reshape(items, lat_total, block)
        return carry

    lax.fori_loop(0, blocks, ask, 0)
    keep_copy(q_vm, q_o)
    run_to(arrived(1))

    def score(k, carry):
        j, n = lax.div(k, items), lax.rem(k, items)
        source = src_vm[n]
        reach = product(spread_heads(q_vm[j, n], heads), weight(j, 1), NT).astype(half)
        value = product(reach, source, NT) * scale
        value = jnp.where(keep[n] > 0, value, NEGATIVE)
        peak = jnp.max(value, axis=1, keepdims=True)
        raised = jnp.exp(value - peak)
        total = jnp.sum(raised, axis=1, keepdims=True)
        low = raised.astype(half)
        p_vm[j, n] = low
        blend_vm[j, n] = product(low, source, NN).astype(half)
        stat_vm[j, n, 0:1] = as_row(peak)
        stat_vm[j, n, 1:2] = as_row(total)
        return carry

    lax.fori_loop(0, blocks * items // 2, score, 0)
    run_to(max(arrived(1) + 1, arrived(2)))
    lax.fori_loop(blocks * items // 2, blocks * items, score, 0)
    keep_copy(p_vm, p_o)
    keep_copy(blend_vm, blend_o)

    def mix(k, carry):
        j, n = lax.div(k, items), lax.rem(k, items)
        value = fold_heads(product(blend_vm[j, n], weight(j, 2), NN), heads)
        mixed_vm[:, j, n] = value.reshape(blocks, lat_own, block)
        return carry

    lax.fori_loop(0, blocks * items, mix, 0)
    mixed_swap.step(0)
    stat_swap.step(0)
    run_to(arrived(3))
    keep_copy(w_vm, w_o)
    run_to(gather_c.steps())
    for part in parts:
        if part is not lat_swap:
            part.finish()
    peaks = [stat_all[k, :, :, 0] for k in range(blocks)]
    top = functools.reduce(jnp.maximum, peaks)
    grow = [jnp.exp(peak - top) for peak in peaks]
    total = sum(stat_all[k, :, :, 1] * grow[k] for k in range(blocks))
    for k in range(blocks):
        stat_o[k] = grow[k] / total
    for copy in kept:
        copy.wait()


def front(
    place, qkv, out_t, cot, latents, ffn_pieces, media, keep, time_rows, norms, halves_w, heads, scale
):
    half, f32 = jnp.bfloat16, jnp.float32
    items, slots, width = media.shape
    lat_own = latents.shape[1]
    rows_d, block = out_t.shape
    blocks = place.count["mp"]
    own_weights = jax.ShapeDtypeStruct((4, halves_w, rows_d // halves_w, block), half)
    low_cot = jax.ShapeDtypeStruct(cot.shape, half)
    latent_norm = jax.ShapeDtypeStruct(latents.shape, half)
    lat, keys = blocks * lat_own, slots + lat_own
    rows = heads * lat
    late = 2 * halves_w
    mixed = jax.ShapeDtypeStruct((blocks, blocks, items, lat_own, block), f32)
    stats = jax.ShapeDtypeStruct((blocks, items, 2, rows), f32)
    parts = [
        Gather(place, own_weights),
        Gather(place, low_cot, late),
        Swap(place, "mp", False, latent_norm),
        Swap(place, "mp", True, mixed),
        Swap(place, "mp", False, stats),
        Swap(place, "dp", True, ffn_pieces, SWAP_AT),
    ]
    shapes = [
        parts[0].out,
        parts[2].out,
        jax.ShapeDtypeStruct((items, keys, width), half),
        jax.ShapeDtypeStruct((blocks, items, lat, block), half),
        jax.ShapeDtypeStruct((blocks, items, rows, keys), half),
        jax.ShapeDtypeStruct((blocks, items, rows, width), half),
        mixed,
        stats,
    ]
    scratch = [pltpu.VMEM(shape.shape, shape.dtype) for shape in shapes]
    scratch.append(pltpu.SemaphoreType.DMA((8,)))
    scratch += [pltpu.VMEM(v.shape, half) for v in (own_weights, low_cot, latent_norm)]
    scratch.append(pltpu.VMEM(parts[4].out.shape, f32))
    for part in parts:
        scratch += part.scratch
    whole = pl.BlockSpec(memory_space=pltpu.VMEM)
    hbm = pl.BlockSpec(memory_space=pl.ANY)
    return pl.pallas_call(
        functools.partial(front_kernel, place, heads, scale, halves_w, parts),
        in_specs=[whole] * 4 + [hbm] + [whole] * 4,
        out_specs=[hbm] * 8 + [whole, hbm],
        out_shape=[
            parts[0].out,
            parts[1].out,
            shapes[2],
            parts[2].out,
            shapes[3],
            shapes[4],
            shapes[5],
            parts[3].out,
            jax.ShapeDtypeStruct((blocks, blocks, items, rows), f32),
            parts[5].out,
        ],
        scratch_shapes=scratch,
        compiler_params=pltpu.CompilerParams(
            collective_id=1, has_side_effects=True, vmem_limit_bytes=64 * 1024 * 1024 - 65536
        ),
        name="front",
    )(qkv, out_t, cot, latents, ffn_pieces, media, keep, time_rows, norms)


def out_grad_shape(place, width, halves_w, block):
    s = place.size
    return (s["y"], s["c"], s["z"], s["x"], halves_w, width // (s["z"] * s["x"] * halves_w), block)


def feed_kernel(place, parts, *refs):
    half, f32 = jnp.bfloat16, jnp.float32
    own_rows, pieces, back_rows, after_attn, cot, mixed, norms, weights = refs[:8]
    (norm_o, ffn_o, back_o, term_o, grad_o, give_o, after_o, low_o, sums_o, lat_o) = refs[8:18]
    (rows_vm, up_vm, down_vm, share_a, share_b, w_out) = refs[18:24]
    (hid_vm, pre_vm, mixed_vm, term_vm, grad_vm, sem) = refs[24:30]
    rest = list(refs[30:])
    gather, first, second, back_swap, term_swap = parts
    ends = (
        (own_rows, rows_vm),
        (share_a, norm_o),
        (share_b, ffn_o),
        (mixed_vm, back_o),
        (term_vm, term_o),
    )
    for part, end in zip(parts, ends):
        size = len(part.scratch)
        part.begin(end + tuple(rest[:size]))
        rest = rest[size:]
    c_count, blocks = place.size["c"], place.count["mp"]
    width, units = norms.shape[1], hid_vm.shape[2]
    greet(gather.peers() + back_swap.peers())
    out_weight = pltpu.make_async_copy(weights.at[:, 3], w_out, sem.at[0])
    gather.step(0)
    out_weight.start()
    up_vm[...] = pieces[:, :, :units].reshape(width, units)
    down_vm[...] = pieces[:, :, units:].reshape(width, units)
    for time in range(1, gather.steps()):
        gather.step(time)

    def inner(m, carry):
        y, c = lax.div(m, c_count), lax.rem(m, c_count)
        w_up, w_down = up_vm[...], down_vm[...]
        rows = rows_vm[y, c].reshape(-1, width)
        pre = product(rows, w_up, NN)
        pulled = product(back_rows[y, c].reshape(-1, width), w_down, NN)
        chance = 0.5 * (1.0 + lax.erf(pre * math.sqrt(0.5)))
        slope = chance + pre * jnp.exp(-0.5 * pre * pre) * math.sqrt(0.5 / math.pi)
        hid_vm[m] = (pre * chance).astype(half)
        pre_back = (pulled * slope).astype(half)
        pre_vm[m] = pre_back
        share = product(pre_back, w_up, NT).astype(half)
        share_a[y, c] = share.reshape(share_a.shape[2:])
        return carry

    lax.fori_loop(0, blocks, inner, 0)
    first.step(0)

    def outer(m, carry):
        y, c = lax.div(m, c_count), lax.rem(m, c_count)
        share = product(hid_vm[m], down_vm[...], NT).astype(half)
        share_b[y, c] = share.reshape(share_b.shape[2:])
        return carry

    lax.fori_loop(0, blocks, outer, 0)
    first.step(1)
    second.step(0)
    give = product(rows_vm[...].reshape(-1, width), pre_vm[...].reshape(-1, units), TN)
    half_shape = give_o.shape[:2] + (units,)
    give_o[:, :, :units] = give.astype(half).reshape(half_shape)
    give = product(back_rows[...].reshape(-1, width), hid_vm[...].reshape(-1, units), TN)
    give_o[:, :, units:] = give.astype(half).reshape(half_shape)
    first.step(2)
    second.step(1)
    first.step(3)
    second.step(2)
    first.step(4)
    pulled = first.scr[first.out_spot]
    factors = jnp.zeros((1, width), f32)
    offsets = jnp.zeros((1, width), f32)
    for t in range(after_attn.shape[0]):
        value, factor, offset = norm_back(after_attn[t], norms[4:5], pulled[t, 0])
        value = cot[t] + value
        after_o[t] = value
        low_o[t] = value.astype(half)
        factors += factor
        offsets += offset
    sums_o[0:1] = factors
    sums_o[1:2] = offsets
    out_weight.wait()
    low = low_o[...].reshape(-1, width)
    heads = term_vm.shape[0] // blocks
    for j in range(blocks):
        back = product(low, w_out[j].reshape(width, -1), NN).astype(half)
        mixed_vm[j] = back
        both = mixed[j] * back.astype(f32)
        owner = lax.broadcasted_iota(jnp.int32, both.shape, 1)
        for h in range(heads):
            mine = (owner >= h * HEAD_DIM) & (owner < (h + 1) * HEAD_DIM)
            term = jnp.sum(jnp.where(mine, both, 0.0), axis=1, keepdims=True)
            term_vm[j * heads + h : j * heads + h + 1] = as_row(term)
    back_swap.step(0)
    term_swap.step(0)
    second.step(3)
    for j in range(blocks):
        grad = product(low, mixed[j].astype(half), TN).astype(half)
        grad_vm[j // c_count, j % c_count] = grad.reshape(grad_vm.shape[2:])
    grad_copy = pltpu.make_async_copy(grad_vm, grad_o, sem.at[1])
    grad_copy.start()
    second.step(4)
    for t in range(after_attn.shape[0]):
        lat_o[t] = after_attn[t] + second.scr[second.out_spot][t, 0]
    for part in parts:
        part.finish()
    grad_copy.wait()


def feed(
    place, own_rows, pieces, back_rows, after_attn, cot, mixed, norms, weights, halves_w
):
    half, f32 = jnp.bfloat16, jnp.float32
    gather = Gather(place, own_rows)
    rows = gather.out
    width = norms.shape[1]
    blocks, flat, block = mixed.shape
    heads = block // HEAD_DIM
    units = pieces.shape[2] // 2
    per = math.prod(rows.shape[2:7])
    mixed_back = jax.ShapeDtypeStruct(mixed.shape, half)
    terms = jax.ShapeDtypeStruct((blocks * heads, flat), f32)
    grad = jax.ShapeDtypeStruct(out_grad_shape(place, width, halves_w, block), half)
    parts = [
        gather,
        Reduce(place, rows),
        Reduce(place, rows),
        Swap(place, "mp", False, mixed_back),
        Swap(place, "mp", False, terms),
    ]
    scratch = [
        pltpu.VMEM(rows.shape, half),
        pltpu.VMEM((width, units), half),
        pltpu.VMEM((width, units), half),
        pltpu.VMEM(rows.shape, half),
        pltpu.VMEM(rows.shape, half),
        pltpu.VMEM(weights.shape[:1] + weights.shape[2:], half),
        pltpu.VMEM((blocks, per, units), half),
        pltpu.VMEM((blocks, per, units), half),
        pltpu.VMEM(mixed.shape, half),
        pltpu.VMEM(terms.shape, f32),
        pltpu.VMEM(grad.shape, half),
        pltpu.SemaphoreType.DMA((2,)),
    ]
    for part in parts:
        scratch += part.scratch
    whole = pl.BlockSpec(memory_space=pltpu.VMEM)
    hbm = pl.BlockSpec(memory_space=pl.ANY)
    return pl.pallas_call(
        functools.partial(feed_kernel, place, parts),
        in_specs=[hbm] + [whole] * 6 + [hbm],
        out_specs=[hbm] * 5 + [whole] * 5,
        out_shape=[part.out for part in parts[1:]]
        + [
            grad,
            jax.ShapeDtypeStruct(pieces.shape, half),
            jax.ShapeDtypeStruct(after_attn.shape, f32),
            jax.ShapeDtypeStruct(after_attn.shape, half),
            jax.ShapeDtypeStruct((2, width), f32),
            jax.ShapeDtypeStruct(after_attn.shape, f32),
        ],
        scratch_shapes=scratch,
        compiler_params=pltpu.CompilerParams(
            collective_id=3, has_side_effects=True, vmem_limit_bytes=60 * 1024 * 1024
        ),
        name="feed",
    )(own_rows, pieces, back_rows, after_attn, cot, mixed, norms, weights)


def feed_apart(
    place, own_rows, pieces, back_rows, after_attn, cot, mixed, norms, weights, halves_w
):
    half, f32 = jnp.bfloat16, jnp.float32
    width, units = norms.shape[1], pieces.shape[2] // 2
    dot = functools.partial(jnp.einsum, preferred_element_type=f32)
    (ffn_rows,) = communicate("rows", 3, [Gather(place, own_rows)])
    shape, half_shape = ffn_rows.shape, pieces.shape[:2] + (units,)
    w_up, w_down = (
        part.reshape(width, units) for part in (pieces[:, :, :units], pieces[:, :, units:])
    )
    ffn_rows, back_rows = ffn_rows.reshape(-1, width), back_rows.reshape(-1, width)
    pre_act = dot("rd,df->rf", ffn_rows, w_up)
    hidden = exact_gelu(pre_act).astype(half)
    hidden_back = dot("rd,df->rf", back_rows, w_down)
    pre_back = jax.vjp(exact_gelu, pre_act)[1](hidden_back)[0].astype(half)
    norm_part = dot("rf,df->rd", pre_back, w_up).astype(half)
    ffn_part = dot("rf,df->rd", hidden, w_down).astype(half)
    down_part = dot("rd,rf->df", back_rows, hidden).astype(half)
    up_part = dot("rd,rf->df", ffn_rows, pre_back).astype(half)
    norm_pulled, ffn_out = communicate(
        "ffn",
        4,
        [Reduce(place, norm_part.reshape(shape)), Reduce(place, ffn_part.reshape(shape))],
    )
    pull = jax.vjp(layer_norm, after_attn, norms[4], norms[5])[1]
    through, factor, offset = pull(norm_pulled.reshape(after_attn.shape))
    after_back = cot + through
    low = after_back.astype(half)
    mixed_back = dot("ld,jde->jle", low.reshape(-1, width), weights[:, 3]).astype(half)
    terms = jnp.sum(
        (mixed * mixed_back.astype(f32)).reshape(*mixed.shape[:2], -1, HEAD_DIM), axis=-1
    )
    terms = terms.transpose(0, 2, 1).reshape(-1, mixed.shape[1])
    mixed_rows, terms = communicate(
        "back", 5, [Swap(place, "mp", False, mixed_back), Swap(place, "mp", False, terms)]
    )
    sums = jnp.stack([factor, offset])
    grad = dot("ld,jle->jde", low.reshape(-1, width), mixed.astype(half)).astype(half)
    return (
        norm_pulled,
        ffn_out,
        mixed_rows,
        terms,
        grad.reshape(out_grad_shape(place, width, halves_w, mixed.shape[2])),
        jnp.concatenate([up_part.reshape(half_shape), down_part.reshape(half_shape)], axis=2),
        after_back,
        low,
        sums,
        after_attn + ffn_out.reshape(after_attn.shape),
    )


def attend_back_kernel(place, heads, scale, reduce, swap, latent_swap, totals, *refs):
    half, f32 = jnp.bfloat16, jnp.float32
    (src, lat, q, p, blend, back, out_part, row, wq, wk, wv, give) = refs[:12]
    (media, time_rows, norms, latents, after_back, ffn_sums) = refs[12:18]
    (grad_o, media_o, owned_o, ffn_o, latents_o, small_o, square_o) = refs[18:25]
    (acc, lat_acc, lat_vm, kept, stage_a, stage_b, small, square, ffn_vm, joined, stage_sem) = refs[
        25:36
    ]
    rest = list(refs[36:])
    phase, block = pl.program_id(0), pl.program_id(1)
    blocks = pl.num_programs(1)
    items = src.shape[0]
    lat_total = lat.shape[1]
    width = src.shape[2]
    for part, give, out in (
        (reduce, grad_o, owned_o),
        (swap, give, ffn_vm),
        (latent_swap, lat_acc, lat_vm),
        (totals[0], small, small_o),
        (totals[1], square, square_o),
    ):
        size = len(part.scratch)
        if part is reduce:
            part.begin((give, out) + tuple(rest[:size]), {3: out_part})
        else:
            part.begin((give, out) + tuple(rest[:size]))
        rest = rest[size:]

    def at(number, index, action):
        pl.when((phase == number) & (block == index))(action)

    last = place.count["mp"] - 1
    plan, moves_1, moves_2 = reduce_plan(len(reduce.chunks), place.count["mp"], items)
    c_count = place.size["c"]
    y_of, c_of = lax.div(block, c_count), lax.rem(block, c_count)

    def staged(t, buffer, number):
        return pltpu.make_async_copy(buffer, grad_o.at[y_of, c_of, t], stage_sem.at[number])

    def hand_over(*shares):
        @pl.when(block > 0)
        def _():
            for k, (t, _) in enumerate(shares):
                staged(t, (stage_a, stage_b)[k], k).wait()

        for k, (t, value) in enumerate(shares):
            buffer = (stage_a, stage_b)[k]
            buffer[...] = value.astype(half).reshape(buffer.shape)
            staged(t, buffer, k).start()

        @pl.when(block == last)
        def _():
            for k, (t, _) in enumerate(shares):
                staged(t, (stage_a, stage_b)[k], k).wait()

    def of_item(ref, item):
        return ref[:, 0, item].reshape(lat_total, ref.shape[4])

    def column(item, which):
        return as_column(row[0, item, which : which + 1])

    def events(number, half_step):
        for (where, point), moves in plan.items():
            if where == number and point % items == half_step:

                def carry_out(moves=moves):
                    for move in moves:
                        reduce.advance(*move)

                at(where, point // items, carry_out)

    def start():
        greet(swap.peers() + latent_swap.peers() + reduce.peers())
        if len(reduce.chunks) == 8:
            reduce.advance(0, 0)
        swap.step(0)

    at(0, 0, start)

    @pl.when(phase == 0)
    def _():
        back_s = jnp.concatenate(
            [
                (spread_heads(of_item(back, n), heads) * column(n, 0)).astype(half)
                for n in range(items)
            ],
            axis=0,
        )
        value_grad = product(blend[0].reshape(back_s.shape[0], width), back_s, TN)
        hand_over((2, value_grad))

    events(0, items - 1)

    @pl.when(phase == 1)
    def _():
        turns = []
        queries = jnp.concatenate([spread_heads(q[0, n], heads) for n in range(items)], axis=0)
        back_s = jnp.concatenate([spread_heads(of_item(back, n), heads) for n in range(items)], axis=0)
        pulls = product(back_s, wv[0, 0], NT).astype(half)
        rows = pulls.shape[0] // items
        for n in range(items):
            prob_back = product(pulls[n * rows : (n + 1) * rows], src[n], NT)
            score_back = (
                p[0, n].astype(jnp.float32) * (column(n, 0) * scale) * (prob_back - column(n, 1))
            ).astype(half)
            kept[block, n] = score_back
            turns.append(product(score_back, src[n], NN).astype(half))
            if n + 1 < items:
                events(1, n)
        turns = jnp.concatenate(turns, axis=0)
        key_turns = product(turns, wk[0, 0], NN)
        query_backs = jnp.concatenate(
            [fold_heads(key_turns[n * rows : (n + 1) * rows], heads) for n in range(items)], axis=0
        ).astype(half)
        latent_back = product(query_backs, wq[0, 0], NT)
        latent_back = latent_back.reshape(items, lat_acc.shape[0], -1, width)

        @pl.when(block == 0)
        def _():
            for n in range(items):
                lat_acc[:, n] = latent_back[n]

        @pl.when(block > 0)
        def _():
            for n in range(items):
                lat_acc[:, n] += latent_back[n]

        key_grad = product(turns, queries, TN)
        query_grad = product(lat[...].reshape(items * lat_total, width), query_backs, TN)
        hand_over((1, key_grad), (0, query_grad))

    events(1, items - 1)
    at(1, last, lambda: latent_swap.step(0))

    @pl.when(phase == 2)
    def _():
        queries = jnp.concatenate([spread_heads(q[0, n], heads) for n in range(items)], axis=0)
        back_s = jnp.concatenate([spread_heads(of_item(back, n), heads) for n in range(items)], axis=0)
        pulls = product(back_s, wv[0, 0], NT)
        reach = product(queries, wk[0, 0], NT).astype(half)
        rows = pulls.shape[0] // items
        for n in range(items):
            mine = slice(n * rows, (n + 1) * rows)
            value = product(
                jnp.concatenate([kept[block, n], p[0, n]], axis=0),
                jnp.concatenate([reach[mine], (pulls[mine] * column(n, 0)).astype(half)], axis=0),
                TN,
            )

            @pl.when(block == 0)
            def _():
                acc[n] = value

            @pl.when(block > 0)
            def _():
                acc[n] += value

            if n + 1 < items:
                events(2, n)

    events(2, items - 1)

    slots = media.shape[1]
    step_rows = math.gcd(64, slots)
    per_item = slots // step_rows
    mp_rank = lax.axis_index("mp")

    def media_back(k, carry):
        item, first = lax.div(k, per_item), lax.rem(k, per_item) * step_rows
        first = pl.multiple_of(first, step_rows)
        frame = lax.div(mp_rank * slots + first, PATCHES)
        value = media[item, pl.ds(first, step_rows)].astype(f32) + time_rows[pl.ds(frame, 1)]
        back, factor, offset = norm_back(
            value, norms[0:1], acc[item, pl.ds(first, step_rows)]
        )
        acc[item, pl.ds(first, step_rows)] = back
        small[0:1] += factor
        small[1:2] += offset
        small[pl.ds(6 + frame, 1)] += jnp.sum(back, axis=0, keepdims=True)
        return carry

    def end():
        small[...] = jnp.zeros_like(small)
        half_way = items * per_item // 2
        lax.fori_loop(0, half_way, media_back, 0)
        for move in moves_1:
            reduce.advance(*move)
        lax.fori_loop(half_way, items * per_item, media_back, 0)
        out = pltpu.make_async_copy(acc.at[:, pl.ds(0, slots)], media_o, stage_sem.at[0])
        out.start()
        latent_swap.finish()
        for n in range(items):
            pulled = acc[n, slots:]
            for k in range(lat_vm.shape[0]):
                pulled = pulled + lat_vm[k, n]
            value, factor, offset = norm_back(latents[n], norms[2:3], pulled)
            latents_o[n] = after_back[n] + value
            small[2:3] += factor
            small[3:4] += offset
        small[4:6] = ffn_sums[...]
        totals[0].advance(0)
        totals[0].advance(1)
        reduce.advance(*moves_2[0])
        totals[0].advance(2)
        for move in moves_2[1:-1]:
            reduce.advance(*move)
        totals[0].advance(3)
        swap.finish()
        units = ffn_vm.shape[2] // 2
        sums = jnp.zeros((1, 1), f32)
        for k in range(ffn_vm.shape[0]):
            piece = ffn_vm[k]
            joined[0, :, k * units : (k + 1) * units] = piece[:, :units]
            joined[1, :, k * units : (k + 1) * units] = piece[:, units:]
            value = piece.astype(f32)
            sums = sums + jnp.sum(value * value, keepdims=True)
        ffn_out = pltpu.make_async_copy(joined, ffn_o, stage_sem.at[1])
        ffn_out.start()
        totals[0].advance(4)
        reduce.advance(*moves_2[-1])
        if totals[0].split:
            totals[0].advance(5)
        owned = reduce.scr[reduce.out_spot]
        for t in range(owned.shape[0]):
            for h in range(owned.shape[1]):
                value = owned[t, h]
                sums = sums + jnp.sum(value * value, keepdims=True)
        square[...] = jnp.broadcast_to(sums, square.shape)
        totals[1].advance(0)
        reduce.finish()
        for stage in range(1, 3):
            totals[1].advance(stage)
        ffn_out.wait()
        out.wait()

    at(2, last, end)


def attend_back(
    place,
    source,
    latent_rows,
    query,
    chance,
    blend,
    back,
    out_part,
    rows_in,
    weights,
    give,
    rows_end,
    weight_halves,
    heads,
    scale,
):
    items, keys, width = source.shape
    lat = latent_rows.shape[1]
    own = back.shape[3]
    blocks, block = weights.shape[0], weights.shape[3]
    rows = heads * lat
    half, f32 = jnp.bfloat16, jnp.float32
    s = place.size
    part = width // (s["z"] * s["x"] * weight_halves)
    inner = (s["z"], s["x"], weight_halves, part, block)
    grad = jax.ShapeDtypeStruct((s["y"], s["c"], 4) + inner, half)
    lat_shares = jax.ShapeDtypeStruct((blocks, items, own, width), f32)
    order = [3, 2, 1, 0]
    reduce = Reduce(place, grad, kept=6 if weight_halves == 2 else 2)
    reduce.chunks = [(t, h) for t in order for h in range(weight_halves)]
    latent_swap = Swap(place, "mp", True, lat_shares)
    swap = Swap(place, "dp", True, give)
    joined = jax.ShapeDtypeStruct((2, give.shape[1], give.shape[0] * give.shape[2] // 2), half)
    small = jax.ShapeDtypeStruct((16, width), f32)
    square = jax.ShapeDtypeStruct((8, 128), f32)
    totals = [
        Total(place, small, split=s["c"] == 2),
        Total(place, square, axes=("mp", "dp")),
    ]
    slots = keys - own

    def weight(t, first):
        return pl.BlockSpec(
            (1, 1, width, block), lambda ph, j: (j * jnp.minimum(ph // first, 1), t, 0, 0)
        )

    def per(*shape):
        return pl.BlockSpec((1, items) + shape, lambda ph, j: (j,) + (0,) * (1 + len(shape)))

    def early(*shape):
        return pl.BlockSpec(
            (1, items) + shape,
            lambda ph, j: (j + (blocks - 1 - j) * jnp.minimum(ph, 1),) + (0,) * (1 + len(shape)),
        )

    def late(*shape):
        return pl.BlockSpec(
            (1, items) + shape,
            lambda ph, j: (j * jnp.minimum(ph, 1),) + (0,) * (1 + len(shape)),
        )

    whole = pl.BlockSpec(memory_space=pltpu.VMEM)
    hbm = pl.BlockSpec(memory_space=pl.ANY)
    scratch = [
        pltpu.VMEM((items, keys, width), f32),
        pltpu.VMEM(lat_shares.shape, f32),
        pltpu.VMEM(lat_shares.shape, f32),
        pltpu.VMEM((blocks, items, rows, keys), half),
        pltpu.VMEM(inner, half),
        pltpu.VMEM(inner, half),
        pltpu.VMEM(small.shape, f32),
        pltpu.VMEM(square.shape, f32),
        pltpu.VMEM(give.shape, half),
        pltpu.VMEM(joined.shape, half),
        pltpu.SemaphoreType.DMA((2,)),
    ]
    for member in [reduce, swap, latent_swap] + totals:
        scratch += member.scratch
    return pl.pallas_call(
        functools.partial(
            attend_back_kernel, place, heads, scale, reduce, swap, latent_swap, totals
        ),
        grid=(3, blocks),
        in_specs=[
            whole,
            whole,
            late(lat, block),
            late(rows, keys),
            early(rows, width),
            pl.BlockSpec(
                (blocks, 1, items, own, block), lambda ph, j: (0, j, 0, 0, 0)
            ),
            hbm,
            per(2, rows),
            weight(0, 1),
            weight(1, 1),
            weight(2, 1),
            hbm,
        ]
        + [whole] * 6,
        out_specs=[hbm] * 4 + [whole] * 3,
        out_shape=[
            grad,
            jax.ShapeDtypeStruct((items, slots, width), f32),
            reduce.out,
            joined,
            jax.ShapeDtypeStruct((items, own, width), f32),
            small,
            square,
        ],
        scratch_shapes=scratch,
        compiler_params=pltpu.CompilerParams(
            collective_id=6, has_side_effects=True, vmem_limit_bytes=64 * 1024 * 1024 - 65536
        ),
        name="attend_back",
    )(
        source,
        latent_rows,
        query,
        chance,
        blend,
        back,
        out_part,
        rows_in,
        weights,
        weights,
        weights,
        give,
        *rows_end,
    )


def reduce_plan(chunks, blocks, items):
    points = blocks * items
    if chunks == 8:
        eighths = {
            (0, 1): [(0, 1)],
            (0, 7): [(1, 0)],
            (1, 2): [(0, 2), (1, 1)],
            (1, 5): [(0, 3), (1, 2)],
            (1, 7): [(2, 0)],
            (2, 0): [(2, 1), (0, 4), (3, 0)],
            (2, 3): [(1, 3)],
            (2, 4): [(3, 1)],
            (2, 6): [(2, 2)],
        }
        ends = ((1, 4), (3, 2), (2, 3)), ((3, 3), (2, 4), (3, 4))
    else:
        eighths = {
            (0, 7): [(0, 0)],
            (1, 1): [(0, 1)],
            (1, 3): [(0, 2)],
            (1, 6): [(0, 3)],
            (1, 7): [(0, 4), (1, 0)],
            (2, 0): [(1, 1)],
        }
        ends = ((1, 2),), ((1, 3), (1, 4))
    plan = {
        (phase, (eighth + 1) * points // 8 - 1): moves for (phase, eighth), moves in eighths.items()
    }
    return plan, *ends


def refresh_kernel(*refs):
    f32 = jnp.float32
    square, small, owned, ffn, media_in = refs[:5]
    groups = [refs[5 + 3 * n : 8 + 3 * n] for n in range(6)]
    norm_o, media_o = refs[23:25]
    outs = [refs[25 + 5 * n : 30 + 5 * n] for n in range(4)]
    outs += [refs[45 + 4 * n : 49 + 4 * n] for n in range(2)]
    media_come = pltpu.make_async_copy(media_in, refs[53], refs[54].at[0])
    media_come.start()
    total = square[0:1, 0:1] + jnp.sum(small[...] * small[...], keepdims=True)
    norm = jnp.sqrt(total)
    norm_o[...] = norm
    clip = 1.0 / jnp.maximum(norm, 1.0)

    def update(number, at, gradient):
        master, momentum, average = groups[number]
        done = advance(
            gradient.astype(f32),
            master[at],
            momentum[at],
            average[at],
            clip,
            STEP_RATES[number],
        )
        for ref, value in zip(outs[number], done):
            ref[at] = value
        if number < 4:
            outs[number][4][at] = done[1].astype(jnp.bfloat16)

    parts, rows = owned.shape[1:3]
    for h in range(parts):
        for t in range(3):
            update(0, (t, pl.ds(h * rows, rows)), owned[t, h])
        update(1, pl.ds(h * rows, rows), owned[3, h])
    media_come.wait()
    media_go = pltpu.make_async_copy(refs[53], media_o, refs[54].at[1])
    media_go.start()
    step = math.gcd(ffn.shape[1], 16)

    def one(k, carry):
        at = pl.ds(pl.multiple_of(k * step, step), step)
        for n in range(2):
            update(2 + n, at, ffn[n, at])
        return carry

    lax.fori_loop(0, ffn.shape[1] // step, one, 0)
    update(4, Ellipsis, small[0:6])
    update(5, Ellipsis, small[6 : 6 + FRAMES])
    media_go.wait()


def refresh(square, small, owned, ffn, media_grad, groups):
    f32 = jnp.float32
    whole = pl.BlockSpec(memory_space=pltpu.VMEM)
    hbm = pl.BlockSpec(memory_space=pl.ANY)
    shapes = [
        jax.ShapeDtypeStruct((1, 1), f32),
        jax.ShapeDtypeStruct(media_grad.shape, f32),
    ]
    for n, group in enumerate(groups):
        shapes += [jax.ShapeDtypeStruct(group[0].shape, f32)] * 4
        if n < 4:
            shapes.append(jax.ShapeDtypeStruct(group[0].shape, jnp.bfloat16))
    arrays = [array for group in groups for array in group]
    return pl.pallas_call(
        refresh_kernel,
        in_specs=[whole] * 4 + [hbm] + [whole] * len(arrays),
        out_specs=[whole, hbm] + [whole] * (len(shapes) - 2),
        out_shape=shapes,
        scratch_shapes=[
            pltpu.VMEM(media_grad.shape, f32),
            pltpu.SemaphoreType.DMA((2,)),
        ],
        compiler_params=pltpu.CompilerParams(vmem_limit_bytes=60 * 1024 * 1024),
        name="refresh",
    )(square, small, owned, ffn, media_grad, *arrays)


def halves(rows):
    return 2 if rows % 32 == 0 else 1


def shards(
    latents,
    media,
    frames,
    cotangent,
    qkv_master,
    qkv_momentum,
    qkv_average,
    out_master,
    out_momentum,
    out_average,
    up_master,
    up_momentum,
    up_average,
    down_master,
    down_momentum,
    down_average,
    norm_params,
    norm_momentum,
    norm_average,
    time_table,
    time_momentum,
    time_average,
):
    f32 = jnp.float32
    half = jnp.bfloat16
    mp_rank = lax.axis_index("mp")
    mp_count = lax.axis_size("mp")
    dp_count = lax.axis_size("dp")
    place = Place(dp_count, mp_count)
    items, lat_own, width = latents.shape
    lat_total = lat_own * mp_count
    slots = media.shape[1]
    block = qkv_master.shape[2]
    rows_d = qkv_master.shape[1]
    heads = block // HEAD_DIM
    hidden_block = up_master.shape[1]
    units = hidden_block // dp_count
    own_rows = items * lat_own
    all_rows = dp_count * mp_count * own_rows
    scale_factor = HEAD_DIM ** (-0.5)
    dot = functools.partial(jnp.einsum, preferred_element_type=f32)

    def as_chunks(rows):
        t = halves(own_rows)
        return rows.reshape(t, 1, own_rows // t, width)

    weight_halves = halves(rows_d)
    ffn_pieces = jnp.concatenate(
        [wide.reshape(rows_d, dp_count, units) for wide in (up_master, down_master.T)], axis=2
    )
    ffn_pieces = ffn_pieces.transpose(1, 0, 2).astype(half)
    slot_ids = mp_rank * slots + jnp.arange(slots)
    frame_ids = slot_ids // PATCHES
    keep = jnp.concatenate(
        [frame_ids[None, :] < frames[:, None], jnp.ones((items, lat_own), jnp.bool_)], axis=1
    )
    (
        weights,
        back_rows,
        source,
        latent_rows,
        queries,
        chances,
        blends,
        mixed_blocks,
        shares,
        ffn_pieces,
    ) = front(
        place,
        qkv_master,
        out_master.T,
        as_chunks(cotangent),
        latents,
        ffn_pieces,
        media,
        keep.astype(f32)[:, None],
        time_table,
        norm_params,
        weight_halves,
        heads,
        scale_factor,
    )
    weights = weights.reshape(mp_count, 4, width, block)
    w_out = weights[:, 3]
    latent_rows = latent_rows.transpose(1, 0, 2, 3).reshape(items, lat_total, width)
    share = lax.dynamic_index_in_dim(shares, mp_rank, 0, keepdims=False)
    own_shares = lax.dynamic_slice_in_dim(
        shares.reshape(mp_count, mp_count, items, heads, lat_total), mp_rank * lat_own, lat_own, 4
    )
    own_shares = jnp.repeat(own_shares.transpose(0, 1, 2, 4, 3), HEAD_DIM, axis=-1)
    mixed_full = jnp.sum(mixed_blocks * own_shares, axis=0)
    mixed_j = mixed_full.astype(half)
    after_attn = latents + dot("jile,jde->ild", mixed_j, w_out)
    ffn_norm = layer_norm(after_attn, norm_params[4], norm_params[5]).astype(half)
    t = halves(own_rows)
    by_chunk = (t, own_rows // t, width)
    (
        _,
        _,
        mixed_back_rows,
        row_terms,
        out_part,
        give,
        after_back,
        attn_low,
        ffn_sums,
        latents_out,
    ) = (feed if 2 * all_rows * width <= ROWS_IN_VMEM else feed_apart)(
        place,
        as_chunks(ffn_norm),
        ffn_pieces,
        back_rows,
        after_attn.reshape(by_chunk),
        cotangent.reshape(by_chunk),
        mixed_full.reshape(mp_count, own_rows, block),
        norm_params,
        weights,
        weight_halves,
    )
    latents_out, after_back = latents_out.reshape(latents.shape), after_back.reshape(latents.shape)
    row_terms = row_terms.reshape(mp_count, mp_count, heads, items, lat_own)
    row_terms = row_terms.transpose(1, 3, 2, 0, 4).reshape(mp_count, items, heads * lat_total)
    back_j = mixed_back_rows.reshape(mp_count, mp_count, items, lat_own, block)
    _, media_grad, owned, ffn_owned, latents_grad, small, square = attend_back(
        place,
        source,
        latent_rows,
        queries,
        chances,
        blends,
        back_j,
        out_part,
        jnp.stack([share, row_terms], axis=2),
        weights,
        give,
        [media, time_table, norm_params, latents, after_back, ffn_sums],
        weight_halves,
        heads,
        scale_factor,
    )
    groups = [
        (qkv_master, qkv_momentum, qkv_average),
        (out_master.T, out_momentum.T, out_average.T),
        (up_master, up_momentum, up_average),
        (down_master.T, down_momentum.T, down_average.T),
        (norm_params, norm_momentum, norm_average),
        (time_table, time_momentum, time_average),
    ]
    (
        grad_norm,
        media_grad,
        qkv_grad,
        qkv_new,
        qkv_momentum_new,
        qkv_average_new,
        qkv_copy,
        out_grad,
        out_new,
        out_momentum_new,
        out_average_new,
        out_copy,
        up_grad,
        up_new,
        up_momentum_new,
        up_average_new,
        up_copy,
        down_grad,
        down_new,
        down_momentum_new,
        down_average_new,
        down_copy,
        norm_grad,
        norm_new,
        norm_momentum_new,
        norm_average_new,
        time_grad,
        time_new,
        time_momentum_new,
        time_average_new,
    ) = refresh(square, small, owned, ffn_owned, media_grad, groups)
    grad_norm = grad_norm.reshape(())
    out_grad, out_new, out_momentum_new, out_average_new, out_copy = (
        value.T for value in (out_grad, out_new, out_momentum_new, out_average_new, out_copy)
    )
    down_grad, down_new, down_momentum_new, down_average_new, down_copy = (
        value.T for value in (down_grad, down_new, down_momentum_new, down_average_new, down_copy)
    )
    return (
        latents_out,
        latents_grad,
        media_grad,
        grad_norm,
        qkv_grad,
        qkv_new,
        qkv_momentum_new,
        qkv_average_new,
        out_grad,
        out_new,
        out_momentum_new,
        out_average_new,
        up_grad,
        up_new,
        up_momentum_new,
        up_average_new,
        down_grad,
        down_new,
        down_momentum_new,
        down_average_new,
        norm_grad,
        norm_new,
        norm_momentum_new,
        norm_average_new,
        time_grad,
        time_new,
        time_momentum_new,
        time_average_new,
        qkv_copy,
        out_copy,
        up_copy,
        down_copy,
    )


def solution(mesh):
    placed = (
        P("dp", "mp", None),
        P("dp", "mp", None),
        P("dp"),
        P("dp", "mp", None),
        P(None, "dp", "mp"),
        P(None, "dp", "mp"),
        P(None, "dp", "mp"),
        P("mp", "dp"),
        P("mp", "dp"),
        P("mp", "dp"),
        P("dp", "mp"),
        P("dp", "mp"),
        P("dp", "mp"),
        P("mp", "dp"),
        P("mp", "dp"),
        P("mp", "dp"),
        P(),
        P(),
        P(),
        P(),
        P(),
        P(),
    )
    return jax.shard_map(
        shards,
        mesh=mesh,
        in_specs=placed,
        out_specs=(
            P("dp", "mp", None),
            P("dp", "mp", None),
            P("dp", "mp", None),
            P(),
            P(None, "dp", "mp"),
            P(None, "dp", "mp"),
            P(None, "dp", "mp"),
            P(None, "dp", "mp"),
            P("mp", "dp"),
            P("mp", "dp"),
            P("mp", "dp"),
            P("mp", "dp"),
            P("dp", "mp"),
            P("dp", "mp"),
            P("dp", "mp"),
            P("dp", "mp"),
            P("mp", "dp"),
            P("mp", "dp"),
            P("mp", "dp"),
            P("mp", "dp"),
            P(),
            P(),
            P(),
            P(),
            P(),
            P(),
            P(),
            P(),
            P(None, "dp", "mp"),
            P("mp", "dp"),
            P("dp", "mp"),
            P("mp", "dp"),
        ),
        check_vma=False,
    )
```
